32 devices in a mesh: dp: 4 (over z), cent: 8 (over y, x, core).
Axes of the slice: x: 2, y: 2, z: 4, core: 2. Of those that a mesh axis runs over, the one named last changes fastest.
Arguments:
- embeddings: bfloat16 [8192, 1024], P(('dp', 'cent')), may hold values from -6 to 6
- codebook: float32 [4096, 1024], P(('cent', 'dp')), may hold values from -2 to 2
Outputs:
- new_codebook: float32 [4096, 1024], P(('cent', 'dp'))
- counts: float32 [4096], P(('cent', 'dp'))
- log_norm: float32 [8192], P(('dp', 'cent'))
The draws below stay inside these ranges and needn't reach their ends.
All inputs are finite; a program needn't handle non-finite values.
Results may differ from the reference program's by a relative error of at most 0.0022.
Values may be sent and summed in bfloat16 or wider, within the bound.
No kernel may reach another device: no remote copies, remote signals or barrier semaphores. Data moves between devices by JAX's collectives and lax.ppermute only.
A program may use at most 128 MiB of HBM per device.

```python
import jax
import jax.numpy as jnp
from jax import lax

D = 1024
ROWS_DEV = 256
N = 8192
K = 4096
N_CENT = 8


def anchor_rows(key):
    first, second = jax.random.split(key)
    signs = jnp.where(jax.random.bernoulli(first, 0.5, (8, D)), 1.0, -1.0)
    sizes = jax.random.uniform(second, (8, D), jnp.float32, 0.8, 1.2)
    sizes = sizes.at[:, 0].set(1.0)
    return signs * sizes


def anchor_strengths():
    return 2.5 + 2.0 / 7.0 * jnp.arange(8, dtype=jnp.float32)


def draw_embeddings(key, part):
    anchors = anchor_rows(key)
    key = jax.random.fold_in(key, 11)
    values = jnp.clip(jax.random.normal(key, (N, D), jnp.float32), -6.0, 6.0)
    places = jnp.arange(8, dtype=jnp.int32) * (N // 8)
    values = values.at[places].set(anchor_strengths()[:, None] * anchors)
    return values.astype(jnp.bfloat16)


def draw_codebook(key, part):
    anchors = anchor_rows(key)
    key = jax.random.fold_in(key, 23)
    values = 0.05 * jnp.clip(jax.random.normal(key, (K, D), jnp.float32), -6.0, 6.0)
    places = jnp.arange(8, dtype=jnp.int32) * (K // 8)
    scaled = 1.5 * anchors
    halved = scaled.at[:, 0].set(0.5 * scaled[:, 0])
    values = values.at[places].set(scaled)
    values = values.at[places + 1].set(halved)
    return values


def setup_inputs(seed: int = 0) -> dict:
    streams_of = jax.random.split(jax.random.key(seed), 3)
    return {
        "embeddings": draw_embeddings(jax.random.fold_in(streams_of[2], 71), 0),
        "codebook": draw_codebook(jax.random.fold_in(streams_of[2], 71), 0),
    }


TEMPER = 0.8
PRIOR = 1.0


def score_block(rows, centers, squares):
    product = jnp.dot(rows, centers.T, preferred_element_type=jnp.float32)
    return (product - 0.5 * squares[None, :]) / TEMPER


def reference(embeddings, codebook):
    centers = codebook.astype(jnp.bfloat16)
    squares = jnp.sum(jnp.square(centers.astype(jnp.float32)), axis=1)
    blocks = embeddings.reshape(-1, ROWS_DEV * N_CENT, D)

    def step(carry, rows):
        scores = score_block(rows, centers, squares)
        highest = jnp.max(scores, axis=1)
        lognorm = highest + jnp.log(jnp.sum(jnp.exp(scores - highest[:, None]), axis=1))
        resp = jnp.exp(scores - lognorm[:, None]).astype(jnp.bfloat16)
        sums = carry[0] + lax.dot_general(resp, rows, (((0,), (0,)), ((), ())), preferred_element_type=jnp.float32)
        tally = carry[1] + jnp.sum(resp.astype(jnp.float32), axis=0)
        return (sums, tally), lognorm

    start = (jnp.zeros((K, D), jnp.float32), jnp.zeros((K,), jnp.float32))
    (sums, tally), lognorm = lax.scan(step, start, blocks)
    new_codebook = (sums + PRIOR * codebook) / (tally + PRIOR)[:, None]
    return new_codebook, tally, lognorm.reshape(-1)
```

```python
import jax
import jax.numpy as jnp
from jax import lax
from jax.sharding import PartitionSpec as P

TEMPER = 0.8
PRIOR = 1.0


def swap(x, axis, size, mask):
    return lax.ppermute(x, axis, [(i, i ^ mask) for i in range(size)])


def gather_rows(own, size):
    if size != 8:
        return [own] + [swap(own, "cent", size, mask) for mask in range(1, size)]
    half = own.shape[0] // 2
    from_x = swap(own, "cent", size, 2)
    from_y = swap(own, "cent", size, 4)
    from_core = swap(own, "cent", size, 1)
    diag_top = swap(from_x[:half], "cent", size, 4)
    diag_low = swap(from_y[half:], "cent", size, 2)
    x_core = swap(from_x, "cent", size, 1)
    y_core = swap(from_y, "cent", size, 1)
    diag = jnp.concatenate([diag_top, diag_low], axis=0)
    diag_core = swap(diag, "cent", size, 1)
    return [own, from_core, from_x, x_core, from_y, y_core, diag, diag_core]


def score_block(rows, centers, squares):
    product = lax.dot_general(
        rows, centers, (((1,), (1,)), ((), ())), preferred_element_type=jnp.float32
    )
    return (product - 0.5 * squares[None, :]) / TEMPER


def local(n_dp, n_cent, embeddings, codebook):
    own_rows = embeddings.shape[0]
    own_cent = codebook.shape[0]
    rounded = codebook.astype(jnp.bfloat16)
    centers = [rounded] + [swap(rounded, "dp", n_dp, m) for m in range(1, n_dp)]
    blocks = gather_rows(embeddings, n_cent)
    centers = jnp.concatenate(centers, axis=0)
    squares = jnp.sum(jnp.square(centers.astype(jnp.float32)), axis=1)
    scores, pairs = [], []
    for rows in blocks:
        s = score_block(rows, centers, squares)
        m = jnp.max(s, axis=1)
        t = jnp.sum(jnp.exp(s - m[:, None]), axis=1)
        scores.append(s)
        pairs.append(jnp.stack([m, t]))
    pairs = jnp.stack(pairs)
    order = jnp.arange(n_cent)
    others = [pairs]
    for mask in range(1, n_cent):
        other = swap(pairs, "cent", n_cent, mask)
        others.append(jnp.stack([other[j ^ mask] for j in range(n_cent)]))
    others = jnp.stack(others)
    top = jnp.max(others[:, :, 0], axis=0)
    total = jnp.sum(others[:, :, 1] * jnp.exp(others[:, :, 0] - top[None]), axis=0)
    lognorm = top + jnp.log(total)
    resp = [jnp.exp(s - lognorm[j][:, None]).astype(jnp.bfloat16) for j, s in enumerate(scores)]
    resp = jnp.concatenate(resp, axis=0)
    gathered = jnp.concatenate(blocks, axis=0)
    tally = jnp.sum(resp.astype(jnp.float32), axis=0)
    sums = lax.dot_general(
        resp, gathered, (((0,), (0,)), ((), ())), preferred_element_type=jnp.float32
    )
    owner_total = sums[:own_cent]
    owner_tally = tally[:own_cent]
    for mask in range(1, n_dp):
        part = sums[mask * own_cent : (mask + 1) * own_cent]
        peak = jnp.max(jnp.abs(part), axis=1)
        power = jnp.exp2(jnp.clip(jnp.ceil(jnp.log2(peak)), -100.0, 100.0))
        packed = (part * (1.0 / power)[:, None]).astype(jnp.float16)
        side = jnp.stack([power, tally[mask * own_cent : (mask + 1) * own_cent]])
        packed = swap(packed, "dp", n_dp, mask)
        side = swap(side, "dp", n_dp, mask)
        owner_total = owner_total + packed.astype(jnp.float32) * side[0][:, None]
        owner_tally = owner_tally + side[1]
    new_codebook = (owner_total + PRIOR * codebook) / (owner_tally + PRIOR)[:, None]
    return (new_codebook, owner_tally, lognorm[0])


def solution(mesh):
    n_dp, n_cent = mesh.shape["dp"], mesh.shape["cent"]

    def run(embeddings, codebook):
        return local(n_dp, n_cent, embeddings, codebook)

    return jax.shard_map(
        run,
        mesh=mesh,
        in_specs=(P(("dp", "cent"), None), P(("cent", "dp"), None)),
        out_specs=(P(("cent", "dp"), None), P(("cent", "dp")), P(("dp", "cent"))),
        check_vma=False,
    )
```

```python
import jax
import jax.numpy as jnp
from jax import lax
from jax.sharding import PartitionSpec as P

TEMPER = 0.8
PRIOR = 1.0
SIDE = 16


def swap(x, axis, size, mask):
    return lax.ppermute(x, axis, [(i, i ^ mask) for i in range(size)])


def gather_centers(own, size):
    if size != 4:
        return [own] + [swap(own, "dp", size, mask) for mask in range(1, size)]
    far = swap(own, "dp", size, 2)
    near = swap(own, "dp", size, 1)
    return [own, near, far, swap(far, "dp", size, 1)]


def gather_rows(own, size):
    if size != 8:
        return [own] + [swap(own, "cent", size, mask) for mask in range(1, size)]
    half = own.shape[0] // 2
    from_x = swap(own, "cent", size, 2)
    from_y = swap(own, "cent", size, 4)
    from_core = swap(own, "cent", size, 1)
    diag_top = swap(from_x[:half], "cent", size, 4)
    diag_low = swap(from_y[half:], "cent", size, 2)
    x_core = swap(from_x, "cent", size, 1)
    y_core = swap(from_y, "cent", size, 1)
    diag = jnp.concatenate([diag_top, diag_low], axis=0)
    diag_core = swap(diag, "cent", size, 1)
    return [own, from_core, from_x, x_core, from_y, y_core, diag, diag_core]


def score_block(rows, centers, squares):
    product = lax.dot_general(
        centers, rows, (((1,), (1,)), ((), ())), preferred_element_type=jnp.float32
    )
    return (product - 0.5 * squares[:, None]) / TEMPER


def join(pairs, other, mask, size):
    other = jnp.concatenate([other[:, j ^ mask : (j ^ mask) + 1] for j in range(size)], axis=1)
    top = jnp.maximum(pairs[0], other[0])
    total = pairs[1] * jnp.exp(pairs[0] - top) + other[1] * jnp.exp(other[0] - top)
    return jnp.stack([top, total])


def encode(part, tally, power, unit):
    count = tally * unit
    high = count.astype(jnp.float16)
    low = ((count - high.astype(jnp.float32)) * 2048.0).astype(jnp.float16)
    tag = jnp.full(high.shape, 1.0, jnp.float32) * power
    side = jnp.stack([high, low, tag.astype(jnp.float16)])
    side = jnp.pad(side, ((0, SIDE - 3), (0, part.shape[1] - side.shape[1])))
    body = (part * jnp.exp2(14.0 - power)).astype(jnp.float16)
    return jnp.concatenate([body, side], axis=0)


def decode(message, unit):
    rows = message.shape[0] - SIDE
    side = message[rows:, :rows].astype(jnp.float32)
    power = side[2, 0]
    tally = (side[0] + side[1] * (1.0 / 2048.0)) * (1.0 / unit)
    return message[:rows].astype(jnp.float32) * jnp.exp2(power - 14.0), tally, power


def local(n_dp, n_cent, embeddings, codebook):
    own_rows = embeddings.shape[0]
    own_cent = codebook.shape[0]
    n_rows = own_rows * n_cent
    blocks = gather_rows(embeddings, n_cent)
    centers = gather_centers(codebook.astype(jnp.bfloat16), n_dp)
    centers = jnp.concatenate(centers, axis=0)
    squares = jnp.sum(jnp.square(centers.astype(jnp.float32)), axis=1)
    scores, tops, totals = [], [], []
    for rows in blocks:
        s = score_block(rows, centers, squares)
        m = jnp.max(s, axis=0)
        scores.append(s)
        tops.append(m)
        totals.append(jnp.sum(jnp.exp(s - m[None, :]), axis=0))
    pairs = jnp.stack([jnp.stack(tops), jnp.stack(totals)])
    mask = 1
    while mask < n_cent:
        pairs = join(pairs, swap(pairs, "cent", n_cent, mask), mask, n_cent)
        mask *= 2
    lognorm = pairs[0] + jnp.log(pairs[1])
    resp = [jnp.exp(s - lognorm[j][None, :]).astype(jnp.bfloat16) for j, s in enumerate(scores)]
    resp = jnp.concatenate(resp, axis=1)
    gathered = jnp.concatenate(blocks, axis=0)
    tally = jnp.sum(resp.astype(jnp.float32), axis=1)
    bound = jnp.max(jnp.stack([jnp.max(jnp.abs(b)) for b in blocks])).astype(jnp.float32)
    power = jnp.clip(jnp.ceil(jnp.log2(bound * n_rows)), -100.0, 100.0)
    unit = 16384.0 / n_rows

    def chunk(j):
        part = slice(j * own_cent, (j + 1) * own_cent)
        sums = lax.dot_general(
            resp[part], gathered, (((1,), (0,)), ((), ())), preferred_element_type=jnp.float32
        )
        return sums, tally[part]

    if n_dp == 4:
        first = swap(encode(*chunk(3), power, unit), "dp", n_dp, 1)
        near = swap(encode(*chunk(1), power, unit), "dp", n_dp, 1)
        part, count = chunk(2)
        more, more_count, more_power = decode(first, unit)
        far = encode(part + more, count + more_count, jnp.maximum(power, more_power) + 1.0, unit * 0.5)
        far = swap(far, "dp", n_dp, 2)
        owner_total, owner_tally = chunk(0)
        got = [decode(near, unit), decode(far, unit * 0.5)]
    else:
        owner_total, owner_tally = chunk(0)
        got = [
            decode(swap(encode(*chunk(j), power, unit), "dp", n_dp, j), unit)
            for j in range(1, n_dp)
        ]
    for more, more_count, _ in got:
        owner_total = owner_total + more
        owner_tally = owner_tally + more_count
    new_codebook = (owner_total + PRIOR * codebook) / (owner_tally + PRIOR)[:, None]
    return (new_codebook, owner_tally, lognorm[0])


def solution(mesh):
    n_dp, n_cent = mesh.shape["dp"], mesh.shape["cent"]

    def run(embeddings, codebook):
        return local(n_dp, n_cent, embeddings, codebook)

    return jax.shard_map(
        run,
        mesh=mesh,
        in_specs=(P(("dp", "cent"), None), P(("cent", "dp"), None)),
        out_specs=(P(("cent", "dp"), None), P(("cent", "dp")), P(("dp", "cent"))),
        check_vma=False,
    )
```

```python
import functools

import jax
import jax.numpy as jnp
from jax import lax
from jax.experimental import pallas as pl
from jax.experimental.pallas import tpu as pltpu
from jax.sharding import PartitionSpec as P

TEMPER = 0.8
PRIOR = 1.0
SIDE = 8
VMEM = pl.BlockSpec(memory_space=pltpu.VMEM)


def swap(x, axis, size, mask):
    return lax.ppermute(x, axis, [(i, i ^ mask) for i in range(size)])


def cut(refs, r):
    return [(ref, at) for ref in refs for at in range(0, ref.shape[0], r)]


def score_kernel(n_cent, n_rows, r, *refs):
    cent_refs, row_refs = refs[:n_cent], refs[n_cent : n_cent + n_rows]
    score_ref, top_ref, total_ref = refs[n_cent + n_rows :]
    centers = jnp.concatenate([ref[...] for ref in cent_refs], axis=0)
    half = 0.5 * jnp.sum(jnp.square(centers.astype(jnp.float32)), axis=1, keepdims=True)
    for j, (ref, at) in enumerate(cut(row_refs, r)):
        product = lax.dot_general(
            centers, ref[at : at + r], (((1,), (1,)), ((), ())), preferred_element_type=jnp.float32
        )
        s = (product - half) * (1.0 / TEMPER)
        top = jnp.max(s, axis=0, keepdims=True)
        score_ref[j] = s
        top_ref[j : j + 1] = top
        total_ref[j : j + 1] = jnp.sum(jnp.exp(s - top), axis=0, keepdims=True)


def score(centers, rows, r):
    n_c, n_in = len(centers), len(rows)
    n_r = sum(x.shape[0] for x in rows) // r
    depth = rows[0].shape[1]
    c = n_c * centers[0].shape[0]
    return pl.pallas_call(
        functools.partial(score_kernel, n_c, n_in, r),
        out_shape=(
            jax.ShapeDtypeStruct((n_r, c, r), jnp.float32),
            jax.ShapeDtypeStruct((n_r, r), jnp.float32),
            jax.ShapeDtypeStruct((n_r, r), jnp.float32),
        ),
        in_specs=[VMEM] * (n_c + n_in),
        out_specs=(VMEM,) * 3,
        compiler_params=pltpu.CompilerParams(vmem_limit_bytes=32 << 20),
        cost_estimate=pl.CostEstimate(
            flops=2 * n_r * c * r * depth,
            bytes_accessed=2 * (n_r * r + c) * depth,
            transcendentals=n_r * c * r,
        ),
        name="score_rows",
    )(*centers, *rows)


def sums_kernel(n_parts, n_rows, r, parts, lognorm_ref, *refs):
    score_refs, row_refs = refs[:n_parts], refs[n_parts : n_parts + n_rows]
    outs = refs[n_parts + n_rows :]
    blocks = cut(row_refs, r)
    ones = jnp.ones((SIDE, r), jnp.bfloat16)
    for out, (k, rows_of, first, size, packed) in zip(outs, parts):
        total, tally = None, None
        for j, (row_ref, at) in enumerate(blocks):
            s = score_refs[rows_of[j][0]][rows_of[j][1], first : first + size, :]
            resp = jnp.exp(s - lognorm_ref[j : j + 1]).astype(jnp.bfloat16)
            more = jnp.dot(resp, row_ref[at : at + r], preferred_element_type=jnp.float32)
            count = lax.dot_general(
                ones, resp, (((1,), (1,)), ((), ())), preferred_element_type=jnp.float32
            )
            total = more if total is None else total + more
            tally = count if tally is None else tally + count
        wide = jnp.concatenate(
            [tally, jnp.zeros((SIDE, total.shape[1] - size), jnp.float32)], axis=1
        )
        if packed:
            total, wide = pack(total, wide[0:1], packed)
        out[0:size] = total
        out[size : size + SIDE] = wide


def pack(total, tally, unit):
    peak = jnp.max(jnp.abs(total), axis=0, keepdims=True)
    power = jnp.clip(jnp.ceil(jnp.log2(peak)), -100.0, 100.0)
    high = jnp.floor(tally * unit)
    rest = (tally * unit - high) * 1024.0
    middle = jnp.floor(rest)
    low = (rest - middle) * 1024.0
    blank = jnp.zeros((SIDE - 4, total.shape[1]), jnp.float32)
    return total * jnp.exp2(14.0 - power), jnp.concatenate([power, high, middle, low, blank])


def unpack(message, unit):
    size = message.shape[0] - SIDE
    values = message.astype(jnp.float32)
    power, high, middle, low = (values[size + i : size + i + 1] for i in range(4))
    tally = (high + (middle + low * (1.0 / 1024.0)) * (1.0 / 1024.0)) * (1.0 / unit)
    return values[:size] * jnp.exp2(power - 14.0), tally


def weighted(parts, lognorm, scores, rows):
    size = parts[0][3]
    depth = rows[0].shape[1]
    n_in, n_p = len(rows), len(scores)
    n_r, r = lognorm.shape
    return pl.pallas_call(
        functools.partial(sums_kernel, n_p, n_in, r, parts),
        out_shape=[jax.ShapeDtypeStruct((size + SIDE, depth), jnp.float32) for _ in parts],
        in_specs=[VMEM] * (1 + n_p + n_in),
        out_specs=[VMEM] * len(parts),
        compiler_params=pltpu.CompilerParams(vmem_limit_bytes=32 << 20),
        cost_estimate=pl.CostEstimate(
            flops=2 * len(parts) * n_r * size * r * depth,
            bytes_accessed=2 * n_r * r * depth,
            transcendentals=len(parts) * n_r * size * r,
        ),
        name="weighted_sums",
    )(lognorm, *scores, *rows)


def merge(a, b):
    top = jnp.maximum(a[0], b[0])
    return top, a[1] * jnp.exp(a[0] - top) + b[1] * jnp.exp(b[0] - top)


def join(pairs, mask, order):
    other = swap(jnp.stack(pairs), "cent", len(order), mask)
    places = [order.index(j ^ mask) for j in order]
    other = jnp.concatenate([other[:, p : p + 1] for p in places], axis=1)
    return merge(pairs, other)


def local(n_dp, n_cent, embeddings, codebook):
    own_rows = embeddings.shape[0]
    size = codebook.shape[0]
    n_rows = own_rows * n_cent
    unit = 1024.0 / n_rows
    rounded = codebook.astype(jnp.bfloat16)
    if n_cent == 8:
        half = own_rows // 2
        from_x = swap(embeddings, "cent", n_cent, 2)
        from_y = swap(embeddings, "cent", n_cent, 4)
    if n_dp == 4:
        far = swap(rounded, "dp", n_dp, 2)
        near = swap(rounded, "dp", n_dp, 1)
    if n_cent == 8:
        if n_dp == 4:
            from_x, from_y, near = lax.optimization_barrier((from_x, from_y, near))
        diag_top = swap(from_x[:half], "cent", n_cent, 4)
        diag_low = swap(from_y[half:], "cent", n_cent, 2)
        four = jnp.concatenate([embeddings, from_x, from_y, diag_top, diag_low], axis=0)
        give = lax.optimization_barrier((four, far))[0] if n_dp == 4 else four
        rows, order = [four, swap(give, "cent", n_cent, 1)], [0, 2, 4, 6, 1, 3, 5, 7]
        early, later = 4, 1
    else:
        rows = [embeddings] + [swap(embeddings, "cent", n_cent, m) for m in range(1, n_cent)]
        order = list(range(n_cent))
        early = later = n_cent // 2
    if n_dp == 4:
        give, near = lax.optimization_barrier((far, near))
        centers = [rounded, near, far, swap(give, "dp", n_dp, 1)]
    else:
        centers = [rounded] + [swap(rounded, "dp", n_dp, m) for m in range(1, n_dp)]
    s_a, top_a, total_a = score(centers[:-1], rows[:-later], own_rows)
    s_b, top_b, total_b = score(centers[:-1], rows[-later:], own_rows)
    s_c, top_c, total_c = score(centers[-1:], rows, own_rows)
    pairs = (jnp.concatenate([top_a, top_b]), jnp.concatenate([total_a, total_b]))
    pairs = merge(pairs, (top_c, total_c))
    mask = 1
    while mask < n_cent:
        pairs = join(pairs, mask, order)
        mask *= 2
    lognorm = pairs[0] + jnp.log(pairs[1])

    split = tuple((0, j) if j < early else (1, j - early) for j in range(n_cent))
    whole = tuple((0, j) for j in range(n_cent))

    def part(k, packed):
        return (k, split, k * size, size, packed)

    last = (n_dp - 1, whole, 0, size, unit)
    (first,) = weighted((last,), lognorm, (s_c,), rows)
    first = first.astype(jnp.float16)
    if n_dp == 4:
        first = swap(first, "dp", n_dp, 1)
        far_out, near_out, own = weighted(
            (part(2, 0), part(1, unit), part(0, 0)), lognorm, (s_a, s_b), rows
        )
        more, count = unpack(first, unit)
        total, wide = pack(far_out[:size] + more, far_out[size : size + 1] + count, unit * 0.5)
        far_out = swap(jnp.concatenate([total, wide]).astype(jnp.float16), "dp", n_dp, 2)
        near_in, _ = lax.optimization_barrier((near_out.astype(jnp.float16), first))
        near_out = swap(near_in, "dp", n_dp, 1)
        got = [unpack(near_out, unit), unpack(far_out, unit * 0.5)]
    else:
        out = weighted(
            tuple(part(k, unit if k else 0) for k in range(n_dp - 1)), lognorm, (s_a, s_b), rows
        )
        own = out[0]
        sent = [o.astype(jnp.float16) for o in out[1:]] + [first]
        got = [unpack(swap(m, "dp", n_dp, k + 1), unit) for k, m in enumerate(sent)]
    owner_total, owner_tally = own[:size], own[size, :size]
    for more, count in got:
        owner_total = owner_total + more
        owner_tally = owner_tally + count[0, :size]
    new_codebook = (owner_total + PRIOR * codebook) / (owner_tally + PRIOR)[:, None]
    return (new_codebook, owner_tally, lognorm[0])


def solution(mesh):
    n_dp, n_cent = mesh.shape["dp"], mesh.shape["cent"]

    def run(embeddings, codebook):
        return local(n_dp, n_cent, embeddings, codebook)

    return jax.shard_map(
        run,
        mesh=mesh,
        in_specs=(P(("dp", "cent"), None), P(("cent", "dp"), None)),
        out_specs=(P(("cent", "dp"), None), P(("cent", "dp")), P(("dp", "cent"))),
        check_vma=False,
    )
```

```python
import functools

import jax
import jax.numpy as jnp
from jax import lax
from jax.experimental import pallas as pl
from jax.experimental.pallas import tpu as pltpu
from jax.sharding import PartitionSpec as P

TEMPER = 0.8
PRIOR = 1.0
SIDE = 8
VMEM = pl.BlockSpec(memory_space=pltpu.VMEM)
PARAMS = pltpu.CompilerParams(vmem_limit_bytes=24 << 20)


def swap(x, axis, size, mask):
    return lax.ppermute(x, axis, [(i, i ^ mask) for i in range(size)])


def merge(a, b):
    top = jnp.maximum(a[0], b[0])
    return top, a[1] * jnp.exp(a[0] - top) + b[1] * jnp.exp(b[0] - top)


def score_kernel(n_cent, n_rows, picks, begin, starts, *refs):
    cent_refs, row_refs = refs[:n_cent], refs[n_cent : n_cent + n_rows]
    early_refs = refs[n_cent + n_rows : -2]
    score_ref, pair_ref = refs[-2:]
    r = score_ref.shape[2]
    centers = jnp.concatenate([ref[...] for ref in cent_refs], axis=0)
    half = 0.5 * jnp.sum(jnp.square(centers.astype(jnp.float32)), axis=1, keepdims=True)
    for j, (i, at) in enumerate(picks):
        product = lax.dot_general(
            centers,
            row_refs[i][at : at + r],
            (((1,), (1,)), ((), ())),
            preferred_element_type=jnp.float32,
        )
        s = (product - half) * (1.0 / TEMPER)
        top = jnp.max(s, axis=0, keepdims=True)
        score_ref[j] = s
        total = jnp.sum(jnp.exp(s - top), axis=0, keepdims=True)
        at = begin + j
        for ref, start in zip(early_refs, starts):
            if start <= at < start + ref.shape[1]:
                k = slice(at - start, at - start + 1)
                top, total = merge((top, total), (ref[0, k], ref[1, k]))
        pair_ref[0, at : at + 1] = top
        pair_ref[1, at : at + 1] = total
    for ref, start in zip(early_refs, starts):
        for k in range(ref.shape[1]):
            if not begin <= start + k < begin + len(picks):
                pair_ref[:, start + k : start + k + 1] = ref[:, k : k + 1]


def score(centers, rows, r, picks, early=(), begin=0):
    n_c, n_r = len(centers), len(picks)
    depth = rows[0].shape[1]
    c = n_c * centers[0].shape[0]
    starts = [sum(e.shape[1] for e in early[:i]) for i in range(len(early))]
    n_out = max(begin + n_r, sum(e.shape[1] for e in early))
    return pl.pallas_call(
        functools.partial(score_kernel, n_c, len(rows), picks, begin, starts),
        out_shape=(
            jax.ShapeDtypeStruct((n_r, c, r), jnp.float32),
            jax.ShapeDtypeStruct((2, n_out, r), jnp.float32),
        ),
        in_specs=[VMEM] * (n_c + len(rows) + len(early)),
        out_specs=(VMEM,) * 2,
        compiler_params=PARAMS,
        cost_estimate=pl.CostEstimate(
            flops=2 * n_r * c * r * depth,
            bytes_accessed=2 * (n_r * r + c) * depth,
            transcendentals=n_r * c * r,
        ),
        name="score_rows",
    )(*centers, *rows, *early)


def join_kernel(places, last, pair_ref, other_ref, out_ref):
    other = [jnp.concatenate([other_ref[i, p : p + 1] for p in places]) for i in range(2)]
    top, total = merge((pair_ref[0], pair_ref[1]), other)
    if last:
        out_ref[...] = top + jnp.log(total)
    else:
        out_ref[0] = top
        out_ref[1] = total


def join(pairs, mask, order, last):
    other = swap(pairs, "cent", len(order), mask)
    places = [order.index(j ^ mask) for j in order]
    return pl.pallas_call(
        functools.partial(join_kernel, places, last),
        out_shape=jax.ShapeDtypeStruct(pairs.shape[1:] if last else pairs.shape, jnp.float32),
        in_specs=[VMEM] * 2,
        out_specs=VMEM,
        compiler_params=PARAMS,
        name="join_rows",
    )(pairs, other)


def sums_kernel(n_parts, picks, parts, lognorm_ref, *refs):
    score_refs, row_refs = refs[:n_parts], refs[n_parts : -len(parts)]
    outs = refs[-len(parts) :]
    r = lognorm_ref.shape[1]
    ones = jnp.ones((SIDE, r), jnp.bfloat16)
    for out, (places, size, unit) in zip(outs, parts):
        total, tally = None, None
        for j, (i, at) in enumerate(picks):
            k, block, first = places[j]
            s = score_refs[k][block, first : first + size, :]
            resp = jnp.exp(s - lognorm_ref[j : j + 1]).astype(jnp.bfloat16)
            more = jnp.dot(resp, row_refs[i][at : at + r], preferred_element_type=jnp.float32)
            count = lax.dot_general(
                ones, resp, (((1,), (1,)), ((), ())), preferred_element_type=jnp.float32
            )
            total = more if total is None else total + more
            tally = count if tally is None else tally + count
        wide = jnp.concatenate(
            [tally, jnp.zeros((SIDE, total.shape[1] - size), jnp.float32)], axis=1
        )
        if unit:
            total, wide = pack(total, wide[0:1], unit)
        out[0:size] = total
        out[size : size + SIDE] = wide


def pack(total, tally, unit):
    peak = jnp.max(jnp.abs(total), axis=0, keepdims=True)
    power = jnp.clip(jnp.ceil(jnp.log2(peak)), -100.0, 100.0)
    high = jnp.floor(tally * unit)
    rest = (tally * unit - high) * 1024.0
    middle = jnp.floor(rest)
    low = (rest - middle) * 1024.0
    blank = jnp.zeros((SIDE - 4, total.shape[1]), jnp.float32)
    return total * jnp.exp2(14.0 - power), jnp.concatenate([power, high, middle, low, blank])


def unpack(values, unit):
    size = values.shape[0] - SIDE
    power, high, middle, low = (values[size + i : size + i + 1] for i in range(4))
    tally = (high + (middle + low * (1.0 / 1024.0)) * (1.0 / 1024.0)) * (1.0 / unit)
    return values[:size] * jnp.exp2(power - 14.0), tally


def relay_kernel(unit, own_ref, got_ref, out_ref):
    size = own_ref.shape[0] - SIDE
    more, count = unpack(got_ref[...], unit)
    total, wide = pack(own_ref[0:size] + more, own_ref[size : size + 1] + count, unit * 0.5)
    out_ref[0:size] = total
    out_ref[size : size + SIDE] = wide


def relay(own, got, unit):
    return pl.pallas_call(
        functools.partial(relay_kernel, unit),
        out_shape=jax.ShapeDtypeStruct(own.shape, jnp.float32),
        in_specs=[VMEM] * 2,
        out_specs=VMEM,
        compiler_params=PARAMS,
        name="relay_sums",
    )(own, got)


def weighted(parts, lognorm, scores, rows, picks):
    size = parts[0][1]
    depth = rows[0].shape[1]
    n_r, r = lognorm.shape
    return pl.pallas_call(
        functools.partial(sums_kernel, len(scores), picks, parts),
        out_shape=[jax.ShapeDtypeStruct((size + SIDE, depth), jnp.float32) for _ in parts],
        in_specs=[VMEM] * (1 + len(scores) + len(rows)),
        out_specs=[VMEM] * len(parts),
        compiler_params=PARAMS,
        cost_estimate=pl.CostEstimate(
            flops=2 * len(parts) * n_r * size * r * depth,
            bytes_accessed=2 * n_r * r * depth,
            transcendentals=len(parts) * n_r * size * r,
        ),
        name="weighted_sums",
    )(lognorm, *scores, *rows)


def local(n_dp, n_cent, embeddings, codebook):
    own_rows = embeddings.shape[0]
    size = codebook.shape[0]
    unit = 1024.0 / (own_rows * n_cent)
    rounded = codebook.astype(jnp.bfloat16)
    if n_cent == 8:
        half = own_rows // 2
        from_x = swap(embeddings, "cent", n_cent, 2)
        from_y = swap(embeddings, "cent", n_cent, 4)
    if n_dp == 4:
        far = swap(rounded, "dp", n_dp, 2)
        near = swap(rounded, "dp", n_dp, 1)
        centers = [rounded, near, far, swap(far, "dp", n_dp, 1)]
    else:
        centers = [rounded] + [swap(rounded, "dp", n_dp, m) for m in range(1, n_dp)]
    if n_cent == 8:
        diag_top = swap(from_x[:half], "cent", n_cent, 4)
        diag_low = swap(from_y[half:], "cent", n_cent, 2)
        s_0, pair_0 = score(
            centers[:-1], [embeddings, from_x, from_y], own_rows, [(0, 0), (1, 0), (2, 0)]
        )
        diag_top, diag_low, s_0, pair_0 = lax.optimization_barrier(
            (diag_top, diag_low, s_0, pair_0)
        )
        four = jnp.concatenate([embeddings, from_x, from_y, diag_top, diag_low], axis=0)
        rows, order = [four, swap(four, "cent", n_cent, 1)], [0, 2, 4, 6, 1, 3, 5, 7]
        picks = [(i, j * own_rows) for i in range(2) for j in range(4)]
        rows[0], centers[-1] = lax.optimization_barrier((four, centers[-1]))
        s_1, pair_1 = score(centers[:-1], rows[:1], own_rows, [(0, 3 * own_rows)])
        s_2, pairs = score(centers[-1:], rows[:1], own_rows, picks[:4], [pair_0, pair_1])
        four_core, s_2, pairs = lax.optimization_barrier((rows[1], s_2, pairs))
        rows[1] = four_core
        s_3, pairs = score(centers, rows[1:], own_rows, picks[:4], [pairs], 4)
        scores = [s_0, s_1, s_3]
        places = [(0, 0), (0, 1), (0, 2), (1, 0), (2, 0), (2, 1), (2, 2), (2, 3)]
        last_scores = [s_2, s_3]
        last_places = [(0, j, 0) for j in range(4)] + [(1, j, (n_dp - 1) * size) for j in range(4)]
    else:
        rows = [embeddings] + [swap(embeddings, "cent", n_cent, m) for m in range(1, n_cent)]
        order = list(range(n_cent))
        picks = [(j, 0) for j in order]
        s_0, pair_0 = score(centers[:-1], rows, own_rows, picks)
        scores = [s_0]
        places = [(0, j) for j in order]
        s_1, pairs = score(centers[-1:], rows, own_rows, picks, [pair_0])
        last_scores, last_places = [s_1], [(0, j, 0) for j in order]
    mask = 1
    while mask < n_cent:
        pairs = join(pairs, mask, order, 2 * mask >= n_cent)
        mask *= 2
    lognorm = pairs

    def part(k, unit):
        return [(i, j, k * size) for i, j in places], size, unit

    (first,) = weighted([(last_places, size, unit)], lognorm, last_scores, rows, picks)
    first = first.astype(jnp.float16)
    if n_dp == 4:
        first = swap(first, "dp", n_dp, 1)
        parts = [part(2, 0), part(1, unit), part(0, 0)]
        far_out, near_out, own = weighted(parts, lognorm, scores, rows, picks)
        far_out = relay(far_out, first.astype(jnp.float32), unit)
        far_out, near_out = lax.optimization_barrier((far_out, near_out))
        far_out = swap(far_out.astype(jnp.float16), "dp", n_dp, 2)
        near_out = swap(near_out.astype(jnp.float16), "dp", n_dp, 1)
        got = [(near_out, unit), (far_out, unit * 0.5)]
    else:
        parts = [part(k, unit if k else 0) for k in range(n_dp - 1)]
        out = weighted(parts, lognorm, scores, rows, picks)
        own = out[0]
        sent = [o.astype(jnp.float16) for o in out[1:]] + [first]
        got = [(swap(m, "dp", n_dp, k + 1), unit) for k, m in enumerate(sent)]
    owner_total, owner_tally = own[:size], own[size, :size]
    for message, of in got:
        more, count = unpack(message.astype(jnp.float32), of)
        owner_total = owner_total + more
        owner_tally = owner_tally + count[0, :size]
    new_codebook = (owner_total + PRIOR * codebook) / (owner_tally + PRIOR)[:, None]
    return (new_codebook, owner_tally, lognorm[0])


def solution(mesh):
    n_dp, n_cent = mesh.shape["dp"], mesh.shape["cent"]

    def run(embeddings, codebook):
        return local(n_dp, n_cent, embeddings, codebook)

    return jax.shard_map(
        run,
        mesh=mesh,
        in_specs=(P(("dp", "cent"), None), P(("cent", "dp"), None)),
        out_specs=(P(("cent", "dp"), None), P(("cent", "dp")), P(("dp", "cent"))),
        check_vma=False,
    )
```

```python
import functools

import jax
import jax.numpy as jnp
from jax import lax
from jax.experimental import pallas as pl
from jax.experimental.pallas import tpu as pltpu
from jax.sharding import PartitionSpec as P

TEMPER = 0.8
PRIOR = 1.0
SIDE = 8
VMEM = pl.BlockSpec(memory_space=pltpu.VMEM)
PARAMS = pltpu.CompilerParams(vmem_limit_bytes=24 << 20)


def swap(x, axis, size, mask):
    return lax.ppermute(x, axis, [(i, i ^ mask) for i in range(size)])


def merge(a, b):
    top = jnp.maximum(a[0], b[0])
    return top, a[1] * jnp.exp(a[0] - top) + b[1] * jnp.exp(b[0] - top)


def score_kernel(n_cent, n_rows, picks, begin, starts, *refs):
    cent_refs, row_refs = refs[:n_cent], refs[n_cent : n_cent + n_rows]
    early_refs = refs[n_cent + n_rows : -2]
    score_ref, pair_ref = refs[-2:]
    r = score_ref.shape[2]
    centers = jnp.concatenate([ref[...] for ref in cent_refs], axis=0)
    half = 0.5 * jnp.sum(jnp.square(centers.astype(jnp.float32)), axis=1, keepdims=True)
    for j, (i, at) in enumerate(picks):
        product = lax.dot_general(
            centers,
            row_refs[i][at : at + r],
            (((1,), (1,)), ((), ())),
            preferred_element_type=jnp.float32,
        )
        s = (product - half) * (1.0 / TEMPER)
        top = jnp.max(s, axis=0, keepdims=True)
        score_ref[j] = s
        total = jnp.sum(jnp.exp(s - top), axis=0, keepdims=True)
        at = begin + j
        for ref, start in zip(early_refs, starts):
            if start <= at < start + ref.shape[1]:
                k = slice(at - start, at - start + 1)
                top, total = merge((top, total), (ref[0, k], ref[1, k]))
        pair_ref[0, at : at + 1] = top
        pair_ref[1, at : at + 1] = total
    for ref, start in zip(early_refs, starts):
        for k in range(ref.shape[1]):
            if not begin <= start + k < begin + len(picks):
                pair_ref[:, start + k : start + k + 1] = ref[:, k : k + 1]


def score(centers, rows, r, picks, early=(), begin=0):
    n_c, n_r = len(centers), len(picks)
    depth = rows[0].shape[1]
    c = sum(x.shape[0] for x in centers)
    starts = [sum(e.shape[1] for e in early[:i]) for i in range(len(early))]
    n_out = max(begin + n_r, sum(e.shape[1] for e in early))
    return pl.pallas_call(
        functools.partial(score_kernel, n_c, len(rows), picks, begin, starts),
        out_shape=(
            jax.ShapeDtypeStruct((n_r, c, r), jnp.float32),
            jax.ShapeDtypeStruct((2, n_out, r), jnp.float32),
        ),
        in_specs=[VMEM] * (n_c + len(rows) + len(early)),
        out_specs=(VMEM,) * 2,
        compiler_params=PARAMS,
        cost_estimate=pl.CostEstimate(
            flops=2 * n_r * c * r * depth,
            bytes_accessed=2 * (n_r * r + c) * depth,
            transcendentals=n_r * c * r,
        ),
        name="score_rows",
    )(*centers, *rows, *early)


def join_kernel(places, last, pair_ref, other_ref, out_ref):
    other = [jnp.concatenate([other_ref[i, p : p + 1] for p in places]) for i in range(2)]
    top, total = merge((pair_ref[0], pair_ref[1]), other)
    if last:
        out_ref[...] = top + jnp.log(total)
    else:
        out_ref[0] = top
        out_ref[1] = total


def join(pairs, mask, order, last):
    other = swap(pairs, "cent", len(order), mask)
    places = [order.index(j ^ mask) for j in order]
    return pl.pallas_call(
        functools.partial(join_kernel, places, last),
        out_shape=jax.ShapeDtypeStruct(pairs.shape[1:] if last else pairs.shape, jnp.float32),
        in_specs=[VMEM] * 2,
        out_specs=VMEM,
        compiler_params=PARAMS,
        name="join_rows",
    )(pairs, other)


def sums_kernel(n_parts, picks, parts, lognorm_ref, *refs):
    score_refs, row_refs = refs[:n_parts], refs[n_parts : -len(parts)]
    outs = refs[-len(parts) :]
    r = lognorm_ref.shape[1]
    ones = jnp.ones((SIDE, r), jnp.bfloat16)
    for out, (places, size, unit) in zip(outs, parts):
        total, tally = None, None
        for j, (i, at) in enumerate(picks):
            k, block, first = places[j]
            s = score_refs[k][block, first : first + size, :]
            resp = jnp.exp(s - lognorm_ref[j : j + 1]).astype(jnp.bfloat16)
            more = jnp.dot(resp, row_refs[i][at : at + r], preferred_element_type=jnp.float32)
            count = lax.dot_general(
                ones, resp, (((1,), (1,)), ((), ())), preferred_element_type=jnp.float32
            )
            total = more if total is None else total + more
            tally = count if tally is None else tally + count
        wide = jnp.concatenate(
            [tally, jnp.zeros((SIDE, total.shape[1] - size), jnp.float32)], axis=1
        )
        if unit:
            total, wide = pack(total, wide[0:1], unit)
        out[0:size] = total
        out[size : size + SIDE] = wide


def pack(total, tally, unit):
    peak = jnp.max(jnp.abs(total), axis=0, keepdims=True)
    power = jnp.clip(jnp.ceil(jnp.log2(peak)), -100.0, 100.0)
    high = jnp.floor(tally * unit)
    rest = (tally * unit - high) * 1024.0
    middle = jnp.floor(rest)
    low = (rest - middle) * 1024.0
    blank = jnp.zeros((SIDE - 4, total.shape[1]), jnp.float32)
    return total * jnp.exp2(14.0 - power), jnp.concatenate([power, high, middle, low, blank])


def unpack(values, unit):
    size = values.shape[0] - SIDE
    power, high, middle, low = (values[size + i : size + i + 1] for i in range(4))
    tally = (high + (middle + low * (1.0 / 1024.0)) * (1.0 / 1024.0)) * (1.0 / unit)
    return values[:size] * jnp.exp2(power - 14.0), tally


def relay_kernel(unit, own_ref, got_ref, out_ref):
    size = own_ref.shape[0] - SIDE
    more, count = unpack(got_ref[...], unit)
    total, wide = pack(own_ref[0:size] + more, own_ref[size : size + 1] + count, unit * 0.5)
    out_ref[0:size] = total
    out_ref[size : size + SIDE] = wide


def relay(own, got, unit):
    return pl.pallas_call(
        functools.partial(relay_kernel, unit),
        out_shape=jax.ShapeDtypeStruct(own.shape, jnp.float32),
        in_specs=[VMEM] * 2,
        out_specs=VMEM,
        compiler_params=PARAMS,
        name="relay_sums",
    )(own, got)


def weighted(parts, lognorm, scores, rows, picks):
    size = parts[0][1]
    depth = rows[0].shape[1]
    n_r, r = lognorm.shape
    return pl.pallas_call(
        functools.partial(sums_kernel, len(scores), picks, parts),
        out_shape=[jax.ShapeDtypeStruct((size + SIDE, depth), jnp.float32) for _ in parts],
        in_specs=[VMEM] * (1 + len(scores) + len(rows)),
        out_specs=[VMEM] * len(parts),
        compiler_params=PARAMS,
        cost_estimate=pl.CostEstimate(
            flops=2 * len(parts) * n_r * size * r * depth,
            bytes_accessed=2 * n_r * r * depth,
            transcendentals=len(parts) * n_r * size * r,
        ),
        name="weighted_sums",
    )(lognorm, *scores, *rows)


def local(n_dp, n_cent, embeddings, codebook):
    own_rows = embeddings.shape[0]
    size = codebook.shape[0]
    unit = 1024.0 / (own_rows * n_cent)
    rounded = codebook.astype(jnp.bfloat16)
    if n_cent == 8:
        half = own_rows // 2
        from_x = swap(embeddings, "cent", n_cent, 2)
        from_y = swap(embeddings, "cent", n_cent, 4)
    if n_dp == 4:
        far = [swap(x, "dp", n_dp, 2) for x in (rounded[: size // 2], rounded[size // 2 :])]
        near = swap(rounded, "dp", n_dp, 1)
        most = [rounded, near] + far
        final = [swap(x, "dp", n_dp, 1) for x in far]
    else:
        most = [rounded] + [swap(rounded, "dp", n_dp, m) for m in range(1, n_dp - 1)]
        final = [swap(rounded, "dp", n_dp, n_dp - 1)]
    end = (n_dp - 1) * size
    if n_cent == 8:
        from_x, from_y, most = lax.optimization_barrier((from_x, from_y, most))
        diag_top = swap(from_x[:half], "cent", n_cent, 4)
        diag_low = swap(from_y[half:], "cent", n_cent, 2)
        three = jnp.concatenate([embeddings, from_x, from_y], axis=0)
        give, final[0] = lax.optimization_barrier((three, final[0]))
        three_core = swap(give, "cent", n_cent, 1)
        diag = jnp.concatenate([diag_top, diag_low], axis=0)
        give, final[-1] = lax.optimization_barrier((diag, final[-1]))
        diag_core = swap(give, "cent", n_cent, 1)
        rows, order = [three, three_core, diag, diag_core], [0, 2, 4, 1, 3, 5, 6, 7]
        picks = [(i, j * own_rows) for i in range(2) for j in range(3)] + [(2, 0), (3, 0)]
        s_0, pair_0 = score(most, rows[:1], own_rows, picks[:3])
        s_1, pair_1 = score(most, rows[1:2], own_rows, picks[:3])
        s_2, pair_2 = score(most + final, rows[2:3], own_rows, [(0, 0)])
        s_3, pairs = score(final, rows[:2], own_rows, picks[:6], [pair_0, pair_1])
        s_4, pairs = score(most + final, rows[3:], own_rows, [(0, 0)], [pairs, pair_2], 7)
        scores = [s_0, s_1, s_2, s_4]
        places = [(i, j) for i in range(2) for j in range(3)] + [(2, 0), (3, 0)]
        last_scores = [s_3, s_2, s_4]
        last_places = [(0, j, 0) for j in range(6)] + [(1, 0, end), (2, 0, end)]
    else:
        rows = [embeddings] + [swap(embeddings, "cent", n_cent, m) for m in range(1, n_cent)]
        order = list(range(n_cent))
        picks = [(j, 0) for j in order]
        s_0, pair_0 = score(most, rows, own_rows, picks)
        scores = [s_0]
        places = [(0, j) for j in order]
        s_1, pairs = score(final, rows, own_rows, picks, [pair_0])
        last_scores, last_places = [s_1], [(0, j, 0) for j in order]
    mask = 1
    while mask < n_cent:
        pairs = join(pairs, mask, order, 2 * mask >= n_cent)
        mask *= 2
    lognorm = pairs

    def part(k, unit):
        return [(i, j, k * size) for i, j in places], size, unit

    (first,) = weighted([(last_places, size, unit)], lognorm, last_scores, rows, picks)
    first = first.astype(jnp.float16)
    if n_dp == 4:
        first = swap(first, "dp", n_dp, 1)
        parts = [part(2, 0), part(1, unit), part(0, 0)]
        far_out, near_out, own = weighted(parts, lognorm, scores, rows, picks)
        far_out = relay(far_out, first.astype(jnp.float32), unit)
        far_out, near_out = lax.optimization_barrier((far_out, near_out))
        far_out = swap(far_out.astype(jnp.float16), "dp", n_dp, 2)
        near_out = swap(near_out.astype(jnp.float16), "dp", n_dp, 1)
        got = [(near_out, unit), (far_out, unit * 0.5)]
    else:
        parts = [part(k, unit if k else 0) for k in range(n_dp - 1)]
        out = weighted(parts, lognorm, scores, rows, picks)
        own = out[0]
        sent = [o.astype(jnp.float16) for o in out[1:]] + [first]
        got = [(swap(m, "dp", n_dp, k + 1), unit) for k, m in enumerate(sent)]
    owner_total, owner_tally = own[:size], own[size, :size]
    for message, of in got:
        more, count = unpack(message.astype(jnp.float32), of)
        owner_total = owner_total + more
        owner_tally = owner_tally + count[0, :size]
    new_codebook = (owner_total + PRIOR * codebook) / (owner_tally + PRIOR)[:, None]
    return (new_codebook, owner_tally, lognorm[0])


def solution(mesh):
    n_dp, n_cent = mesh.shape["dp"], mesh.shape["cent"]

    def run(embeddings, codebook):
        return local(n_dp, n_cent, embeddings, codebook)

    return jax.shard_map(
        run,
        mesh=mesh,
        in_specs=(P(("dp", "cent"), None), P(("cent", "dp"), None)),
        out_specs=(P(("cent", "dp"), None), P(("cent", "dp")), P(("dp", "cent"))),
        check_vma=False,
    )
```

```python
import functools

import jax
import jax.numpy as jnp
from jax import lax
from jax.experimental import pallas as pl
from jax.experimental.pallas import tpu as pltpu
from jax.sharding import PartitionSpec as P

TEMPER = 0.8
PRIOR = 1.0
SIDE = 8
VMEM = pl.BlockSpec(memory_space=pltpu.VMEM)
PARAMS = pltpu.CompilerParams(vmem_limit_bytes=24 << 20)


def swap(x, axis, size, mask):
    return lax.ppermute(x, axis, [(i, i ^ mask) for i in range(size)])


def merge(a, b):
    top = jnp.maximum(a[0], b[0])
    return top, a[1] * jnp.exp(a[0] - top) + b[1] * jnp.exp(b[0] - top)


def score_kernel(n_cent, n_rows, picks, begin, starts, *refs):
    cent_refs, row_refs = refs[:n_cent], refs[n_cent : n_cent + n_rows]
    early_refs = refs[n_cent + n_rows : -2]
    score_ref, pair_ref = refs[-2:]
    r = score_ref.shape[2]
    centers = jnp.concatenate([ref[...] for ref in cent_refs], axis=0)
    half = 0.5 * jnp.sum(jnp.square(centers.astype(jnp.float32)), axis=1, keepdims=True)
    for j, (i, at) in enumerate(picks):
        product = lax.dot_general(
            centers,
            row_refs[i][at : at + r],
            (((1,), (1,)), ((), ())),
            preferred_element_type=jnp.float32,
        )
        s = (product - half) * (1.0 / TEMPER)
        top = jnp.max(s, axis=0, keepdims=True)
        score_ref[j] = s
        total = jnp.sum(jnp.exp(s - top), axis=0, keepdims=True)
        at = begin + j
        for ref, start in zip(early_refs, starts):
            if start <= at < start + ref.shape[1]:
                k = slice(at - start, at - start + 1)
                top, total = merge((top, total), (ref[0, k], ref[1, k]))
        pair_ref[0, at : at + 1] = top
        pair_ref[1, at : at + 1] = total
    for ref, start in zip(early_refs, starts):
        for k in range(ref.shape[1]):
            if not begin <= start + k < begin + len(picks):
                pair_ref[:, start + k : start + k + 1] = ref[:, k : k + 1]


def score(centers, rows, r, picks, early=(), begin=0):
    n_c, n_r = len(centers), len(picks)
    depth = rows[0].shape[1]
    c = n_c * centers[0].shape[0]
    starts = [sum(e.shape[1] for e in early[:i]) for i in range(len(early))]
    n_out = max(begin + n_r, sum(e.shape[1] for e in early))
    return pl.pallas_call(
        functools.partial(score_kernel, n_c, len(rows), picks, begin, starts),
        out_shape=(
            jax.ShapeDtypeStruct((n_r, c, r), jnp.float32),
            jax.ShapeDtypeStruct((2, n_out, r), jnp.float32),
        ),
        in_specs=[VMEM] * (n_c + len(rows) + len(early)),
        out_specs=(VMEM,) * 2,
        compiler_params=PARAMS,
        cost_estimate=pl.CostEstimate(
            flops=2 * n_r * c * r * depth,
            bytes_accessed=2 * (n_r * r + c) * depth,
            transcendentals=n_r * c * r,
        ),
        name="score_rows",
    )(*centers, *rows, *early)


def join_kernel(places, last, pair_ref, other_ref, out_ref):
    other = [jnp.concatenate([other_ref[i, p : p + 1] for p in places]) for i in range(2)]
    top, total = merge((pair_ref[0], pair_ref[1]), other)
    if last:
        out_ref[...] = top + jnp.log(total)
    else:
        out_ref[0] = top
        out_ref[1] = total


def join(pairs, mask, order, last):
    other = swap(pairs, "cent", len(order), mask)
    places = [order.index(j ^ mask) for j in order]
    return pl.pallas_call(
        functools.partial(join_kernel, places, last),
        out_shape=jax.ShapeDtypeStruct(pairs.shape[1:] if last else pairs.shape, jnp.float32),
        in_specs=[VMEM] * 2,
        out_specs=VMEM,
        compiler_params=PARAMS,
        name="join_rows",
    )(pairs, other)


def gather_kernel(core_ref, all_ref, out_ref):
    n, half = all_ref.shape[0], out_ref.shape[0] // 2
    of_core = []
    for core in range(2):
        top, total = all_ref[core, 0], all_ref[core, 1]
        for i in range(core + 2, n, 2):
            top, total = merge((top, total), (all_ref[i, 0], all_ref[i, 1]))
        of_core.append((top, total))
    other = [jnp.concatenate([x[half:], x[:half]]) for x in of_core[1]]
    top, total = merge(of_core[0], other)
    lognorm = top + jnp.log(total)
    swapped = jnp.concatenate([lognorm[half:], lognorm[:half]])
    out_ref[...] = jnp.where(core_ref[0] == 1, swapped, lognorm)


def gather_totals(pairs, size):
    sent = jnp.broadcast_to(pairs, (size,) + pairs.shape)
    got = lax.all_to_all(sent, "cent", 0, 0, tiled=True)
    core = jnp.reshape(lax.axis_index("cent") & 1, (1,))
    return pl.pallas_call(
        gather_kernel,
        out_shape=jax.ShapeDtypeStruct(pairs.shape[1:], jnp.float32),
        in_specs=[pl.BlockSpec(memory_space=pltpu.SMEM), VMEM],
        out_specs=VMEM,
        compiler_params=PARAMS,
        name="join_rows",
    )(core, got)


def sums_kernel(n_parts, picks, parts, lognorm_ref, *refs):
    score_refs, row_refs = refs[:n_parts], refs[n_parts : -len(parts)]
    outs = refs[-len(parts) :]
    r = lognorm_ref.shape[1]
    ones = jnp.ones((SIDE, r), jnp.bfloat16)
    for out, (places, size, unit) in zip(outs, parts):
        total, tally = None, None
        for j, (i, at) in enumerate(picks):
            k, block, first = places[j]
            s = score_refs[k][block, first : first + size, :]
            resp = jnp.exp(s - lognorm_ref[j : j + 1]).astype(jnp.bfloat16)
            more = jnp.dot(resp, row_refs[i][at : at + r], preferred_element_type=jnp.float32)
            count = lax.dot_general(
                ones, resp, (((1,), (1,)), ((), ())), preferred_element_type=jnp.float32
            )
            total = more if total is None else total + more
            tally = count if tally is None else tally + count
        wide = jnp.concatenate(
            [tally, jnp.zeros((SIDE, total.shape[1] - size), jnp.float32)], axis=1
        )
        if unit:
            total, wide = pack(total, wide[0:1], unit)
        out[0:size] = total
        out[size : size + SIDE] = wide


def pack(total, tally, unit):
    peak = jnp.max(jnp.abs(total), axis=0, keepdims=True)
    power = jnp.clip(jnp.ceil(jnp.log2(peak)), -100.0, 100.0)
    high = jnp.floor(tally * unit)
    rest = (tally * unit - high) * 1024.0
    middle = jnp.floor(rest)
    low = (rest - middle) * 1024.0
    blank = jnp.zeros((SIDE - 4, total.shape[1]), jnp.float32)
    return total * jnp.exp2(14.0 - power), jnp.concatenate([power, high, middle, low, blank])


def unpack(values, unit):
    size = values.shape[0] - SIDE
    power, high, middle, low = (values[size + i : size + i + 1] for i in range(4))
    tally = (high + (middle + low * (1.0 / 1024.0)) * (1.0 / 1024.0)) * (1.0 / unit)
    return values[:size] * jnp.exp2(power - 14.0), tally


def relay_kernel(unit, own_ref, got_ref, out_ref):
    size = own_ref.shape[0] - SIDE
    more, count = unpack(got_ref[...], unit)
    total, wide = pack(own_ref[0:size] + more, own_ref[size : size + 1] + count, unit * 0.5)
    out_ref[0:size] = total
    out_ref[size : size + SIDE] = wide


def relay(own, got, unit):
    return pl.pallas_call(
        functools.partial(relay_kernel, unit),
        out_shape=jax.ShapeDtypeStruct(own.shape, jnp.float32),
        in_specs=[VMEM] * 2,
        out_specs=VMEM,
        compiler_params=PARAMS,
        name="relay_sums",
    )(own, got)


def weighted(parts, lognorm, scores, rows, picks):
    size = parts[0][1]
    depth = rows[0].shape[1]
    n_r, r = lognorm.shape
    return pl.pallas_call(
        functools.partial(sums_kernel, len(scores), picks, parts),
        out_shape=[jax.ShapeDtypeStruct((size + SIDE, depth), jnp.float32) for _ in parts],
        in_specs=[VMEM] * (1 + len(scores) + len(rows)),
        out_specs=[VMEM] * len(parts),
        compiler_params=PARAMS,
        cost_estimate=pl.CostEstimate(
            flops=2 * len(parts) * n_r * size * r * depth,
            bytes_accessed=2 * n_r * r * depth,
            transcendentals=len(parts) * n_r * size * r,
        ),
        name="weighted_sums",
    )(lognorm, *scores, *rows)


def local(n_dp, n_cent, embeddings, codebook):
    own_rows = embeddings.shape[0]
    size = codebook.shape[0]
    unit = 1024.0 / (own_rows * n_cent)
    rounded = codebook.astype(jnp.bfloat16)
    centers = [rounded] + [swap(rounded, "dp", n_dp, m) for m in range(1, n_dp)]
    if n_cent == 8:
        groups = [[i for i in range(n_cent) if i % 2 == core] for core in range(2)]
        sent = jnp.broadcast_to(embeddings, (n_cent // 2,) + embeddings.shape)
        four = lax.all_to_all(sent, "cent", 0, 0, axis_index_groups=groups, tiled=True)
        four = four.reshape(-1, embeddings.shape[1])
        give, centers = lax.optimization_barrier((four, centers))
        rows = [four, swap(give, "cent", n_cent, 1)]
        picks = [(i, j * own_rows) for i in range(2) for j in range(4)]
        s_0, pairs = score(centers, rows[:1], own_rows, picks[:4])
        s_1, pairs = score(centers, rows[1:], own_rows, picks[:4], [pairs], 4)
        scores = [s_0, s_1]
        places = [(i, j) for i in range(2) for j in range(4)]
        last_scores = scores
        last_places = [(i, j, (n_dp - 1) * size) for i, j in places]
        lognorm = gather_totals(pairs, n_cent)
        own_norm = lax.dynamic_slice_in_dim(lognorm, lax.axis_index("cent") >> 1, 1)[0]
    else:
        rows = [embeddings] + [swap(embeddings, "cent", n_cent, m) for m in range(1, n_cent)]
        order = list(range(n_cent))
        picks = [(j, 0) for j in order]
        s_0, pair_0 = score(centers[:-1], rows, own_rows, picks)
        scores = [s_0]
        places = [(0, j) for j in order]
        s_1, pairs = score(centers[-1:], rows, own_rows, picks, [pair_0])
        last_scores, last_places = [s_1], [(0, j, 0) for j in order]
        mask = 1
        while mask < n_cent:
            pairs = join(pairs, mask, order, 2 * mask >= n_cent)
            mask *= 2
        lognorm = pairs
        own_norm = lognorm[0]
    def part(k, unit):
        return [(i, j, k * size) for i, j in places], size, unit

    (first,) = weighted([(last_places, size, unit)], lognorm, last_scores, rows, picks)
    first = first.astype(jnp.float16)
    if n_dp == 4:
        first = swap(first, "dp", n_dp, 1)
        parts = [part(2, 0), part(1, unit), part(0, 0)]
        far_out, near_out, own = weighted(parts, lognorm, scores, rows, picks)
        far_out = relay(far_out, first.astype(jnp.float32), unit)
        far_out, near_out = lax.optimization_barrier((far_out, near_out))
        far_out = swap(far_out.astype(jnp.float16), "dp", n_dp, 2)
        near_out = swap(near_out.astype(jnp.float16), "dp", n_dp, 1)
        got = [(near_out, unit), (far_out, unit * 0.5)]
    else:
        parts = [part(k, unit if k else 0) for k in range(n_dp - 1)]
        out = weighted(parts, lognorm, scores, rows, picks)
        own = out[0]
        sent = [o.astype(jnp.float16) for o in out[1:]] + [first]
        got = [(swap(m, "dp", n_dp, k + 1), unit) for k, m in enumerate(sent)]
    owner_total, owner_tally = own[:size], own[size, :size]
    for message, of in got:
        more, count = unpack(message.astype(jnp.float32), of)
        owner_total = owner_total + more
        owner_tally = owner_tally + count[0, :size]
    new_codebook = (owner_total + PRIOR * codebook) / (owner_tally + PRIOR)[:, None]
    return (new_codebook, owner_tally, own_norm)


def solution(mesh):
    n_dp, n_cent = mesh.shape["dp"], mesh.shape["cent"]

    def run(embeddings, codebook):
        return local(n_dp, n_cent, embeddings, codebook)

    return jax.shard_map(
        run,
        mesh=mesh,
        in_specs=(P(("dp", "cent"), None), P(("cent", "dp"), None)),
        out_specs=(P(("cent", "dp"), None), P(("cent", "dp")), P(("dp", "cent"))),
        check_vma=False,
    )
```

```python
import functools

import jax
import jax.numpy as jnp
from jax import lax
from jax.experimental import pallas as pl
from jax.experimental.pallas import tpu as pltpu
from jax.sharding import PartitionSpec as P

TEMPER = 0.8
PRIOR = 1.0
SIDE = 8
VMEM = pl.BlockSpec(memory_space=pltpu.VMEM)
PARAMS = pltpu.CompilerParams(vmem_limit_bytes=24 << 20)


def swap(x, axis, size, mask):
    return lax.ppermute(x, axis, [(i, i ^ mask) for i in range(size)])


def merge(a, b):
    top = jnp.maximum(a[0], b[0])
    return top, a[1] * jnp.exp(a[0] - top) + b[1] * jnp.exp(b[0] - top)


def score_kernel(n_cent, n_rows, picks, begin, starts, *refs):
    cent_refs, row_refs = refs[:n_cent], refs[n_cent : n_cent + n_rows]
    early_refs = refs[n_cent + n_rows : -2]
    score_ref, pair_ref = refs[-2:]
    r = score_ref.shape[2]
    centers = jnp.concatenate([ref[...] for ref in cent_refs], axis=0)
    half = 0.5 * jnp.sum(jnp.square(centers.astype(jnp.float32)), axis=1, keepdims=True)
    for j, (i, at) in enumerate(picks):
        product = lax.dot_general(
            centers,
            row_refs[i][at : at + r],
            (((1,), (1,)), ((), ())),
            preferred_element_type=jnp.float32,
        )
        s = (product - half) * (1.0 / TEMPER)
        top = jnp.max(s, axis=0, keepdims=True)
        score_ref[j] = s
        total = jnp.sum(jnp.exp(s - top), axis=0, keepdims=True)
        at = begin + j
        for ref, start in zip(early_refs, starts):
            if start <= at < start + ref.shape[1]:
                k = slice(at - start, at - start + 1)
                top, total = merge((top, total), (ref[0, k], ref[1, k]))
        pair_ref[0, at : at + 1] = top
        pair_ref[1, at : at + 1] = total
    for ref, start in zip(early_refs, starts):
        for k in range(ref.shape[1]):
            if not begin <= start + k < begin + len(picks):
                pair_ref[:, start + k : start + k + 1] = ref[:, k : k + 1]


def score(centers, rows, r, picks, early=(), begin=0):
    n_c, n_r = len(centers), len(picks)
    depth = rows[0].shape[1]
    c = sum(x.shape[0] for x in centers)
    starts = [sum(e.shape[1] for e in early[:i]) for i in range(len(early))]
    n_out = max(begin + n_r, sum(e.shape[1] for e in early))
    return pl.pallas_call(
        functools.partial(score_kernel, n_c, len(rows), picks, begin, starts),
        out_shape=(
            jax.ShapeDtypeStruct((n_r, c, r), jnp.float32),
            jax.ShapeDtypeStruct((2, n_out, r), jnp.float32),
        ),
        in_specs=[VMEM] * (n_c + len(rows) + len(early)),
        out_specs=(VMEM,) * 2,
        compiler_params=PARAMS,
        cost_estimate=pl.CostEstimate(
            flops=2 * n_r * c * r * depth,
            bytes_accessed=2 * (n_r * r + c) * depth,
            transcendentals=n_r * c * r,
        ),
        name="score_rows",
    )(*centers, *rows, *early)


def join_kernel(places, last, pair_ref, other_ref, out_ref):
    other = [jnp.concatenate([other_ref[i, p : p + 1] for p in places]) for i in range(2)]
    top, total = merge((pair_ref[0], pair_ref[1]), other)
    if last:
        out_ref[...] = top + jnp.log(total)
    else:
        out_ref[0] = top
        out_ref[1] = total


def join(pairs, mask, order, last):
    other = swap(pairs, "cent", len(order), mask)
    places = [order.index(j ^ mask) for j in order]
    return pl.pallas_call(
        functools.partial(join_kernel, places, last),
        out_shape=jax.ShapeDtypeStruct(pairs.shape[1:] if last else pairs.shape, jnp.float32),
        in_specs=[VMEM] * 2,
        out_specs=VMEM,
        compiler_params=PARAMS,
        name="join_rows",
    )(pairs, other)


def sums_kernel(n_parts, picks, parts, lognorm_ref, *refs):
    score_refs, row_refs = refs[:n_parts], refs[n_parts : -len(parts)]
    outs = refs[-len(parts) :]
    r = lognorm_ref.shape[1]
    ones = jnp.ones((SIDE, r), jnp.bfloat16)
    for out, (places, size, unit) in zip(outs, parts):
        total, tally = None, None
        for j, (i, at) in enumerate(picks):
            k, block, first = places[j]
            s = score_refs[k][block, first : first + size, :]
            resp = jnp.exp(s - lognorm_ref[j : j + 1]).astype(jnp.bfloat16)
            more = jnp.dot(resp, row_refs[i][at : at + r], preferred_element_type=jnp.float32)
            count = lax.dot_general(
                ones, resp, (((1,), (1,)), ((), ())), preferred_element_type=jnp.float32
            )
            total = more if total is None else total + more
            tally = count if tally is None else tally + count
        wide = jnp.concatenate(
            [tally, jnp.zeros((SIDE, total.shape[1] - size), jnp.float32)], axis=1
        )
        if unit:
            total, wide = pack(total, wide[0:1], unit)
        out[0:size] = total
        out[size : size + SIDE] = wide


def pack(total, tally, unit):
    peak = jnp.max(jnp.abs(total), axis=0, keepdims=True)
    power = jnp.clip(jnp.ceil(jnp.log2(peak)), -100.0, 100.0)
    high = jnp.floor(tally * unit)
    rest = (tally * unit - high) * 1024.0
    middle = jnp.floor(rest)
    low = (rest - middle) * 1024.0
    blank = jnp.zeros((SIDE - 4, total.shape[1]), jnp.float32)
    return total * jnp.exp2(14.0 - power), jnp.concatenate([power, high, middle, low, blank])


def unpack(values, unit):
    size = values.shape[0] - SIDE
    power, high, middle, low = (values[size + i : size + i + 1] for i in range(4))
    tally = (high + (middle + low * (1.0 / 1024.0)) * (1.0 / 1024.0)) * (1.0 / unit)
    return values[:size] * jnp.exp2(power - 14.0), tally


def relay_kernel(unit, own_ref, got_ref, out_ref):
    size = own_ref.shape[0] - SIDE
    more, count = unpack(got_ref[...], unit)
    total, wide = pack(own_ref[0:size] + more, own_ref[size : size + 1] + count, unit * 0.5)
    out_ref[0:size] = total
    out_ref[size : size + SIDE] = wide


def relay(own, got, unit):
    return pl.pallas_call(
        functools.partial(relay_kernel, unit),
        out_shape=jax.ShapeDtypeStruct(own.shape, jnp.float32),
        in_specs=[VMEM] * 2,
        out_specs=VMEM,
        compiler_params=PARAMS,
        name="relay_sums",
    )(own, got)


def weighted(parts, lognorm, scores, rows, picks):
    size = parts[0][1]
    depth = rows[0].shape[1]
    n_r, r = lognorm.shape
    return pl.pallas_call(
        functools.partial(sums_kernel, len(scores), picks, parts),
        out_shape=[jax.ShapeDtypeStruct((size + SIDE, depth), jnp.float32) for _ in parts],
        in_specs=[VMEM] * (1 + len(scores) + len(rows)),
        out_specs=[VMEM] * len(parts),
        compiler_params=PARAMS,
        cost_estimate=pl.CostEstimate(
            flops=2 * len(parts) * n_r * size * r * depth,
            bytes_accessed=2 * n_r * r * depth,
            transcendentals=len(parts) * n_r * size * r,
        ),
        name="weighted_sums",
    )(lognorm, *scores, *rows)


def local(n_dp, n_cent, embeddings, codebook):
    own_rows = embeddings.shape[0]
    size = codebook.shape[0]
    unit = 1024.0 / (own_rows * n_cent)
    rounded = codebook.astype(jnp.bfloat16)
    if n_cent == 8:
        half = own_rows // 2
        from_x = swap(embeddings, "cent", n_cent, 2)
        from_y = swap(embeddings, "cent", n_cent, 4)
    most = [rounded] + [swap(rounded, "dp", n_dp, m) for m in range(1, n_dp - 1)]
    final = [swap(rounded, "dp", n_dp, n_dp - 1)]
    end = (n_dp - 1) * size
    if n_cent == 8:
        diag_top = swap(from_x[:half], "cent", n_cent, 4)
        diag_low = swap(from_y[half:], "cent", n_cent, 2)
        four = jnp.concatenate([embeddings, from_x, from_y, diag_top, diag_low], axis=0)
        give, most, final = lax.optimization_barrier((four, most, final))
        rows, order = [four, swap(give, "cent", n_cent, 1)], [0, 2, 4, 6, 1, 3, 5, 7]
        picks = [(i, j * own_rows) for i in range(2) for j in range(4)]
        s_0, pairs = score(most + final, rows[:1], own_rows, picks[:4])
        s_1, pairs = score(most + final, rows[1:], own_rows, picks[:4], [pairs], 4)
        scores = last_scores = [s_0, s_1]
        places = [(i, j) for i in range(2) for j in range(4)]
        last_places = [(i, j, end) for i, j in places]
    else:
        rows = [embeddings] + [swap(embeddings, "cent", n_cent, m) for m in range(1, n_cent)]
        order = list(range(n_cent))
        picks = [(j, 0) for j in order]
        s_0, pair_0 = score(most, rows, own_rows, picks)
        scores = [s_0]
        places = [(0, j) for j in order]
        s_1, pairs = score(final, rows, own_rows, picks, [pair_0])
        last_scores, last_places = [s_1], [(0, j, 0) for j in order]
    mask = 1
    while mask < n_cent:
        pairs = join(pairs, mask, order, 2 * mask >= n_cent)
        mask *= 2
    lognorm = pairs

    def part(k, unit):
        return [(i, j, k * size) for i, j in places], size, unit

    (first,) = weighted([(last_places, size, unit)], lognorm, last_scores, rows, picks)
    first = first.astype(jnp.float16)
    if n_dp == 4:
        first = swap(first, "dp", n_dp, 1)
        parts = [part(2, 0), part(1, unit), part(0, 0)]
        far_out, near_out, own = weighted(parts, lognorm, scores, rows, picks)
        far_out = relay(far_out, first.astype(jnp.float32), unit)
        far_out, near_out = lax.optimization_barrier((far_out, near_out))
        far_out = swap(far_out.astype(jnp.float16), "dp", n_dp, 2)
        near_out = swap(near_out.astype(jnp.float16), "dp", n_dp, 1)
        got = [(near_out, unit), (far_out, unit * 0.5)]
    else:
        parts = [part(k, unit if k else 0) for k in range(n_dp - 1)]
        out = weighted(parts, lognorm, scores, rows, picks)
        own = out[0]
        sent = [o.astype(jnp.float16) for o in out[1:]] + [first]
        got = [(swap(m, "dp", n_dp, k + 1), unit) for k, m in enumerate(sent)]
    owner_total, owner_tally = own[:size], own[size, :size]
    for message, of in got:
        more, count = unpack(message.astype(jnp.float32), of)
        owner_total = owner_total + more
        owner_tally = owner_tally + count[0, :size]
    new_codebook = (owner_total + PRIOR * codebook) / (owner_tally + PRIOR)[:, None]
    return (new_codebook, owner_tally, lognorm[0])


def solution(mesh):
    n_dp, n_cent = mesh.shape["dp"], mesh.shape["cent"]

    def run(embeddings, codebook):
        return local(n_dp, n_cent, embeddings, codebook)

    return jax.shard_map(
        run,
        mesh=mesh,
        in_specs=(P(("dp", "cent"), None), P(("cent", "dp"), None)),
        out_specs=(P(("cent", "dp"), None), P(("cent", "dp")), P(("dp", "cent"))),
        check_vma=False,
    )
```

```python
import functools

import jax
import jax.numpy as jnp
from jax import lax
from jax.experimental import pallas as pl
from jax.experimental.pallas import tpu as pltpu
from jax.sharding import PartitionSpec as P

TEMPER = 0.8
PRIOR = 1.0
SIDE = 8
VMEM = pl.BlockSpec(memory_space=pltpu.VMEM)
PARAMS = pltpu.CompilerParams(vmem_limit_bytes=24 << 20)


def swap(x, axis, size, mask):
    return lax.ppermute(x, axis, [(i, i ^ mask) for i in range(size)])


def merge(a, b):
    top = jnp.maximum(a[0], b[0])
    return top, a[1] * jnp.exp(a[0] - top) + b[1] * jnp.exp(b[0] - top)


def score_kernel(n_cent, n_rows, picks, begin, starts, *refs):
    cent_refs, row_refs = refs[:n_cent], refs[n_cent : n_cent + n_rows]
    early_refs = refs[n_cent + n_rows : -2]
    score_ref, pair_ref = refs[-2:]
    r = score_ref.shape[2]
    centers = jnp.concatenate([ref[...] for ref in cent_refs], axis=0)
    half = 0.5 * jnp.sum(jnp.square(centers.astype(jnp.float32)), axis=1, keepdims=True)
    for j, (i, at) in enumerate(picks):
        product = lax.dot_general(
            centers,
            row_refs[i][at : at + r],
            (((1,), (1,)), ((), ())),
            preferred_element_type=jnp.float32,
        )
        s = (product - half) * (1.0 / TEMPER)
        top = jnp.max(s, axis=0, keepdims=True)
        score_ref[j] = s
        total = jnp.sum(jnp.exp(s - top), axis=0, keepdims=True)
        at = begin + j
        for ref, start in zip(early_refs, starts):
            if start <= at < start + ref.shape[1]:
                k = slice(at - start, at - start + 1)
                top, total = merge((top, total), (ref[0, k], ref[1, k]))
        pair_ref[0, at : at + 1] = top
        pair_ref[1, at : at + 1] = total
    for ref, start in zip(early_refs, starts):
        for k in range(ref.shape[1]):
            if not begin <= start + k < begin + len(picks):
                pair_ref[:, start + k : start + k + 1] = ref[:, k : k + 1]


def score(centers, rows, r, picks, early=(), begin=0):
    n_c, n_r = len(centers), len(picks)
    depth = rows[0].shape[1]
    c = sum(x.shape[0] for x in centers)
    starts = [sum(e.shape[1] for e in early[:i]) for i in range(len(early))]
    n_out = max(begin + n_r, sum(e.shape[1] for e in early))
    return pl.pallas_call(
        functools.partial(score_kernel, n_c, len(rows), picks, begin, starts),
        out_shape=(
            jax.ShapeDtypeStruct((n_r, c, r), jnp.float32),
            jax.ShapeDtypeStruct((2, n_out, r), jnp.float32),
        ),
        in_specs=[VMEM] * (n_c + len(rows) + len(early)),
        out_specs=(VMEM,) * 2,
        compiler_params=PARAMS,
        cost_estimate=pl.CostEstimate(
            flops=2 * n_r * c * r * depth,
            bytes_accessed=2 * (n_r * r + c) * depth,
            transcendentals=n_r * c * r,
        ),
        name="score_rows",
    )(*centers, *rows, *early)


def join_kernel(places, last, pair_ref, *refs):
    out_ref = refs[-1]
    top, total = pair_ref[0], pair_ref[1]
    for ref, where in zip(refs[:-1], places):
        other = [jnp.concatenate([ref[i, p : p + 1] for p in where]) for i in range(2)]
        top, total = merge((top, total), other)
    if last:
        out_ref[...] = top + jnp.log(total)
    else:
        out_ref[0] = top
        out_ref[1] = total


def join(pairs, masks, order, last):
    others = [swap(pairs, "cent", len(order), mask) for mask in masks]
    places = [[order.index(j ^ mask) for j in order] for mask in masks]
    return pl.pallas_call(
        functools.partial(join_kernel, places, last),
        out_shape=jax.ShapeDtypeStruct(pairs.shape[1:] if last else pairs.shape, jnp.float32),
        in_specs=[VMEM] * (1 + len(others)),
        out_specs=VMEM,
        compiler_params=PARAMS,
        name="join_rows",
    )(pairs, *others)


def sums_kernel(n_parts, picks, parts, lognorm_ref, *refs):
    score_refs, row_refs = refs[:n_parts], refs[n_parts : -len(parts)]
    outs = refs[-len(parts) :]
    r = lognorm_ref.shape[1]
    ones = jnp.ones((SIDE, r), jnp.bfloat16)
    for out, (places, size, unit) in zip(outs, parts):
        total, tally = None, None
        for j, (i, at) in enumerate(picks):
            k, block, first = places[j]
            s = score_refs[k][block, first : first + size, :]
            resp = jnp.exp(s - lognorm_ref[j : j + 1]).astype(jnp.bfloat16)
            more = jnp.dot(resp, row_refs[i][at : at + r], preferred_element_type=jnp.float32)
            count = lax.dot_general(
                ones, resp, (((1,), (1,)), ((), ())), preferred_element_type=jnp.float32
            )
            total = more if total is None else total + more
            tally = count if tally is None else tally + count
        wide = jnp.concatenate(
            [tally, jnp.zeros((SIDE, total.shape[1] - size), jnp.float32)], axis=1
        )
        if unit:
            total, wide = pack(total, wide[0:1], unit)
        out[0:size] = total
        out[size : size + SIDE] = wide


def pack(total, tally, unit):
    peak = jnp.max(jnp.abs(total), axis=0, keepdims=True)
    power = jnp.clip(jnp.ceil(jnp.log2(peak)), -100.0, 100.0)
    high = jnp.floor(tally * unit)
    rest = (tally * unit - high) * 1024.0
    middle = jnp.floor(rest)
    low = (rest - middle) * 1024.0
    blank = jnp.zeros((SIDE - 4, total.shape[1]), jnp.float32)
    return total * jnp.exp2(14.0 - power), jnp.concatenate([power, high, middle, low, blank])


def unpack(values, unit):
    size = values.shape[0] - SIDE
    power, high, middle, low = (values[size + i : size + i + 1] for i in range(4))
    tally = (high + (middle + low * (1.0 / 1024.0)) * (1.0 / 1024.0)) * (1.0 / unit)
    return values[:size] * jnp.exp2(power - 14.0), tally


def relay_kernel(unit, own_ref, got_ref, out_ref):
    size = own_ref.shape[0] - SIDE
    more, count = unpack(got_ref[...], unit)
    total, wide = pack(own_ref[0:size] + more, own_ref[size : size + 1] + count, unit * 0.5)
    out_ref[0:size] = total
    out_ref[size : size + SIDE] = wide


def relay(own, got, unit):
    return pl.pallas_call(
        functools.partial(relay_kernel, unit),
        out_shape=jax.ShapeDtypeStruct(own.shape, jnp.float32),
        in_specs=[VMEM] * 2,
        out_specs=VMEM,
        compiler_params=PARAMS,
        name="relay_sums",
    )(own, got)


def weighted(parts, lognorm, scores, rows, picks):
    size = parts[0][1]
    depth = rows[0].shape[1]
    n_r, r = lognorm.shape
    return pl.pallas_call(
        functools.partial(sums_kernel, len(scores), picks, parts),
        out_shape=[jax.ShapeDtypeStruct((size + SIDE, depth), jnp.float32) for _ in parts],
        in_specs=[VMEM] * (1 + len(scores) + len(rows)),
        out_specs=[VMEM] * len(parts),
        compiler_params=PARAMS,
        cost_estimate=pl.CostEstimate(
            flops=2 * len(parts) * n_r * size * r * depth,
            bytes_accessed=2 * n_r * r * depth,
            transcendentals=len(parts) * n_r * size * r,
        ),
        name="weighted_sums",
    )(lognorm, *scores, *rows)


def local(n_dp, n_cent, embeddings, codebook):
    own_rows = embeddings.shape[0]
    size = codebook.shape[0]
    unit = 1024.0 / (own_rows * n_cent)
    rounded = codebook.astype(jnp.bfloat16)
    if n_cent == 8:
        half = own_rows // 2
        from_x = swap(embeddings, "cent", n_cent, 2)
        from_y = swap(embeddings, "cent", n_cent, 4)
    if n_dp == 4:
        far = swap(rounded, "dp", n_dp, 2)
        near = swap(rounded, "dp", n_dp, 1)
        most, final = [rounded, near, far], [swap(far, "dp", n_dp, 1)]
    else:
        most = [rounded] + [swap(rounded, "dp", n_dp, m) for m in range(1, n_dp - 1)]
        final = [swap(rounded, "dp", n_dp, n_dp - 1)]
    end = (n_dp - 1) * size
    if n_cent == 8:
        diag_top = swap(from_x[:half], "cent", n_cent, 4)
        diag_low = swap(from_y[half:], "cent", n_cent, 2)
        four = jnp.concatenate([embeddings, from_x, from_y, diag_top, diag_low], axis=0)
        give, most, final = lax.optimization_barrier((four, most, final))
        rows, order = [four, swap(give, "cent", n_cent, 1)], [0, 2, 4, 6, 1, 3, 5, 7]
        picks = [(i, j * own_rows) for i in range(2) for j in range(4)]
        s_0, pairs = score(most + final, rows[:1], own_rows, picks[:4])
        s_1, pairs = score(most + final, rows[1:], own_rows, picks[:4], [pairs], 4)
        scores = last_scores = [s_0, s_1]
        places = [(i, j) for i in range(2) for j in range(4)]
        last_places = [(i, j, end) for i, j in places]
    else:
        rows = [embeddings] + [swap(embeddings, "cent", n_cent, m) for m in range(1, n_cent)]
        order = list(range(n_cent))
        picks = [(j, 0) for j in order]
        s_0, pair_0 = score(most, rows, own_rows, picks)
        scores = [s_0]
        places = [(0, j) for j in order]
        s_1, pairs = score(final, rows, own_rows, picks, [pair_0])
        last_scores, last_places = [s_1], [(0, j, 0) for j in order]
    bits = [1 << i for i in range(n_cent.bit_length() - 1)]
    rounds = [[1], [2, 4, 6]] if n_cent == 8 else [[bit] for bit in bits]
    for masks in rounds:
        pairs = join(pairs, masks, order, masks is rounds[-1])
    lognorm = pairs

    def part(k, unit):
        return [(i, j, k * size) for i, j in places], size, unit

    (first,) = weighted([(last_places, size, unit)], lognorm, last_scores, rows, picks)
    first = first.astype(jnp.float16)
    if n_dp == 4:
        first = swap(first, "dp", n_dp, 1)
        parts = [part(2, 0), part(1, unit), part(0, 0)]
        far_out, near_out, own = weighted(parts, lognorm, scores, rows, picks)
        far_out = relay(far_out, first.astype(jnp.float32), unit).astype(jnp.float16)
        far_out, near_out = lax.optimization_barrier((far_out, near_out))
        far_out = swap(far_out, "dp", n_dp, 2)
        near_out = swap(near_out.astype(jnp.float16), "dp", n_dp, 1)
        got = [(near_out, unit), (far_out, unit * 0.5)]
    else:
        parts = [part(k, unit if k else 0) for k in range(n_dp - 1)]
        out = weighted(parts, lognorm, scores, rows, picks)
        own = out[0]
        sent = [o.astype(jnp.float16) for o in out[1:]] + [first]
        got = [(swap(m, "dp", n_dp, k + 1), unit) for k, m in enumerate(sent)]
    owner_total, owner_tally = own[:size], own[size, :size]
    for message, of in got:
        more, count = unpack(message.astype(jnp.float32), of)
        owner_total = owner_total + more
        owner_tally = owner_tally + count[0, :size]
    new_codebook = (owner_total + PRIOR * codebook) / (owner_tally + PRIOR)[:, None]
    return (new_codebook, owner_tally, lognorm[0])


def solution(mesh):
    n_dp, n_cent = mesh.shape["dp"], mesh.shape["cent"]

    def run(embeddings, codebook):
        return local(n_dp, n_cent, embeddings, codebook)

    return jax.shard_map(
        run,
        mesh=mesh,
        in_specs=(P(("dp", "cent"), None), P(("cent", "dp"), None)),
        out_specs=(P(("cent", "dp"), None), P(("cent", "dp")), P(("dp", "cent"))),
        check_vma=False,
    )
```

```python
import functools

import jax
import jax.numpy as jnp
from jax import lax
from jax.experimental import pallas as pl
from jax.experimental.pallas import tpu as pltpu
from jax.sharding import PartitionSpec as P

TEMPER = 0.8
PRIOR = 1.0
SIDE = 8
VMEM = pl.BlockSpec(memory_space=pltpu.VMEM)
PARAMS = pltpu.CompilerParams(vmem_limit_bytes=24 << 20)


def swap(x, axis, size, mask):
    return lax.ppermute(x, axis, [(i, i ^ mask) for i in range(size)])


def merge(a, b):
    top = jnp.maximum(a[0], b[0])
    return top, a[1] * jnp.exp(a[0] - top) + b[1] * jnp.exp(b[0] - top)


def score_kernel(n_cent, n_rows, picks, begin, starts, *refs):
    cent_refs, row_refs = refs[:n_cent], refs[n_cent : n_cent + n_rows]
    early_refs = refs[n_cent + n_rows : -2]
    score_ref, pair_ref = refs[-2:]
    r = score_ref.shape[2]
    centers = jnp.concatenate([ref[...] for ref in cent_refs], axis=0)
    half = 0.5 * jnp.sum(jnp.square(centers.astype(jnp.float32)), axis=1, keepdims=True)
    for j, (i, at) in enumerate(picks):
        product = lax.dot_general(
            centers,
            row_refs[i][at : at + r],
            (((1,), (1,)), ((), ())),
            preferred_element_type=jnp.float32,
        )
        s = (product - half) * (1.0 / TEMPER)
        top = jnp.max(s, axis=0, keepdims=True)
        score_ref[j] = s
        total = jnp.sum(jnp.exp(s - top), axis=0, keepdims=True)
        at = begin + j
        for ref, start in zip(early_refs, starts):
            if start <= at < start + ref.shape[1]:
                k = slice(at - start, at - start + 1)
                top, total = merge((top, total), (ref[0, k], ref[1, k]))
        pair_ref[0, at : at + 1] = top
        pair_ref[1, at : at + 1] = total
    for ref, start in zip(early_refs, starts):
        for k in range(ref.shape[1]):
            if not begin <= start + k < begin + len(picks):
                pair_ref[:, start + k : start + k + 1] = ref[:, k : k + 1]


def score(centers, rows, r, picks, early=(), begin=0):
    n_c, n_r = len(centers), len(picks)
    depth = rows[0].shape[1]
    c = sum(x.shape[0] for x in centers)
    starts = [sum(e.shape[1] for e in early[:i]) for i in range(len(early))]
    n_out = max(begin + n_r, sum(e.shape[1] for e in early))
    return pl.pallas_call(
        functools.partial(score_kernel, n_c, len(rows), picks, begin, starts),
        out_shape=(
            jax.ShapeDtypeStruct((n_r, c, r), jnp.float32),
            jax.ShapeDtypeStruct((2, n_out, r), jnp.float32),
        ),
        in_specs=[VMEM] * (n_c + len(rows) + len(early)),
        out_specs=(VMEM,) * 2,
        compiler_params=PARAMS,
        cost_estimate=pl.CostEstimate(
            flops=2 * n_r * c * r * depth,
            bytes_accessed=2 * (n_r * r + c) * depth,
            transcendentals=n_r * c * r,
        ),
        name="score_rows",
    )(*centers, *rows, *early)


def join_kernel(places, last, pair_ref, *refs):
    out_ref = refs[-1]
    top, total = pair_ref[0], pair_ref[1]
    for ref, where in zip(refs[:-1], places):
        other = [jnp.concatenate([ref[i, p : p + 1] for p in where]) for i in range(2)]
        top, total = merge((top, total), other)
    if last:
        out_ref[...] = top + jnp.log(total)
    else:
        out_ref[0] = top
        out_ref[1] = total


def join(pairs, masks, order, size, last):
    others = [swap(pairs, "cent", size, mask) for mask in masks]
    places = [[order.index(j ^ mask) for j in order] for mask in masks]
    return pl.pallas_call(
        functools.partial(join_kernel, places, last),
        out_shape=jax.ShapeDtypeStruct(pairs.shape[1:] if last else pairs.shape, jnp.float32),
        in_specs=[VMEM] * (1 + len(others)),
        out_specs=VMEM,
        compiler_params=PARAMS,
        name="join_rows",
    )(pairs, *others)


def sums_kernel(n_parts, picks, parts, lognorm_ref, *refs):
    score_refs, row_refs, out = refs[:n_parts], refs[n_parts:-1], refs[-1]
    r = lognorm_ref.shape[1]
    ones = jnp.ones((SIDE, r), jnp.bfloat16)
    for n, (places, size, unit) in enumerate(parts):
        total, tally = None, None
        for j, (i, at) in enumerate(picks):
            k, block, first = places[j]
            s = score_refs[k][block, first : first + size, :]
            resp = jnp.exp(s - lognorm_ref[j : j + 1]).astype(jnp.bfloat16)
            more = jnp.dot(resp, row_refs[i][at : at + r], preferred_element_type=jnp.float32)
            count = lax.dot_general(
                ones, resp, (((1,), (1,)), ((), ())), preferred_element_type=jnp.float32
            )
            total = more if total is None else total + more
            tally = count if tally is None else tally + count
        wide = jnp.concatenate(
            [tally, jnp.zeros((SIDE, total.shape[1] - size), jnp.float32)], axis=1
        )
        if unit:
            total, wide = pack(total, wide[0:1], unit)
        at = n * (size + SIDE)
        out[at : at + size] = total
        out[at + size : at + size + SIDE] = wide


def pack(total, tally, unit):
    peak = jnp.max(jnp.abs(total), axis=0, keepdims=True)
    power = jnp.clip(jnp.ceil(jnp.log2(peak)), -100.0, 100.0)
    high = jnp.floor(tally * unit)
    rest = (tally * unit - high) * 1024.0
    middle = jnp.floor(rest)
    low = (rest - middle) * 1024.0
    blank = jnp.zeros((SIDE - 4, total.shape[1]), jnp.float32)
    return total * jnp.exp2(14.0 - power), jnp.concatenate([power, high, middle, low, blank])


def unpack(values, unit):
    size = values.shape[0] - SIDE
    power, high, middle, low = (values[size + i : size + i + 1] for i in range(4))
    tally = (high + (middle + low * (1.0 / 1024.0)) * (1.0 / 1024.0)) * (1.0 / unit)
    return values[:size] * jnp.exp2(power - 14.0), tally


def relay_kernel(units, offsets, unit, *refs):
    own_ref, got_refs, out_ref = refs[0], refs[1:-1], refs[-1]
    size = out_ref.shape[0] - SIDE
    at = offsets[0]
    total, tally = own_ref[at : at + size], own_ref[at + size : at + size + 1]
    for ref, of, at in zip(got_refs, units, offsets[1:]):
        more, count = unpack(ref[at : at + size + SIDE], of)
        total, tally = total + more, tally + count
    total, wide = pack(total, tally, unit)
    out_ref[0:size] = total
    out_ref[size : size + SIDE] = wide


def relay(size, own, got, unit):
    arrays = [own[0]] + [g[0].astype(jnp.float32) for g in got]
    offsets = [(size + SIDE) * g[1] for g in [own] + got]
    return pl.pallas_call(
        functools.partial(relay_kernel, [g[2] for g in got], offsets, unit),
        out_shape=jax.ShapeDtypeStruct((size + SIDE, own[0].shape[1]), jnp.float32),
        in_specs=[VMEM] * len(arrays),
        out_specs=VMEM,
        compiler_params=PARAMS,
        name="relay_sums",
    )(*arrays).astype(jnp.float16)


def final_kernel(units, offsets, *refs):
    own_ref, got_refs, codebook_ref, new_ref, tally_ref = refs[0], refs[1:-3], *refs[-3:]
    size, depth = codebook_ref.shape
    at = offsets[0]
    total, tally = own_ref[at : at + size], own_ref[at + size : at + size + 1]
    for ref, of, at in zip(got_refs, units, offsets[1:]):
        more, count = unpack(ref[at : at + size + SIDE], of)
        total, tally = total + more, tally + count
    tally = tally[:, :size]
    tally_ref[...] = tally
    column = jnp.transpose(jnp.broadcast_to(tally, (size, size)))[:, 0:1]
    new_ref[...] = (total + PRIOR * codebook_ref[...]) / (column + PRIOR)


def finish(codebook, own, got):
    size = codebook.shape[0]
    arrays = [own[0]] + [g[0].astype(jnp.float32) for g in got] + [codebook]
    offsets = [(size + SIDE) * g[1] for g in [own] + got]
    new, tally = pl.pallas_call(
        functools.partial(final_kernel, [g[2] for g in got], offsets),
        out_shape=(
            jax.ShapeDtypeStruct(codebook.shape, jnp.float32),
            jax.ShapeDtypeStruct((1, size), jnp.float32),
        ),
        in_specs=[VMEM] * len(arrays),
        out_specs=(VMEM, VMEM),
        compiler_params=PARAMS,
        name="update_centroids",
    )(*arrays)
    return new, tally[0]


def weighted(parts, lognorm, scores, rows, picks):
    size = parts[0][1]
    depth = rows[0].shape[1]
    n_r, r = lognorm.shape
    return pl.pallas_call(
        functools.partial(sums_kernel, len(scores), picks, parts),
        out_shape=jax.ShapeDtypeStruct((len(parts) * (size + SIDE), depth), jnp.float32),
        in_specs=[VMEM] * (1 + len(scores) + len(rows)),
        out_specs=VMEM,
        compiler_params=PARAMS,
        cost_estimate=pl.CostEstimate(
            flops=2 * len(parts) * n_r * size * r * depth,
            bytes_accessed=2 * n_r * r * depth,
            transcendentals=len(parts) * n_r * size * r,
        ),
        name="weighted_sums",
    )(lognorm, *scores, *rows)


def local_split(n_dp, n_cent, embeddings, codebook):
    r, size = embeddings.shape[0], codebook.shape[0]
    order = [0, 2, 4, 6]
    from_x = swap(embeddings, "cent", n_cent, 2)
    from_y = swap(embeddings, "cent", n_cent, 4)
    top = swap(from_x[: r // 2], "cent", n_cent, 4)
    low = swap(from_y[r // 2 :], "cent", n_cent, 2)
    rows = [embeddings, from_x, from_y, jnp.concatenate([top, low], axis=0)]
    picks = [(i, 0) for i in range(4)]
    rounded = codebook.astype(jnp.bfloat16)
    far = swap(rounded, "dp", n_dp, 2)
    near = swap(rounded, "dp", n_dp, 1)
    last = swap(far, "dp", n_dp, 1)
    mine = jnp.concatenate([rounded, near, far], axis=0)
    theirs = swap(mine, "cent", n_cent, 1)
    last_theirs = swap(last, "cent", n_cent, 1)
    s_0, pair_0 = score([mine, theirs], rows[:3], r, picks[:3])
    s_1, pair_1 = score([mine, theirs], rows[3:], r, picks[:1])
    s_2, pairs = score([last, last_theirs], rows, r, picks, [pair_0, pair_1])
    lognorm = join(pairs, order[1:], order, n_cent, True)

    def part(core, k, unit):
        if k == 3:
            return [(2, j, core * size) for j in range(4)], size, unit
        first = (3 * core + k) * size
        return [(0, j, first) for j in range(3)] + [(1, 0, first)], size, unit

    def sums(parts, lognorm):
        return weighted(parts, lognorm, [s_0, s_1, s_2], rows, picks)

    unit = 1024.0 / (4 * r)
    over = sums([part(1, 3, unit)], lognorm).astype(jnp.float16)
    over, lognorm = lax.optimization_barrier((over, lognorm))
    over = swap(over, "cent", n_cent, 1)
    own = sums([part(0, 3, 0)], lognorm)
    rest = sums([part(1, k, unit) for k in (2, 1, 0)], lognorm).astype(jnp.float16)
    over, rest = lax.optimization_barrier((over, rest))
    first = relay(size, (own, 0), [(over, 0, unit)], unit * 0.5)
    lognorm, first, rest = lax.optimization_barrier((lognorm, first, rest))
    first = swap(first, "dp", n_dp, 1)
    over = swap(rest, "cent", n_cent, 1)
    own = sums([part(0, k, 0) for k in (2, 1)], lognorm)
    near_sum = relay(size, (own, 1), [(over, 1, unit)], unit * 0.5)
    far_sum = relay(size, (own, 0), [(over, 0, unit), (first, 0, unit * 0.5)], unit * 0.25)
    lognorm, far_sum = lax.optimization_barrier((lognorm, far_sum))
    own = sums([part(0, 0, 0)], lognorm)
    far_sum = swap(far_sum, "dp", n_dp, 2)
    near_sum = swap(near_sum, "dp", n_dp, 1)
    new_codebook, tally = finish(
        codebook,
        (own, 0),
        [(over, 2, unit), (near_sum, 0, unit * 0.5), (far_sum, 0, unit * 0.25)],
    )
    return new_codebook, tally, lognorm[0]


def local(n_dp, n_cent, embeddings, codebook):
    r, size = embeddings.shape[0], codebook.shape[0]
    order = list(range(n_cent))
    rows = [embeddings] + [swap(embeddings, "cent", n_cent, mask) for mask in order[1:]]
    picks = [(j, 0) for j in order]
    rounded = codebook.astype(jnp.bfloat16)
    centers = [rounded] + [swap(rounded, "dp", n_dp, mask) for mask in range(1, n_dp)]
    scores, pairs = [], ()
    for block in centers:
        s, pairs = score([block], rows, r, picks, [pairs] if scores else ())
        scores.append(s)
    for bit in range(n_cent.bit_length() - 1):
        pairs = join(pairs, [1 << bit], order, n_cent, 2 << bit >= n_cent)
    lognorm = pairs
    unit = 1024.0 / (n_cent * r)
    got = []
    for k in range(n_dp):
        places = [(0, j, 0) for j in order]
        block = weighted([(places, size, unit if k else 0)], lognorm, scores[k : k + 1], rows, picks)
        if k:
            got.append((swap(block.astype(jnp.float16), "dp", n_dp, k), 0, unit))
        else:
            own = block
    new_codebook, tally = finish(codebook, (own, 0), got)
    return new_codebook, tally, lognorm[0]


def solution(mesh):
    n_dp, n_cent = mesh.shape["dp"], mesh.shape["cent"]
    body = local_split if (n_dp, n_cent) == (4, 8) else local

    def run(embeddings, codebook):
        return body(n_dp, n_cent, embeddings, codebook)

    return jax.shard_map(
        run,
        mesh=mesh,
        in_specs=(P(("dp", "cent"), None), P(("cent", "dp"), None)),
        out_specs=(P(("cent", "dp"), None), P(("cent", "dp")), P(("dp", "cent"))),
        check_vma=False,
    )
```

```python
import functools

import jax
import jax.numpy as jnp
from jax import lax
from jax.experimental import pallas as pl
from jax.experimental.pallas import tpu as pltpu
from jax.sharding import PartitionSpec as P

TEMPER = 0.8
PRIOR = 1.0
SIDE = 8
VMEM = pl.BlockSpec(memory_space=pltpu.VMEM)
PARAMS = pltpu.CompilerParams(vmem_limit_bytes=24 << 20)


def partner(size, mask):
    return [(i, i ^ mask) for i in range(size)]


def swap(x, axis, size, mask):
    return lax.ppermute(x, axis, partner(size, mask))


def merge(a, b):
    top = jnp.maximum(a[0], b[0])
    return top, a[1] * jnp.exp(a[0] - top) + b[1] * jnp.exp(b[0] - top)


def score_kernel(n_cent, n_rows, picks, begin, starts, *refs):
    cent_refs, row_refs = refs[:n_cent], refs[n_cent : n_cent + n_rows]
    early_refs = refs[n_cent + n_rows : -2]
    score_ref, pair_ref = refs[-2:]
    r = score_ref.shape[2]
    centers = jnp.concatenate([ref[...] for ref in cent_refs], axis=0)
    half = 0.5 * jnp.sum(jnp.square(centers.astype(jnp.float32)), axis=1, keepdims=True)
    for j, (i, at) in enumerate(picks):
        product = lax.dot_general(
            centers,
            row_refs[i][at : at + r],
            (((1,), (1,)), ((), ())),
            preferred_element_type=jnp.float32,
        )
        s = (product - half) * (1.0 / TEMPER)
        top = jnp.max(s, axis=0, keepdims=True)
        score_ref[j] = s
        total = jnp.sum(jnp.exp(s - top), axis=0, keepdims=True)
        at = begin + j
        for ref, start in zip(early_refs, starts):
            if start <= at < start + ref.shape[1]:
                k = slice(at - start, at - start + 1)
                top, total = merge((top, total), (ref[0, k], ref[1, k]))
        pair_ref[0, at : at + 1] = top
        pair_ref[1, at : at + 1] = total
    for ref, start in zip(early_refs, starts):
        for k in range(ref.shape[1]):
            if not begin <= start + k < begin + len(picks):
                pair_ref[:, start + k : start + k + 1] = ref[:, k : k + 1]


def score(centers, rows, r, picks, early=(), begin=0):
    n_c, n_r = len(centers), len(picks)
    depth = rows[0].shape[1]
    c = sum(x.shape[0] for x in centers)
    starts = [sum(e.shape[1] for e in early[:i]) for i in range(len(early))]
    n_out = max(begin + n_r, sum(e.shape[1] for e in early))
    return pl.pallas_call(
        functools.partial(score_kernel, n_c, len(rows), picks, begin, starts),
        out_shape=(
            jax.ShapeDtypeStruct((n_r, c, r), jnp.float32),
            jax.ShapeDtypeStruct((2, n_out, r), jnp.float32),
        ),
        in_specs=[VMEM] * (n_c + len(rows) + len(early)),
        out_specs=(VMEM,) * 2,
        compiler_params=PARAMS,
        cost_estimate=pl.CostEstimate(
            flops=2 * n_r * c * r * depth,
            bytes_accessed=2 * (n_r * r + c) * depth,
            transcendentals=n_r * c * r,
        ),
        name="score_rows",
    )(*centers, *rows, *early)


def join_kernel(places, last, pair_ref, *refs):
    out_ref = refs[-1]
    top, total = pair_ref[0], pair_ref[1]
    for ref, where in zip(refs[:-1], places):
        other = [jnp.concatenate([ref[i, p : p + 1] for p in where]) for i in range(2)]
        top, total = merge((top, total), other)
    if last:
        out_ref[...] = top + jnp.log(total)
    else:
        out_ref[0] = top
        out_ref[1] = total


def join(pairs, routes, places, last):
    others = [lax.ppermute(pairs, "cent", route) for route in routes]
    return pl.pallas_call(
        functools.partial(join_kernel, places, last),
        out_shape=jax.ShapeDtypeStruct(pairs.shape[1:] if last else pairs.shape, jnp.float32),
        in_specs=[VMEM] * (1 + len(others)),
        out_specs=VMEM,
        compiler_params=PARAMS,
        name="join_rows",
    )(pairs, *others)


def sums_kernel(n_parts, picks, parts, lognorm_ref, *refs):
    score_refs, row_refs = refs[:n_parts], refs[n_parts : -len(parts)]
    outs = refs[-len(parts) :]
    r = lognorm_ref.shape[1]
    ones = jnp.ones((SIDE, r), jnp.bfloat16)
    for out, (places, size, unit) in zip(outs, parts):
        total, tally = None, None
        for j, (i, at) in enumerate(picks):
            k, block, first = places[j]
            s = score_refs[k][block, first : first + size, :]
            resp = jnp.exp(s - lognorm_ref[j : j + 1]).astype(jnp.bfloat16)
            more = jnp.dot(resp, row_refs[i][at : at + r], preferred_element_type=jnp.float32)
            count = lax.dot_general(
                ones, resp, (((1,), (1,)), ((), ())), preferred_element_type=jnp.float32
            )
            total = more if total is None else total + more
            tally = count if tally is None else tally + count
        wide = jnp.concatenate(
            [tally, jnp.zeros((SIDE, total.shape[1] - size), jnp.float32)], axis=1
        )
        if unit:
            total, wide = pack(total, wide[0:1], unit)
        out[0:size] = total
        out[size : size + SIDE] = wide


def pack(total, tally, unit):
    peak = jnp.max(jnp.abs(total), axis=0, keepdims=True)
    power = jnp.clip(jnp.ceil(jnp.log2(peak)), -100.0, 100.0)
    high = jnp.floor(tally * unit)
    rest = (tally * unit - high) * 1024.0
    middle = jnp.floor(rest)
    low = (rest - middle) * 1024.0
    blank = jnp.zeros((SIDE - 4, total.shape[1]), jnp.float32)
    return total * jnp.exp2(14.0 - power), jnp.concatenate([power, high, middle, low, blank])


def unpack(values, unit):
    size = values.shape[0] - SIDE
    power, high, middle, low = (values[size + i : size + i + 1] for i in range(4))
    tally = (high + (middle + low * (1.0 / 1024.0)) * (1.0 / 1024.0)) * (1.0 / unit)
    return values[:size] * jnp.exp2(power - 14.0), tally


def relay_kernel(unit, own_ref, got_ref, out_ref):
    size = own_ref.shape[0] - SIDE
    more, count = unpack(got_ref[...], unit)
    total, wide = pack(own_ref[0:size] + more, own_ref[size : size + 1] + count, unit * 0.5)
    out_ref[0:size] = total
    out_ref[size : size + SIDE] = wide


def relay(own, got, unit):
    return pl.pallas_call(
        functools.partial(relay_kernel, unit),
        out_shape=jax.ShapeDtypeStruct(own.shape, jnp.float32),
        in_specs=[VMEM] * 2,
        out_specs=VMEM,
        compiler_params=PARAMS,
        name="relay_sums",
    )(own, got)


def final_kernel(units, *refs):
    own_ref, got_refs, codebook_ref, new_ref, tally_ref = refs[0], refs[1:-3], *refs[-3:]
    size, depth = codebook_ref.shape
    total, tally = own_ref[0:size], own_ref[size : size + 1]
    for ref, unit in zip(got_refs, units):
        more, count = unpack(ref[...], unit)
        total, tally = total + more, tally + count
    tally = tally[:, :size]
    tally_ref[...] = tally
    column = jnp.transpose(jnp.broadcast_to(tally, (size, size)))[:, 0:1]
    new_ref[...] = (total + PRIOR * codebook_ref[...]) / (column + PRIOR)


def finish(codebook, own, got):
    size = codebook.shape[0]
    arrays = [own] + [message.astype(jnp.float32) for message, _ in got] + [codebook]
    new, tally = pl.pallas_call(
        functools.partial(final_kernel, [unit for _, unit in got]),
        out_shape=(
            jax.ShapeDtypeStruct(codebook.shape, jnp.float32),
            jax.ShapeDtypeStruct((1, size), jnp.float32),
        ),
        in_specs=[VMEM] * len(arrays),
        out_specs=(VMEM, VMEM),
        compiler_params=PARAMS,
        name="update_centroids",
    )(*arrays)
    return new, tally[0]


def weighted(parts, lognorm, scores, rows, picks):
    size = parts[0][1]
    depth = rows[0].shape[1]
    n_r, r = lognorm.shape
    return pl.pallas_call(
        functools.partial(sums_kernel, len(scores), picks, parts),
        out_shape=[jax.ShapeDtypeStruct((size + SIDE, depth), jnp.float32) for _ in parts],
        in_specs=[VMEM] * (1 + len(scores) + len(rows)),
        out_specs=[VMEM] * len(parts),
        compiler_params=PARAMS,
        cost_estimate=pl.CostEstimate(
            flops=2 * len(parts) * n_r * size * r * depth,
            bytes_accessed=2 * n_r * r * depth,
            transcendentals=len(parts) * n_r * size * r,
        ),
        name="weighted_sums",
    )(lognorm, *scores, *rows)


def local(n_dp, n_cent, embeddings, codebook):
    own_rows = embeddings.shape[0]
    size = codebook.shape[0]
    unit = 1024.0 / (own_rows * n_cent)
    rounded = codebook.astype(jnp.bfloat16)
    if n_cent == 8:
        by_p = [(i, i ^ (4 if i & 1 else 2)) for i in range(n_cent)]
        by_q = [(i, i ^ (2 if i & 1 else 4)) for i in range(n_cent)]
        from_p = lax.ppermute(embeddings, "cent", by_p)
        from_q = lax.ppermute(embeddings, "cent", by_q)
    if n_dp == 4:
        far = swap(rounded, "dp", n_dp, 2)
        near = swap(rounded, "dp", n_dp, 1)
        most, final = [rounded, near, far], [swap(far, "dp", n_dp, 1)]
    else:
        most = [rounded] + [swap(rounded, "dp", n_dp, m) for m in range(1, n_dp - 1)]
        final = [swap(rounded, "dp", n_dp, n_dp - 1)]
    end = (n_dp - 1) * size
    if n_cent == 8:
        diag = lax.ppermute(from_p, "cent", by_q)
        three = jnp.concatenate([embeddings, from_p, from_q], axis=0)
        give, most = lax.optimization_barrier((three, most))
        three_core = swap(give, "cent", n_cent, 1)
        s_0, pair_0 = score(most, [three], own_rows, [(0, j * own_rows) for j in range(3)])
        s_1, pair_1 = score(most, [three_core], own_rows, [(0, j * own_rows) for j in range(3)])
        give, pair_0, pair_1, final = lax.optimization_barrier(
            (diag, pair_0, pair_1, final)
        )
        rows = [three, three_core, diag, swap(give, "cent", n_cent, 1)]
        order = [0, 2, 4, 1, 5, 3, 6, 7]
        picks = [(i, j * own_rows) for i in range(2) for j in range(3)] + [(2, 0), (3, 0)]
        s_2, pairs = score(final, rows[:2], own_rows, picks[:6], [pair_0, pair_1])
        s_3, pair_3 = score(most + final, rows[2:3], own_rows, [(0, 0)])
        s_4, pairs = score(most + final, rows[3:], own_rows, [(0, 0)], [pairs, pair_3], 7)
        scores = [s_0, s_1, s_3, s_4]
        places = [(i, j) for i in range(2) for j in range(3)] + [(2, 0), (3, 0)]
        last_scores = [s_2, s_3, s_4]
        last_places = [(0, j, 0) for j in range(6)] + [(1, 0, end), (2, 0, end)]
    else:
        rows = [embeddings] + [swap(embeddings, "cent", n_cent, m) for m in range(1, n_cent)]
        order = list(range(n_cent))
        picks = [(j, 0) for j in order]
        s_0, pair_0 = score(most, rows, own_rows, picks)
        scores = [s_0]
        places = [(0, j) for j in order]
        s_1, pairs = score(final, rows, own_rows, picks, [pair_0])
        last_scores, last_places = [s_1], [(0, j, 0) for j in order]
    if n_cent == 8:
        where = [order.index((j ^ 1) & 1 | (j & 2) << 1 | (j & 4) >> 1) for j in order]
        pairs = join(pairs, [partner(n_cent, 1)], [where], False)
        routes = [by_p, by_q, partner(n_cent, 6)]
        where = [[order.index(j ^ mask) for j in order] for mask in (2, 4, 6)]
        lognorm = join(pairs, routes, where, True)
    else:
        for bit in range(n_cent.bit_length() - 1):
            where = [j ^ (1 << bit) for j in order]
            pairs = join(pairs, [partner(n_cent, 1 << bit)], [where], 2 << bit >= n_cent)
        lognorm = pairs

    def part(k, unit):
        return [(i, j, k * size) for i, j in places], size, unit

    (first,) = weighted([(last_places, size, unit)], lognorm, last_scores, rows, picks)
    first = first.astype(jnp.float16)
    if n_dp == 4:
        first = swap(first, "dp", n_dp, 1)
        parts = [part(2, 0), part(1, unit), part(0, 0)]
        far_out, near_out, own = weighted(parts, lognorm, scores, rows, picks)
        far_out = relay(far_out, first.astype(jnp.float32), unit).astype(jnp.float16)
        far_out, near_out = lax.optimization_barrier((far_out, near_out))
        far_out = swap(far_out, "dp", n_dp, 2)
        near_out = swap(near_out.astype(jnp.float16), "dp", n_dp, 1)
        got = [(near_out, unit), (far_out, unit * 0.5)]
    else:
        parts = [part(k, unit if k else 0) for k in range(n_dp - 1)]
        out = weighted(parts, lognorm, scores, rows, picks)
        own = out[0]
        sent = [o.astype(jnp.float16) for o in out[1:]] + [first]
        got = [(swap(m, "dp", n_dp, k + 1), unit) for k, m in enumerate(sent)]
    new_codebook, tally = finish(codebook, own, got)
    return new_codebook, tally, lognorm[0]


def solution(mesh):
    n_dp, n_cent = mesh.shape["dp"], mesh.shape["cent"]

    def run(embeddings, codebook):
        return local(n_dp, n_cent, embeddings, codebook)

    return jax.shard_map(
        run,
        mesh=mesh,
        in_specs=(P(("dp", "cent"), None), P(("cent", "dp"), None)),
        out_specs=(P(("cent", "dp"), None), P(("cent", "dp")), P(("dp", "cent"))),
        check_vma=False,
    )
```

```python
import functools

import jax
import jax.numpy as jnp
from jax import lax
from jax.experimental import pallas as pl
from jax.experimental.pallas import tpu as pltpu
from jax.sharding import PartitionSpec as P

TEMPER = 0.8
PRIOR = 1.0
SIDE = 8
VMEM = pl.BlockSpec(memory_space=pltpu.VMEM)
PARAMS = pltpu.CompilerParams(vmem_limit_bytes=24 << 20)


def partner(size, mask):
    return [(i, i ^ mask) for i in range(size)]


def swap(x, axis, size, mask):
    return lax.ppermute(x, axis, partner(size, mask))


def merge(a, b):
    top = jnp.maximum(a[0], b[0])
    return top, a[1] * jnp.exp(a[0] - top) + b[1] * jnp.exp(b[0] - top)


def score_kernel(n_cent, n_rows, picks, begin, starts, *refs):
    cent_refs, row_refs = refs[:n_cent], refs[n_cent : n_cent + n_rows]
    early_refs = refs[n_cent + n_rows : -2]
    score_ref, pair_ref = refs[-2:]
    r = score_ref.shape[2]
    centers = jnp.concatenate([ref[...] for ref in cent_refs], axis=0)
    half = 0.5 * jnp.sum(jnp.square(centers.astype(jnp.float32)), axis=1, keepdims=True)
    for j, (i, at) in enumerate(picks):
        product = lax.dot_general(
            centers,
            row_refs[i][at : at + r],
            (((1,), (1,)), ((), ())),
            preferred_element_type=jnp.float32,
        )
        s = (product - half) * (1.0 / TEMPER)
        top = jnp.max(s, axis=0, keepdims=True)
        score_ref[j] = s
        total = jnp.sum(jnp.exp(s - top), axis=0, keepdims=True)
        at = begin + j
        for ref, start in zip(early_refs, starts):
            if start <= at < start + ref.shape[1]:
                k = slice(at - start, at - start + 1)
                top, total = merge((top, total), (ref[0, k], ref[1, k]))
        pair_ref[0, at : at + 1] = top
        pair_ref[1, at : at + 1] = total
    for ref, start in zip(early_refs, starts):
        for k in range(ref.shape[1]):
            if not begin <= start + k < begin + len(picks):
                pair_ref[:, start + k : start + k + 1] = ref[:, k : k + 1]


def score(centers, rows, r, picks, early=(), begin=0):
    n_c, n_r = len(centers), len(picks)
    depth = rows[0].shape[1]
    c = sum(x.shape[0] for x in centers)
    starts = [sum(e.shape[1] for e in early[:i]) for i in range(len(early))]
    n_out = max(begin + n_r, sum(e.shape[1] for e in early))
    return pl.pallas_call(
        functools.partial(score_kernel, n_c, len(rows), picks, begin, starts),
        out_shape=(
            jax.ShapeDtypeStruct((n_r, c, r), jnp.float32),
            jax.ShapeDtypeStruct((2, n_out, r), jnp.float32),
        ),
        in_specs=[VMEM] * (n_c + len(rows) + len(early)),
        out_specs=(VMEM,) * 2,
        compiler_params=PARAMS,
        cost_estimate=pl.CostEstimate(
            flops=2 * n_r * c * r * depth,
            bytes_accessed=2 * (n_r * r + c) * depth,
            transcendentals=n_r * c * r,
        ),
        name="score_rows",
    )(*centers, *rows, *early)


def join_kernel(places, last, pair_ref, *refs):
    others, outs = refs[: len(places)], refs[len(places) :]
    top, total = pair_ref[0], pair_ref[1]
    for ref, where in zip(others, places):
        other = [jnp.concatenate([ref[i, p : p + 1] for p in where]) for i in range(2)]
        top, total = merge((top, total), other)
    if last:
        outs[0][...] = top + jnp.log(total)
    for ref in outs[1:] if last else outs:
        for i in range(0, ref.shape[0], 2):
            ref[i] = top
            ref[i + 1] = total


def join(pairs, sent, routes, places, last, copies=()):
    others = [lax.ppermute(x, "cent", route) for x, route in zip(sent, routes)]
    n, r = pairs.shape[1:]
    shapes = [(n, r) if last else (2, n, r)] + [(2 * c, n, r) for c in copies]
    return pl.pallas_call(
        functools.partial(join_kernel, places, last),
        out_shape=[jax.ShapeDtypeStruct(shape, jnp.float32) for shape in shapes],
        in_specs=[VMEM] * (1 + len(others)),
        out_specs=[VMEM] * len(shapes),
        compiler_params=PARAMS,
        name="join_rows",
    )(pairs, *others)


def sums_kernel(n_parts, picks, parts, lognorm_ref, *refs):
    n_out = 2 * len(parts)
    score_refs, row_refs, outs = refs[:n_parts], refs[n_parts:-n_out], refs[-n_out:]
    r = lognorm_ref.shape[1]
    ones = jnp.ones((SIDE, r), jnp.bfloat16)
    for n, (places, size, packed) in enumerate(parts):
        total, tally = None, None
        for j, (i, at) in enumerate(picks):
            k, block, first = places[j]
            s = score_refs[k][block, first : first + size, :]
            resp = jnp.exp(s - lognorm_ref[j : j + 1]).astype(jnp.bfloat16)
            more = jnp.dot(resp, row_refs[i][at : at + r], preferred_element_type=jnp.float32)
            count = lax.dot_general(
                ones, resp, (((1,), (1,)), ((), ())), preferred_element_type=jnp.float32
            )
            total = more if total is None else total + more
            tally = count if tally is None else tally + count
        blank = jnp.zeros((1, total.shape[1] - size), jnp.float32)
        tally = jnp.concatenate([tally[0:1], blank], axis=1)
        write(outs[2 * n], outs[2 * n + 1], total, tally, packed)


def write(body_ref, side_ref, total, tally, packed):
    power = jnp.zeros_like(tally)
    if packed:
        peak = jnp.max(jnp.abs(total), axis=0, keepdims=True)
        power = jnp.clip(jnp.ceil(jnp.log2(peak)), -100.0, 100.0)
        total = total * jnp.exp2(14.0 - power)
    body_ref[...] = total
    blank = jnp.zeros((SIDE - 2, tally.shape[1]), jnp.float32)
    side_ref[...] = jnp.concatenate([power, tally, blank])


def gather_parts(own, refs):
    total, tally = own[0][...], own[1][1:2]
    for body, side in zip(refs[0::2], refs[1::2]):
        total = total + body[...] * jnp.exp2(side[0:1] - 14.0)
        tally = tally + side[1:2]
    return total, tally


def send(part, mask, size):
    body, side = part
    return swap(body.astype(jnp.float16), "dp", size, mask), swap(side, "dp", size, mask)


def widen(messages):
    return [x for body, side in messages for x in (body.astype(jnp.float32), side)]


def relay_kernel(*refs):
    total, tally = gather_parts(refs[:2], refs[2:-2])
    write(refs[-2], refs[-1], total, tally, True)


def relay(own, got):
    return pl.pallas_call(
        relay_kernel,
        out_shape=[jax.ShapeDtypeStruct(x.shape, jnp.float32) for x in own],
        in_specs=[VMEM] * (2 + 2 * len(got)),
        out_specs=[VMEM] * 2,
        compiler_params=PARAMS,
        name="relay_sums",
    )(*own, *widen(got))


def final_kernel(*refs):
    codebook_ref, new_ref, tally_ref, buffer, sems = refs[-5:]
    size = codebook_ref.shape[0]
    total, tally = gather_parts(refs[:2], refs[2:-5])
    tally = tally[:, :size]
    tally_ref[...] = tally
    weight = jnp.transpose(jnp.broadcast_to(tally, (size, size)))[:, 0:1] + PRIOR
    step = size // sems.shape[0]
    copies = []
    for i in range(sems.shape[0]):
        at = slice(i * step, (i + 1) * step)
        buffer[at] = (total[at] + PRIOR * codebook_ref[at]) / weight[at]
        copy = pltpu.make_async_copy(buffer.at[at], new_ref.at[at], sems.at[i])
        copy.start()
        copies.append(copy)
    for copy in copies:
        copy.wait()


def finish(codebook, own, got):
    size = codebook.shape[0]
    new, tally = pl.pallas_call(
        final_kernel,
        out_shape=(
            jax.ShapeDtypeStruct(codebook.shape, jnp.float32),
            jax.ShapeDtypeStruct((1, size), jnp.float32),
        ),
        in_specs=[VMEM] * (3 + 2 * len(got)),
        out_specs=(pl.BlockSpec(memory_space=pl.ANY), VMEM),
        scratch_shapes=[
            pltpu.VMEM(codebook.shape, jnp.float32),
            pltpu.SemaphoreType.DMA((4,)),
        ],
        compiler_params=PARAMS,
        name="update_centroids",
    )(*own, *widen(got), codebook)
    return new, tally[0]


def weighted(parts, lognorm, scores, rows, picks):
    size = parts[0][1]
    depth = rows[0].shape[1]
    n_r, r = lognorm.shape
    out = pl.pallas_call(
        functools.partial(sums_kernel, len(scores), picks, parts),
        out_shape=[
            jax.ShapeDtypeStruct((n, depth), jnp.float32) for _ in parts for n in (size, SIDE)
        ],
        in_specs=[VMEM] * (1 + len(scores) + len(rows)),
        out_specs=[VMEM] * (2 * len(parts)),
        compiler_params=PARAMS,
        cost_estimate=pl.CostEstimate(
            flops=2 * len(parts) * n_r * size * r * depth,
            bytes_accessed=2 * n_r * r * depth,
            transcendentals=len(parts) * n_r * size * r,
        ),
        name="weighted_sums",
    )(lognorm, *scores, *rows)
    return list(zip(out[0::2], out[1::2]))


def local(n_dp, n_cent, embeddings, codebook):
    own_rows = embeddings.shape[0]
    size = codebook.shape[0]
    rounded = codebook.astype(jnp.bfloat16)
    if n_cent == 8:
        by_p = [(i, i ^ (4 if i & 1 else 2)) for i in range(n_cent)]
        by_q = [(i, i ^ (2 if i & 1 else 4)) for i in range(n_cent)]
        from_p = lax.ppermute(embeddings, "cent", by_p)
        from_q = lax.ppermute(embeddings, "cent", by_q)
    if n_dp == 4:
        far = swap(rounded, "dp", n_dp, 2)
        near = swap(rounded, "dp", n_dp, 1)
        most, final = [rounded, near, far], [swap(far, "dp", n_dp, 1)]
    else:
        most = [rounded] + [swap(rounded, "dp", n_dp, m) for m in range(1, n_dp - 1)]
        final = [swap(rounded, "dp", n_dp, n_dp - 1)]
    end = (n_dp - 1) * size
    if n_cent == 8:
        diag = lax.ppermute(from_p, "cent", by_q)
        three = jnp.concatenate([embeddings, from_p, from_q], axis=0)
        give, most = lax.optimization_barrier((three, most))
        three_core = swap(give, "cent", n_cent, 1)
        s_0, pair_0 = score(most, [three], own_rows, [(0, j * own_rows) for j in range(3)])
        s_1, pair_1 = score(most, [three_core], own_rows, [(0, j * own_rows) for j in range(3)])
        give, pair_0, pair_1, final = lax.optimization_barrier(
            (diag, pair_0, pair_1, final)
        )
        rows = [three, three_core, diag, swap(give, "cent", n_cent, 1)]
        order = [0, 2, 4, 1, 5, 3, 6, 7]
        picks = [(i, j * own_rows) for i in range(2) for j in range(3)] + [(2, 0), (3, 0)]
        s_2, pairs = score(final, rows[:2], own_rows, picks[:6], [pair_0, pair_1])
        s_3, pair_3 = score(most + final, rows[2:3], own_rows, [(0, 0)])
        s_4, pairs = score(most + final, rows[3:], own_rows, [(0, 0)], [pairs, pair_3], 7)
        scores = [s_0, s_1, s_3, s_4]
        places = [(i, j) for i in range(2) for j in range(3)] + [(2, 0), (3, 0)]
        last_scores = [s_2, s_3, s_4]
        last_places = [(0, j, 0) for j in range(6)] + [(1, 0, end), (2, 0, end)]
    else:
        rows = [embeddings] + [swap(embeddings, "cent", n_cent, m) for m in range(1, n_cent)]
        order = list(range(n_cent))
        picks = [(j, 0) for j in order]
        s_0, pair_0 = score(most, rows, own_rows, picks)
        scores = [s_0]
        places = [(0, j) for j in order]
        s_1, pairs = score(final, rows, own_rows, picks, [pair_0])
        last_scores, last_places = [s_1], [(0, j, 0) for j in order]
    if n_cent == 8:
        where = [order.index((j ^ 1) & 1 | (j & 2) << 1 | (j & 4) >> 1) for j in order]
        pairs, twice = join(pairs, [pairs], [partner(n_cent, 1)], [where], False, (2,))
        routes = [partner(n_cent, 6), by_p, by_q]
        where = [[order.index(j ^ mask) for j in order] for mask in (6, 2, 4)]
        (lognorm,) = join(pairs, [twice, pairs, pairs], routes, where, True)
    else:
        for bit in range(n_cent.bit_length() - 1):
            where = [j ^ (1 << bit) for j in order]
            route = partner(n_cent, 1 << bit)
            (pairs,) = join(pairs, [pairs], [route], [where], 2 << bit >= n_cent)
        lognorm = pairs

    def part(k, packed):
        return [(i, j, k * size) for i, j in places], size, packed

    (first,) = weighted([(last_places, size, True)], lognorm, last_scores, rows, picks)
    if n_dp == 4:
        first = send(first, 1, n_dp)
        parts = [part(2, False), part(1, True), part(0, False)]
        far_sum, near_sum, own = weighted(parts, lognorm, scores, rows, picks)
        far_sum = relay(far_sum, [first])
        far_sum, near_sum = lax.optimization_barrier((far_sum, near_sum))
        got = [send(near_sum, 1, n_dp), send(far_sum, 2, n_dp)]
    else:
        parts = [part(k, k > 0) for k in range(n_dp - 1)]
        own, *others = weighted(parts, lognorm, scores, rows, picks)
        got = [send(other, k + 1, n_dp) for k, other in enumerate(others + [first])]
    new_codebook, tally = finish(codebook, own, got)
    return new_codebook, tally, lognorm[0]


def solution(mesh):
    n_dp, n_cent = mesh.shape["dp"], mesh.shape["cent"]

    def run(embeddings, codebook):
        return local(n_dp, n_cent, embeddings, codebook)

    return jax.shard_map(
        run,
        mesh=mesh,
        in_specs=(P(("dp", "cent"), None), P(("cent", "dp"), None)),
        out_specs=(P(("cent", "dp"), None), P(("cent", "dp")), P(("dp", "cent"))),
        check_vma=False,
    )
```

```python
import functools

import jax
import jax.numpy as jnp
from jax import lax
from jax.experimental import pallas as pl
from jax.experimental.pallas import tpu as pltpu
from jax.sharding import PartitionSpec as P

TEMPER = 0.8
PRIOR = 1.0
SIDE = 8
VMEM = pl.BlockSpec(memory_space=pltpu.VMEM)
PARAMS = pltpu.CompilerParams(vmem_limit_bytes=24 << 20)


def partner(size, mask):
    return [(i, i ^ mask) for i in range(size)]


def swap(x, axis, size, mask):
    return lax.ppermute(x, axis, partner(size, mask))


def merge(a, b):
    top = jnp.maximum(a[0], b[0])
    return top, a[1] * jnp.exp(a[0] - top) + b[1] * jnp.exp(b[0] - top)


def score_kernel(n_cent, n_half, n_rows, picks, begin, starts, r, *refs):
    cent_refs, refs = refs[:n_cent], refs[n_cent:]
    half_refs, refs = refs[:n_half], refs[n_half:]
    row_refs, early_refs = refs[:n_rows], refs[n_rows:-3]
    score_ref, pair_ref, half_ref = refs[-3:]
    halves = [ref[...] for ref in half_refs]
    for ref in cent_refs[n_half:]:
        squares = jnp.square(ref[...].astype(jnp.float32))
        half = 0.5 * jnp.sum(squares, axis=1, keepdims=True)
        halves.append(jnp.broadcast_to(half, (half.shape[0], half_ref.shape[1])))
    half_ref[...] = halves[-1]
    repeat = r // half_ref.shape[1]
    halves = [jnp.concatenate([half] * repeat, axis=1) for half in halves]
    for j, (i, at) in enumerate(picks):
        parts, first = [], 0
        for ref, half in zip(cent_refs, halves):
            product = lax.dot_general(
                ref[...],
                row_refs[i][at : at + r],
                (((1,), (1,)), ((), ())),
                preferred_element_type=jnp.float32,
            )
            s = (product - half) * (1.0 / TEMPER)
            score_ref[j, first : first + s.shape[0]] = s
            first += s.shape[0]
            parts.append(s)
        top = functools.reduce(jnp.maximum, [jnp.max(s, axis=0, keepdims=True) for s in parts])
        total = sum(jnp.sum(jnp.exp(s - top), axis=0, keepdims=True) for s in parts)
        at = begin + j
        for ref, start in zip(early_refs, starts):
            if start <= at < start + ref.shape[1]:
                k = slice(at - start, at - start + 1)
                top, total = merge((top, total), (ref[0, k], ref[1, k]))
        pair_ref[0, at : at + 1] = top
        pair_ref[1, at : at + 1] = total
    for ref, start in zip(early_refs, starts):
        for k in range(ref.shape[1]):
            if not begin <= start + k < begin + len(picks):
                pair_ref[:, start + k : start + k + 1] = ref[:, k : k + 1]


def score(centers, halves, rows, r, picks, early=(), begin=0):
    n_r = len(picks)
    depth = rows[0].shape[1]
    c = sum(x.shape[0] for x in centers)
    lanes = min(r, 128)
    starts = [sum(e.shape[1] for e in early[:i]) for i in range(len(early))]
    n_out = max(begin + n_r, sum(e.shape[1] for e in early))
    operands = [*centers, *halves, *rows, *early]
    return pl.pallas_call(
        functools.partial(
            score_kernel, len(centers), len(halves), len(rows), picks, begin, starts, r
        ),
        out_shape=(
            jax.ShapeDtypeStruct((n_r, c, r), jnp.float32),
            jax.ShapeDtypeStruct((2, n_out, r), jnp.float32),
            jax.ShapeDtypeStruct((centers[-1].shape[0], lanes), jnp.float32),
        ),
        in_specs=[VMEM] * len(operands),
        out_specs=(VMEM,) * 3,
        compiler_params=PARAMS,
        cost_estimate=pl.CostEstimate(
            flops=2 * n_r * c * r * depth,
            bytes_accessed=2 * (n_r * r + c) * depth,
            transcendentals=n_r * c * r,
        ),
        name="score_rows",
    )(*operands)


def join_kernel(places, last, pair_ref, *refs):
    out_ref = refs[-1]
    top, total = pair_ref[0], pair_ref[1]
    for ref, where in zip(refs[:-1], places):
        other = [jnp.concatenate([ref[i, p : p + 1] for p in where]) for i in range(2)]
        top, total = merge((top, total), other)
    if last:
        out_ref[...] = top + jnp.log(total)
    else:
        out_ref[0] = top
        out_ref[1] = total


def join(pairs, routes, places, last):
    others = [lax.ppermute(pairs, "cent", route) for route in routes]
    return pl.pallas_call(
        functools.partial(join_kernel, places, last),
        out_shape=jax.ShapeDtypeStruct(pairs.shape[1:] if last else pairs.shape, jnp.float32),
        in_specs=[VMEM] * (1 + len(others)),
        out_specs=VMEM,
        compiler_params=PARAMS,
        name="join_rows",
    )(pairs, *others)


def sums_kernel(n_parts, picks, parts, lognorm_ref, *refs):
    score_refs, row_refs = refs[:n_parts], refs[n_parts : -len(parts)]
    outs = refs[-len(parts) :]
    ones = jnp.ones((SIDE, max(ref.shape[0] for ref in row_refs)), jnp.bfloat16)
    for out, (places, size, unit) in zip(outs, parts):
        total, tally = None, None
        for i, ref in enumerate(row_refs):
            mine = [j for j, pick in enumerate(picks) if pick[0] == i]
            resp = []
            for j in mine:
                k, block, first = places[j]
                s = score_refs[k][block, first : first + size, :]
                resp.append(jnp.exp(s - lognorm_ref[j : j + 1]).astype(jnp.bfloat16))
            resp = jnp.concatenate(resp, axis=1)
            more = jnp.dot(resp, ref[...], preferred_element_type=jnp.float32)
            count = lax.dot_general(
                ones[:, : ref.shape[0]],
                resp,
                (((1,), (1,)), ((), ())),
                preferred_element_type=jnp.float32,
            )
            total = more if total is None else total + more
            tally = count if tally is None else tally + count
        wide = jnp.concatenate(
            [tally, jnp.zeros((SIDE, total.shape[1] - size), jnp.float32)], axis=1
        )
        if unit:
            total, wide = pack(total, wide[0:1], unit)
        out[0:size] = total
        out[size : size + SIDE] = wide


def pack(total, tally, unit):
    peak = jnp.max(jnp.abs(total), axis=0, keepdims=True)
    power = jnp.clip(jnp.ceil(jnp.log2(peak)), -100.0, 100.0)
    high = jnp.floor(tally * unit)
    rest = (tally * unit - high) * 1024.0
    middle = jnp.floor(rest)
    low = (rest - middle) * 1024.0
    blank = jnp.zeros((SIDE - 4, total.shape[1]), jnp.float32)
    return total * jnp.exp2(14.0 - power), jnp.concatenate([power, high, middle, low, blank])


def unpack(values, unit):
    size = values.shape[0] - SIDE
    power, high, middle, low = (values[size + i : size + i + 1] for i in range(4))
    tally = (high + (middle + low * (1.0 / 1024.0)) * (1.0 / 1024.0)) * (1.0 / unit)
    return values[:size] * jnp.exp2(power - 14.0), tally


def relay_kernel(unit, own_ref, got_ref, out_ref):
    size = own_ref.shape[0] - SIDE
    more, count = unpack(got_ref[...], unit)
    total, wide = pack(own_ref[0:size] + more, own_ref[size : size + 1] + count, unit * 0.5)
    out_ref[0:size] = total
    out_ref[size : size + SIDE] = wide


def relay(own, got, unit):
    return pl.pallas_call(
        functools.partial(relay_kernel, unit),
        out_shape=jax.ShapeDtypeStruct(own.shape, jnp.float32),
        in_specs=[VMEM] * 2,
        out_specs=VMEM,
        compiler_params=PARAMS,
        name="relay_sums",
    )(own, got)


def final_kernel(units, *refs):
    own_ref, got_refs, codebook_ref, new_ref, tally_ref = refs[0], refs[1:-3], *refs[-3:]
    size, depth = codebook_ref.shape
    total, tally = own_ref[0:size], own_ref[size : size + 1]
    for ref, unit in zip(got_refs, units):
        more, count = unpack(ref[...], unit)
        total, tally = total + more, tally + count
    tally = tally[:, :size]
    tally_ref[...] = tally
    weight = 1.0 / (jnp.transpose(jnp.broadcast_to(tally, (size, size)))[:, 0:1] + PRIOR)
    new_ref[...] = (total + PRIOR * codebook_ref[...]) * weight


def finish(codebook, own, got):
    size = codebook.shape[0]
    arrays = [own] + [message.astype(jnp.float32) for message, _ in got] + [codebook]
    new, tally = pl.pallas_call(
        functools.partial(final_kernel, [unit for _, unit in got]),
        out_shape=(
            jax.ShapeDtypeStruct(codebook.shape, jnp.float32),
            jax.ShapeDtypeStruct((1, size), jnp.float32),
        ),
        in_specs=[VMEM] * len(arrays),
        out_specs=(VMEM, VMEM),
        compiler_params=PARAMS,
        name="update_centroids",
    )(*arrays)
    return new, tally[0]


def weighted(parts, lognorm, scores, rows, picks):
    size = parts[0][1]
    depth = rows[0].shape[1]
    n_r, r = lognorm.shape
    return pl.pallas_call(
        functools.partial(sums_kernel, len(scores), picks, parts),
        out_shape=[jax.ShapeDtypeStruct((size + SIDE, depth), jnp.float32) for _ in parts],
        in_specs=[VMEM] * (1 + len(scores) + len(rows)),
        out_specs=[VMEM] * len(parts),
        compiler_params=PARAMS,
        cost_estimate=pl.CostEstimate(
            flops=2 * len(parts) * n_r * size * r * depth,
            bytes_accessed=2 * n_r * r * depth,
            transcendentals=len(parts) * n_r * size * r,
        ),
        name="weighted_sums",
    )(lognorm, *scores, *rows)


def local(n_dp, n_cent, embeddings, codebook):
    own_rows = embeddings.shape[0]
    size = codebook.shape[0]
    unit = 1024.0 / (own_rows * n_cent)
    rounded = codebook.astype(jnp.bfloat16)
    if n_cent == 8:
        by_p = [(i, i ^ (4 if i & 1 else 2)) for i in range(n_cent)]
        by_q = [(i, i ^ (2 if i & 1 else 4)) for i in range(n_cent)]
        from_p = lax.ppermute(embeddings, "cent", by_p)
        from_q = lax.ppermute(embeddings, "cent", by_q)
    if n_dp == 4:
        far = swap(rounded, "dp", n_dp, 2)
        near = swap(rounded, "dp", n_dp, 1)
        most, final = [rounded, near, far], [swap(far, "dp", n_dp, 1)]
    else:
        most = [rounded] + [swap(rounded, "dp", n_dp, m) for m in range(1, n_dp - 1)]
        final = [swap(rounded, "dp", n_dp, n_dp - 1)]
    end = (n_dp - 1) * size
    if n_cent == 8:
        diag = lax.ppermute(from_p, "cent", by_q)
        three = jnp.concatenate([embeddings, from_p, from_q], axis=0)
        give, most = lax.optimization_barrier((three, most))
        three_core = swap(give, "cent", n_cent, 1)
        most = [jnp.concatenate(most, axis=0)]
        of_three = [(0, j * own_rows) for j in range(3)]
        s_0, pair_0, half = score(most, [], [three], own_rows, of_three)
        s_1, pair_1, _ = score(most, [half], [three_core], own_rows, of_three)
        give, pair_0, pair_1, final = lax.optimization_barrier(
            (diag, pair_0, pair_1, final)
        )
        rows = [three, three_core, diag, swap(give, "cent", n_cent, 1)]
        order = [0, 2, 4, 1, 5, 3, 6, 7]
        picks = [(i, j * own_rows) for i in range(2) for j in range(3)] + [(2, 0), (3, 0)]
        both = most + final
        s_3, pair_3, last = score(both, [half], rows[2:3], own_rows, [(0, 0)])
        s_2, pairs, _ = score(final, [last], rows[:2], own_rows, picks[:6], [pair_0, pair_1])
        s_4, pairs, _ = score(both, [half, last], rows[3:], own_rows, [(0, 0)], [pairs, pair_3], 7)
        scores = [s_0, s_1, s_3, s_4]
        places = [(i, j) for i in range(2) for j in range(3)] + [(2, 0), (3, 0)]
        last_scores = [s_2, s_3, s_4]
        last_places = [(0, j, 0) for j in range(6)] + [(1, 0, end), (2, 0, end)]
    else:
        rows = [embeddings] + [swap(embeddings, "cent", n_cent, m) for m in range(1, n_cent)]
        order = list(range(n_cent))
        picks = [(j, 0) for j in order]
        s_0, pair_0, _ = score(most, [], rows, own_rows, picks)
        scores = [s_0]
        places = [(0, j) for j in order]
        s_1, pairs, _ = score(final, [], rows, own_rows, picks, [pair_0])
        last_scores, last_places = [s_1], [(0, j, 0) for j in order]
    if n_cent == 8:
        where = [order.index((j ^ 1) & 1 | (j & 2) << 1 | (j & 4) >> 1) for j in order]
        pairs = join(pairs, [partner(n_cent, 1)], [where], False)
        routes = [by_p, by_q, partner(n_cent, 6)]
        where = [[order.index(j ^ mask) for j in order] for mask in (2, 4, 6)]
        lognorm = join(pairs, routes, where, True)
    else:
        for bit in range(n_cent.bit_length() - 1):
            where = [j ^ (1 << bit) for j in order]
            pairs = join(pairs, [partner(n_cent, 1 << bit)], [where], 2 << bit >= n_cent)
        lognorm = pairs

    def part(k, unit):
        return [(i, j, k * size) for i, j in places], size, unit

    (first,) = weighted([(last_places, size, unit)], lognorm, last_scores, rows, picks)
    first = first.astype(jnp.float16)
    if n_dp == 4:
        first = swap(first, "dp", n_dp, 1)
        parts = [part(2, 0), part(1, unit), part(0, 0)]
        far_out, near_out, own = weighted(parts, lognorm, scores, rows, picks)
        far_out = relay(far_out, first.astype(jnp.float32), unit).astype(jnp.float16)
        far_out, near_out = lax.optimization_barrier((far_out, near_out))
        far_out = swap(far_out, "dp", n_dp, 2)
        near_out = swap(near_out.astype(jnp.float16), "dp", n_dp, 1)
        got = [(near_out, unit), (far_out, unit * 0.5)]
    else:
        parts = [part(k, unit if k else 0) for k in range(n_dp - 1)]
        out = weighted(parts, lognorm, scores, rows, picks)
        own = out[0]
        sent = [o.astype(jnp.float16) for o in out[1:]] + [first]
        got = [(swap(m, "dp", n_dp, k + 1), unit) for k, m in enumerate(sent)]
    new_codebook, tally = finish(codebook, own, got)
    return new_codebook, tally, lognorm[0]


def solution(mesh):
    n_dp, n_cent = mesh.shape["dp"], mesh.shape["cent"]

    def run(embeddings, codebook):
        return local(n_dp, n_cent, embeddings, codebook)

    return jax.shard_map(
        run,
        mesh=mesh,
        in_specs=(P(("dp", "cent"), None), P(("cent", "dp"), None)),
        out_specs=(P(("cent", "dp"), None), P(("cent", "dp")), P(("dp", "cent"))),
        check_vma=False,
    )
```

```python
import functools

import jax
import jax.numpy as jnp
from jax import lax
from jax.experimental import pallas as pl
from jax.experimental.pallas import tpu as pltpu
from jax.sharding import PartitionSpec as P

TEMPER = 0.8
PRIOR = 1.0
SIDE = 8
VMEM = pl.BlockSpec(memory_space=pltpu.VMEM)
PARAMS = pltpu.CompilerParams(vmem_limit_bytes=24 << 20)


def partner(size, mask):
    return [(i, i ^ mask) for i in range(size)]


def swap(x, axis, size, mask):
    return lax.ppermute(x, axis, partner(size, mask))


def merge(a, b):
    top = jnp.maximum(a[0], b[0])
    return top, a[1] * jnp.exp(a[0] - top) + b[1] * jnp.exp(b[0] - top)


def score_kernel(n_cent, n_half, n_rows, picks, begin, starts, r, *refs):
    cent_refs, refs = refs[:n_cent], refs[n_cent:]
    half_refs, refs = refs[:n_half], refs[n_half:]
    row_refs, refs = refs[:n_rows], refs[n_rows:]
    early_refs, (score_ref, pair_ref, *half_out) = refs[: len(starts)], refs[len(starts) :]
    lanes = min(r, 128)
    halves = [ref[...] for ref in half_refs]
    for ref in cent_refs[n_half:]:
        squares = jnp.square(ref[...].astype(jnp.float32))
        half = 0.5 * jnp.sum(squares, axis=1, keepdims=True)
        halves.append(jnp.broadcast_to(half, (half.shape[0], lanes)))
    for ref in half_out:
        ref[...] = halves[-1]
    halves = [jnp.concatenate([half] * (r // lanes), axis=1) for half in halves]
    for j, (i, at) in enumerate(picks):
        parts, first = [], 0
        for ref, half in zip(cent_refs, halves):
            product = lax.dot_general(
                ref[...],
                row_refs[i][at : at + r],
                (((1,), (1,)), ((), ())),
                preferred_element_type=jnp.float32,
            )
            s = (product - half) * (1.0 / TEMPER)
            score_ref[j, first : first + s.shape[0]] = s
            first += s.shape[0]
            parts.append(s)
        top = functools.reduce(jnp.maximum, [jnp.max(s, axis=0, keepdims=True) for s in parts])
        total = sum(jnp.sum(jnp.exp(s - top), axis=0, keepdims=True) for s in parts)
        at = begin + j
        for ref, start in zip(early_refs, starts):
            if start <= at < start + ref.shape[1]:
                k = slice(at - start, at - start + 1)
                top, total = merge((top, total), (ref[0, k], ref[1, k]))
        pair_ref[0, at : at + 1] = top
        pair_ref[1, at : at + 1] = total
    for ref, start in zip(early_refs, starts):
        for k in range(ref.shape[1]):
            if not begin <= start + k < begin + len(picks):
                pair_ref[:, start + k : start + k + 1] = ref[:, k : k + 1]


def score(centers, halves, rows, r, picks, early=(), begin=0, give_half=False, weight=1):
    n_r = len(picks)
    depth = rows[0].shape[1]
    c = sum(x.shape[0] for x in centers)
    starts = [sum(e.shape[1] for e in early[:i]) for i in range(len(early))]
    n_out = max(begin + n_r, sum(e.shape[1] for e in early))
    operands = [*centers, *halves, *rows, *early]
    shapes = [(n_r, c, r), (2, n_out, r)]
    if give_half:
        shapes.append((centers[-1].shape[0], min(r, 128)))
    return pl.pallas_call(
        functools.partial(
            score_kernel, len(centers), len(halves), len(rows), picks, begin, starts, r
        ),
        out_shape=[jax.ShapeDtypeStruct(shape, jnp.float32) for shape in shapes],
        in_specs=[VMEM] * len(operands),
        out_specs=[VMEM] * len(shapes),
        compiler_params=PARAMS,
        cost_estimate=pl.CostEstimate(
            flops=int(2 * n_r * c * r * depth * weight),
            bytes_accessed=int(2 * (n_r * r + c) * depth * weight),
            transcendentals=n_r * c * r,
        ),
        name="score_rows",
    )(*operands)


def join_kernel(places, last, pair_ref, *refs):
    out_ref = refs[-1]
    top, total = pair_ref[0], pair_ref[1]
    for ref, where in zip(refs[:-1], places):
        other = [jnp.concatenate([ref[i, p : p + 1] for p in where]) for i in range(2)]
        top, total = merge((top, total), other)
    if last:
        out_ref[...] = top + jnp.log(total)
    else:
        out_ref[0] = top
        out_ref[1] = total


def join(pairs, routes, places, last):
    others = [lax.ppermute(pairs, "cent", route) for route in routes]
    return pl.pallas_call(
        functools.partial(join_kernel, places, last),
        out_shape=jax.ShapeDtypeStruct(pairs.shape[1:] if last else pairs.shape, jnp.float32),
        in_specs=[VMEM] * (1 + len(others)),
        out_specs=VMEM,
        compiler_params=PARAMS,
        name="join_rows",
    )(pairs, *others)


def sums_kernel(n_parts, picks, parts, lognorm_ref, *refs):
    score_refs, row_refs = refs[:n_parts], refs[n_parts : -len(parts)]
    outs = refs[-len(parts) :]
    ones = jnp.ones((SIDE, max(ref.shape[0] for ref in row_refs)), jnp.bfloat16)
    for out, (places, size, unit) in zip(outs, parts):
        total, tally = None, None
        for i, ref in enumerate(row_refs):
            mine = [j for j, pick in enumerate(picks) if pick[0] == i]
            resp = []
            for j in mine:
                k, block, first = places[j]
                s = score_refs[k][block, first : first + size, :]
                resp.append(jnp.exp(s - lognorm_ref[j : j + 1]).astype(jnp.bfloat16))
            resp = jnp.concatenate(resp, axis=1)
            more = jnp.dot(resp, ref[...], preferred_element_type=jnp.float32)
            count = lax.dot_general(
                ones[:, : ref.shape[0]],
                resp,
                (((1,), (1,)), ((), ())),
                preferred_element_type=jnp.float32,
            )
            total = more if total is None else total + more
            tally = count if tally is None else tally + count
        wide = jnp.concatenate(
            [tally, jnp.zeros((SIDE, total.shape[1] - size), jnp.float32)], axis=1
        )
        if unit:
            total, wide = pack(total, wide[0:1], unit)
        out[0:size] = total
        out[size : size + SIDE] = wide


def pack(total, tally, unit):
    peak = jnp.max(jnp.abs(total), axis=0, keepdims=True)
    power = jnp.clip(jnp.ceil(jnp.log2(peak)), -100.0, 100.0)
    high = jnp.floor(tally * unit)
    rest = (tally * unit - high) * 1024.0
    middle = jnp.floor(rest)
    low = (rest - middle) * 1024.0
    blank = jnp.zeros((SIDE - 4, total.shape[1]), jnp.float32)
    return total * jnp.exp2(14.0 - power), jnp.concatenate([power, high, middle, low, blank])


def unpack(values, unit):
    size = values.shape[0] - SIDE
    power, high, middle, low = (values[size + i : size + i + 1] for i in range(4))
    tally = (high + (middle + low * (1.0 / 1024.0)) * (1.0 / 1024.0)) * (1.0 / unit)
    return values[:size] * jnp.exp2(power - 14.0), tally


def relay_kernel(unit, own_ref, got_ref, out_ref):
    size = own_ref.shape[0] - SIDE
    more, count = unpack(got_ref[...], unit)
    total, wide = pack(own_ref[0:size] + more, own_ref[size : size + 1] + count, unit * 0.5)
    out_ref[0:size] = total
    out_ref[size : size + SIDE] = wide


def relay(own, got, unit):
    return pl.pallas_call(
        functools.partial(relay_kernel, unit),
        out_shape=jax.ShapeDtypeStruct(own.shape, jnp.float32),
        in_specs=[VMEM] * 2,
        out_specs=VMEM,
        compiler_params=PARAMS,
        name="relay_sums",
    )(own, got)


def final_kernel(units, *refs):
    own_ref, got_refs, codebook_ref, new_ref, tally_ref = refs[0], refs[1:-3], *refs[-3:]
    size, depth = codebook_ref.shape
    total, tally = own_ref[0:size], own_ref[size : size + 1]
    for ref, unit in zip(got_refs, units):
        more, count = unpack(ref[...], unit)
        total, tally = total + more, tally + count
    tally = tally[:, :size]
    tally_ref[...] = tally
    weight = 1.0 / (jnp.transpose(jnp.broadcast_to(tally, (size, size)))[:, 0:1] + PRIOR)
    new_ref[...] = (total + PRIOR * codebook_ref[...]) * weight


def finish(codebook, own, got):
    size = codebook.shape[0]
    arrays = [own] + [message.astype(jnp.float32) for message, _ in got] + [codebook]
    new, tally = pl.pallas_call(
        functools.partial(final_kernel, [unit for _, unit in got]),
        out_shape=(
            jax.ShapeDtypeStruct(codebook.shape, jnp.float32),
            jax.ShapeDtypeStruct((1, size), jnp.float32),
        ),
        in_specs=[VMEM] * len(arrays),
        out_specs=(VMEM, VMEM),
        compiler_params=PARAMS,
        name="update_centroids",
    )(*arrays)
    return new, tally[0]


def weighted(parts, lognorm, scores, rows, picks):
    size = parts[0][1]
    depth = rows[0].shape[1]
    n_r, r = lognorm.shape
    return pl.pallas_call(
        functools.partial(sums_kernel, len(scores), picks, parts),
        out_shape=[jax.ShapeDtypeStruct((size + SIDE, depth), jnp.float32) for _ in parts],
        in_specs=[VMEM] * (1 + len(scores) + len(rows)),
        out_specs=[VMEM] * len(parts),
        compiler_params=PARAMS,
        cost_estimate=pl.CostEstimate(
            flops=2 * len(parts) * n_r * size * r * depth,
            bytes_accessed=2 * n_r * r * depth,
            transcendentals=len(parts) * n_r * size * r,
        ),
        name="weighted_sums",
    )(lognorm, *scores, *rows)


def local(n_dp, n_cent, embeddings, codebook):
    own_rows = embeddings.shape[0]
    size = codebook.shape[0]
    unit = 1024.0 / (own_rows * n_cent)
    rounded = codebook.astype(jnp.bfloat16)
    if n_cent == 8:
        by_p = [(i, i ^ (4 if i & 1 else 2)) for i in range(n_cent)]
        by_q = [(i, i ^ (2 if i & 1 else 4)) for i in range(n_cent)]
        from_p = lax.ppermute(embeddings, "cent", by_p)
        from_q = lax.ppermute(embeddings, "cent", by_q)
    if n_dp == 4:
        far = swap(rounded, "dp", n_dp, 2)
        near = swap(rounded, "dp", n_dp, 1)
        most, final = [rounded, near, far], [swap(far, "dp", n_dp, 1)]
    else:
        most = [rounded] + [swap(rounded, "dp", n_dp, m) for m in range(1, n_dp - 1)]
        final = [swap(rounded, "dp", n_dp, n_dp - 1)]
    end = (n_dp - 1) * size
    if n_cent == 8:
        diag = lax.ppermute(from_p, "cent", by_q)
        three = jnp.concatenate([embeddings, from_p, from_q], axis=0)
        give = three
        most = [jnp.concatenate(most, axis=0)]
        of_three = [(0, j * own_rows) for j in range(3)]
        s_0, pair_0, half = score(most, [], [three], own_rows, of_three, give_half=True, weight=1)
        three_core = swap(give, "cent", n_cent, 1)
        s_1, pair_1 = score(most, [half], [three_core], own_rows, of_three, weight=.1)
        diag, pair_0, final = lax.optimization_barrier((diag, pair_0, final))
        s_2, pair_d = score(most, [half], [diag], own_rows, [(0, 0)], weight=40)
        give, pair_d = lax.optimization_barrier((diag, pair_d))
        diag_core = swap(give, "cent", n_cent, 1)
        rows = [three, three_core, diag, diag_core]
        order = [0, 2, 4, 1, 5, 3, 6, 7]
        picks = [(i, j * own_rows) for i in range(2) for j in range(3)] + [(2, 0), (3, 0)]
        early = [pair_0, pair_1, pair_d]
        s_3, pairs, last = score(
            final, [], rows[:3], own_rows, picks[:7], early, give_half=True, weight=1
        )
        s_4, pairs = score(most + final, [half, last], rows[3:], own_rows, [(0, 0)], [pairs], 7)
        scores = [s_0, s_1, s_2, s_4]
        places = [(i, j) for i in range(2) for j in range(3)] + [(2, 0), (3, 0)]
        last_scores = [s_3, s_4]
        last_places = [(0, j, 0) for j in range(7)] + [(1, 0, end)]
    else:
        rows = [embeddings] + [swap(embeddings, "cent", n_cent, m) for m in range(1, n_cent)]
        order = list(range(n_cent))
        picks = [(j, 0) for j in order]
        s_0, pair_0 = score(most, [], rows, own_rows, picks)
        scores = [s_0]
        places = [(0, j) for j in order]
        s_1, pairs = score(final, [], rows, own_rows, picks, [pair_0])
        last_scores, last_places = [s_1], [(0, j, 0) for j in order]
    if n_cent == 8:
        where = [order.index((j ^ 1) & 1 | (j & 2) << 1 | (j & 4) >> 1) for j in order]
        pairs = join(pairs, [partner(n_cent, 1)], [where], False)
        routes = [by_p, by_q, partner(n_cent, 6)]
        where = [[order.index(j ^ mask) for j in order] for mask in (2, 4, 6)]
        lognorm = join(pairs, routes, where, True)
    else:
        for bit in range(n_cent.bit_length() - 1):
            where = [j ^ (1 << bit) for j in order]
            pairs = join(pairs, [partner(n_cent, 1 << bit)], [where], 2 << bit >= n_cent)
        lognorm = pairs

    def part(k, unit):
        return [(i, j, k * size) for i, j in places], size, unit

    (first,) = weighted([(last_places, size, unit)], lognorm, last_scores, rows, picks)
    first = first.astype(jnp.float16)
    if n_dp == 4:
        first = swap(first, "dp", n_dp, 1)
        parts = [part(2, 0), part(1, unit), part(0, 0)]
        far_out, near_out, own = weighted(parts, lognorm, scores, rows, picks)
        far_out = relay(far_out, first.astype(jnp.float32), unit).astype(jnp.float16)
        far_out, near_out = lax.optimization_barrier((far_out, near_out))
        far_out = swap(far_out, "dp", n_dp, 2)
        near_out = swap(near_out.astype(jnp.float16), "dp", n_dp, 1)
        got = [(near_out, unit), (far_out, unit * 0.5)]
    else:
        parts = [part(k, unit if k else 0) for k in range(n_dp - 1)]
        out = weighted(parts, lognorm, scores, rows, picks)
        own = out[0]
        sent = [o.astype(jnp.float16) for o in out[1:]] + [first]
        got = [(swap(m, "dp", n_dp, k + 1), unit) for k, m in enumerate(sent)]
    new_codebook, tally = finish(codebook, own, got)
    return new_codebook, tally, lognorm[0]


def solution(mesh):
    n_dp, n_cent = mesh.shape["dp"], mesh.shape["cent"]

    def run(embeddings, codebook):
        return local(n_dp, n_cent, embeddings, codebook)

    return jax.shard_map(
        run,
        mesh=mesh,
        in_specs=(P(("dp", "cent"), None), P(("cent", "dp"), None)),
        out_specs=(P(("cent", "dp"), None), P(("cent", "dp")), P(("dp", "cent"))),
        check_vma=False,
    )
```

```python
import functools

import jax
import jax.numpy as jnp
from jax import lax
from jax.experimental import pallas as pl
from jax.experimental.pallas import tpu as pltpu
from jax.sharding import PartitionSpec as P

TEMPER = 0.8
PRIOR = 1.0
SIDE = 8
VMEM = pl.BlockSpec(memory_space=pltpu.VMEM)
PARAMS = pltpu.CompilerParams(vmem_limit_bytes=24 << 20)


def partner(size, mask):
    return [(i, i ^ mask) for i in range(size)]


def swap(x, axis, size, mask):
    return lax.ppermute(x, axis, partner(size, mask))


def merge(a, b):
    top = jnp.maximum(a[0], b[0])
    return top, a[1] * jnp.exp(a[0] - top) + b[1] * jnp.exp(b[0] - top)


def score_kernel(n_cent, n_half, n_rows, picks, begin, starts, r, *refs):
    cent_refs, refs = refs[:n_cent], refs[n_cent:]
    half_refs, refs = refs[:n_half], refs[n_half:]
    row_refs, refs = refs[:n_rows], refs[n_rows:]
    early_refs, (score_ref, pair_ref, *half_out) = refs[: len(starts)], refs[len(starts) :]
    lanes = min(r, 128)
    halves = [ref[...] for ref in half_refs]
    for ref in cent_refs[n_half:]:
        squares = jnp.square(ref[...].astype(jnp.float32))
        half = 0.5 * jnp.sum(squares, axis=1, keepdims=True)
        halves.append(jnp.broadcast_to(half, (half.shape[0], lanes)))
    for ref in half_out:
        ref[...] = halves[-1]
    halves = [jnp.concatenate([half] * (r // lanes), axis=1) for half in halves]
    for j, (i, at) in enumerate(picks):
        parts, first = [], 0
        for ref, half in zip(cent_refs, halves):
            product = lax.dot_general(
                ref[...],
                row_refs[i][at : at + r],
                (((1,), (1,)), ((), ())),
                preferred_element_type=jnp.float32,
            )
            s = (product - half) * (1.0 / TEMPER)
            score_ref[j, first : first + s.shape[0]] = s
            first += s.shape[0]
            parts.append(s)
        top = functools.reduce(jnp.maximum, [jnp.max(s, axis=0, keepdims=True) for s in parts])
        total = sum(jnp.sum(jnp.exp(s - top), axis=0, keepdims=True) for s in parts)
        at = begin + j
        for ref, start in zip(early_refs, starts):
            if start <= at < start + ref.shape[1]:
                k = slice(at - start, at - start + 1)
                top, total = merge((top, total), (ref[0, k], ref[1, k]))
        pair_ref[0, at : at + 1] = top
        pair_ref[1, at : at + 1] = total
    for ref, start in zip(early_refs, starts):
        for k in range(ref.shape[1]):
            if not begin <= start + k < begin + len(picks):
                pair_ref[:, start + k : start + k + 1] = ref[:, k : k + 1]


def score(centers, halves, rows, r, picks, early=(), begin=0, give_half=False, weight=1):
    n_r = len(picks)
    depth = rows[0].shape[1]
    c = sum(x.shape[0] for x in centers)
    starts = [sum(e.shape[1] for e in early[:i]) for i in range(len(early))]
    n_out = max(begin + n_r, sum(e.shape[1] for e in early))
    operands = [*centers, *halves, *rows, *early]
    shapes = [(n_r, c, r), (2, n_out, r)]
    if give_half:
        shapes.append((centers[-1].shape[0], min(r, 128)))
    return pl.pallas_call(
        functools.partial(
            score_kernel, len(centers), len(halves), len(rows), picks, begin, starts, r
        ),
        out_shape=[jax.ShapeDtypeStruct(shape, jnp.float32) for shape in shapes],
        in_specs=[VMEM] * len(operands),
        out_specs=[VMEM] * len(shapes),
        compiler_params=PARAMS,
        cost_estimate=pl.CostEstimate(
            flops=int(2 * n_r * c * r * depth * weight),
            bytes_accessed=int(2 * (n_r * r + c) * depth * weight),
            transcendentals=n_r * c * r,
        ),
        name="score_rows",
    )(*operands)


def join_kernel(places, last, pair_ref, *refs):
    out_ref = refs[-1]
    top, total = pair_ref[0], pair_ref[1]
    for ref, where in zip(refs[:-1], places):
        other = [jnp.concatenate([ref[i, p : p + 1] for p in where]) for i in range(2)]
        top, total = merge((top, total), other)
    if last:
        out_ref[...] = top + jnp.log(total)
    else:
        out_ref[0] = top
        out_ref[1] = total


def join(pairs, routes, places, last):
    others = [lax.ppermute(pairs, "cent", route) for route in routes]
    return pl.pallas_call(
        functools.partial(join_kernel, places, last),
        out_shape=jax.ShapeDtypeStruct(pairs.shape[1:] if last else pairs.shape, jnp.float32),
        in_specs=[VMEM] * (1 + len(others)),
        out_specs=VMEM,
        compiler_params=PARAMS,
        name="join_rows",
    )(pairs, *others)


def sums_kernel(n_parts, picks, parts, lognorm_ref, *refs):
    score_refs, row_refs = refs[:n_parts], refs[n_parts : -len(parts)]
    outs = refs[-len(parts) :]
    ones = jnp.ones((SIDE, max(ref.shape[0] for ref in row_refs)), jnp.bfloat16)
    for out, (places, size, unit) in zip(outs, parts):
        total, tally = None, None
        for i, ref in enumerate(row_refs):
            mine = [j for j, pick in enumerate(picks) if pick[0] == i]
            resp = []
            for j in mine:
                k, block, first = places[j]
                s = score_refs[k][block, first : first + size, :]
                resp.append(jnp.exp(s - lognorm_ref[j : j + 1]).astype(jnp.bfloat16))
            resp = jnp.concatenate(resp, axis=1)
            more = jnp.dot(resp, ref[...], preferred_element_type=jnp.float32)
            count = lax.dot_general(
                ones[:, : ref.shape[0]],
                resp,
                (((1,), (1,)), ((), ())),
                preferred_element_type=jnp.float32,
            )
            total = more if total is None else total + more
            tally = count if tally is None else tally + count
        wide = jnp.concatenate(
            [tally, jnp.zeros((SIDE, total.shape[1] - size), jnp.float32)], axis=1
        )
        if unit:
            total, wide = pack(total, wide[0:1], unit)
        out[0:size] = total
        out[size : size + SIDE] = wide


def pack(total, tally, unit):
    peak = jnp.max(jnp.abs(total), axis=0, keepdims=True)
    power = jnp.clip(jnp.ceil(jnp.log2(peak)), -100.0, 100.0)
    high = jnp.floor(tally * unit)
    rest = (tally * unit - high) * 1024.0
    middle = jnp.floor(rest)
    low = (rest - middle) * 1024.0
    blank = jnp.zeros((SIDE - 4, total.shape[1]), jnp.float32)
    return total * jnp.exp2(14.0 - power), jnp.concatenate([power, high, middle, low, blank])


def unpack(values, unit):
    size = values.shape[0] - SIDE
    power, high, middle, low = (values[size + i : size + i + 1] for i in range(4))
    tally = (high + (middle + low * (1.0 / 1024.0)) * (1.0 / 1024.0)) * (1.0 / unit)
    return values[:size] * jnp.exp2(power - 14.0), tally


def relay_kernel(unit, own_ref, got_ref, out_ref):
    size = own_ref.shape[0] - SIDE
    more, count = unpack(got_ref[...], unit)
    total, wide = pack(own_ref[0:size] + more, own_ref[size : size + 1] + count, unit * 0.5)
    out_ref[0:size] = total
    out_ref[size : size + SIDE] = wide


def relay(own, got, unit):
    return pl.pallas_call(
        functools.partial(relay_kernel, unit),
        out_shape=jax.ShapeDtypeStruct(own.shape, jnp.float32),
        in_specs=[VMEM] * 2,
        out_specs=VMEM,
        compiler_params=PARAMS,
        name="relay_sums",
    )(own, got)


def final_kernel(units, *refs):
    own_ref, got_refs, codebook_ref, new_ref, tally_ref = refs[0], refs[1:-3], *refs[-3:]
    size, depth = codebook_ref.shape
    total, tally = own_ref[0:size], own_ref[size : size + 1]
    for ref, unit in zip(got_refs, units):
        more, count = unpack(ref[...], unit)
        total, tally = total + more, tally + count
    tally = tally[:, :size]
    tally_ref[...] = tally
    weight = 1.0 / (jnp.transpose(jnp.broadcast_to(tally, (size, size)))[:, 0:1] + PRIOR)
    new_ref[...] = (total + PRIOR * codebook_ref[...]) * weight


def finish(codebook, own, got):
    size = codebook.shape[0]
    arrays = [own] + [message.astype(jnp.float32) for message, _ in got] + [codebook]
    new, tally = pl.pallas_call(
        functools.partial(final_kernel, [unit for _, unit in got]),
        out_shape=(
            jax.ShapeDtypeStruct(codebook.shape, jnp.float32),
            jax.ShapeDtypeStruct((1, size), jnp.float32),
        ),
        in_specs=[VMEM] * len(arrays),
        out_specs=(VMEM, VMEM),
        compiler_params=PARAMS,
        name="update_centroids",
    )(*arrays)
    return new, tally[0]


def weighted(parts, lognorm, scores, rows, picks):
    size = parts[0][1]
    depth = rows[0].shape[1]
    n_r, r = lognorm.shape
    return pl.pallas_call(
        functools.partial(sums_kernel, len(scores), picks, parts),
        out_shape=[jax.ShapeDtypeStruct((size + SIDE, depth), jnp.float32) for _ in parts],
        in_specs=[VMEM] * (1 + len(scores) + len(rows)),
        out_specs=[VMEM] * len(parts),
        compiler_params=PARAMS,
        cost_estimate=pl.CostEstimate(
            flops=2 * len(parts) * n_r * size * r * depth,
            bytes_accessed=2 * n_r * r * depth,
            transcendentals=len(parts) * n_r * size * r,
        ),
        name="weighted_sums",
    )(lognorm, *scores, *rows)


def local(n_dp, n_cent, embeddings, codebook):
    own_rows = embeddings.shape[0]
    size = codebook.shape[0]
    unit = 1024.0 / (own_rows * n_cent)
    rounded = codebook.astype(jnp.bfloat16)
    if n_cent == 8:
        by_p = [(i, i ^ (4 if i & 1 else 2)) for i in range(n_cent)]
        by_q = [(i, i ^ (2 if i & 1 else 4)) for i in range(n_cent)]
        from_p = lax.ppermute(embeddings, "cent", by_p)
        from_q = lax.ppermute(embeddings, "cent", by_q)
    if n_dp == 4:
        far = swap(rounded, "dp", n_dp, 2)
        near = swap(rounded, "dp", n_dp, 1)
        most, final = [rounded, near, far], [swap(far, "dp", n_dp, 1)]
    else:
        most = [rounded] + [swap(rounded, "dp", n_dp, m) for m in range(1, n_dp - 1)]
        final = [swap(rounded, "dp", n_dp, n_dp - 1)]
    end = (n_dp - 1) * size
    if n_cent == 8:
        diag = lax.ppermute(from_p, "cent", by_q)
        three = jnp.concatenate([embeddings, from_p, from_q], axis=0)
        give, most = lax.optimization_barrier((three, most))
        three_core = swap(give, "cent", n_cent, 1)
        most = [jnp.concatenate(most, axis=0)]
        of_three = [(0, j * own_rows) for j in range(3)]
        s_0, pair_0, half = score(most, [], [three], own_rows, of_three, give_half=True)
        s_1, pair_1 = score(most, [half], [three_core], own_rows, of_three)
        final, pair_1 = lax.optimization_barrier((final, pair_1))
        s_2, pair_2, last = score(
            final, [], [three], own_rows, of_three, [pair_0], give_half=True, weight=3
        )
        give, pair_1, pair_2 = lax.optimization_barrier((diag, pair_1, pair_2))
        rows = [three, three_core, diag, swap(give, "cent", n_cent, 1)]
        order = [0, 2, 4, 1, 5, 3, 6, 7]
        picks = [(i, j * own_rows) for i in range(2) for j in range(3)] + [(2, 0), (3, 0)]
        both = most + final
        s_3, pairs = score(final, [last], rows[1:2], own_rows, of_three, [pair_2, pair_1], 3)
        s_4, pair_4 = score(both, [half, last], rows[2:3], own_rows, [(0, 0)])
        s_5, pairs = score(both, [half, last], rows[3:], own_rows, [(0, 0)], [pairs, pair_4], 7)
        scores = [s_0, s_1, s_4, s_5]
        places = [(i, j) for i in range(2) for j in range(3)] + [(2, 0), (3, 0)]
        last_scores = [s_2, s_3, s_4, s_5]
        last_places = [(i, j, 0) for i in range(2) for j in range(3)] + [(2, 0, end), (3, 0, end)]
    else:
        rows = [embeddings] + [swap(embeddings, "cent", n_cent, m) for m in range(1, n_cent)]
        order = list(range(n_cent))
        picks = [(j, 0) for j in order]
        s_0, pair_0 = score(most, [], rows, own_rows, picks)
        scores = [s_0]
        places = [(0, j) for j in order]
        s_1, pairs = score(final, [], rows, own_rows, picks, [pair_0])
        last_scores, last_places = [s_1], [(0, j, 0) for j in order]
    if n_cent == 8:
        where = [order.index((j ^ 1) & 1 | (j & 2) << 1 | (j & 4) >> 1) for j in order]
        pairs = join(pairs, [partner(n_cent, 1)], [where], False)
        routes = [by_p, by_q, partner(n_cent, 6)]
        where = [[order.index(j ^ mask) for j in order] for mask in (2, 4, 6)]
        lognorm = join(pairs, routes, where, True)
    else:
        for bit in range(n_cent.bit_length() - 1):
            where = [j ^ (1 << bit) for j in order]
            pairs = join(pairs, [partner(n_cent, 1 << bit)], [where], 2 << bit >= n_cent)
        lognorm = pairs

    def part(k, unit):
        return [(i, j, k * size) for i, j in places], size, unit

    (first,) = weighted([(last_places, size, unit)], lognorm, last_scores, rows, picks)
    first = first.astype(jnp.float16)
    if n_dp == 4:
        first = swap(first, "dp", n_dp, 1)
        parts = [part(2, 0), part(1, unit), part(0, 0)]
        far_out, near_out, own = weighted(parts, lognorm, scores, rows, picks)
        far_out = relay(far_out, first.astype(jnp.float32), unit).astype(jnp.float16)
        far_out, near_out = lax.optimization_barrier((far_out, near_out))
        far_out = swap(far_out, "dp", n_dp, 2)
        near_out = swap(near_out.astype(jnp.float16), "dp", n_dp, 1)
        got = [(near_out, unit), (far_out, unit * 0.5)]
    else:
        parts = [part(k, unit if k else 0) for k in range(n_dp - 1)]
        out = weighted(parts, lognorm, scores, rows, picks)
        own = out[0]
        sent = [o.astype(jnp.float16) for o in out[1:]] + [first]
        got = [(swap(m, "dp", n_dp, k + 1), unit) for k, m in enumerate(sent)]
    new_codebook, tally = finish(codebook, own, got)
    return new_codebook, tally, lognorm[0]


def solution(mesh):
    n_dp, n_cent = mesh.shape["dp"], mesh.shape["cent"]

    def run(embeddings, codebook):
        return local(n_dp, n_cent, embeddings, codebook)

    return jax.shard_map(
        run,
        mesh=mesh,
        in_specs=(P(("dp", "cent"), None), P(("cent", "dp"), None)),
        out_specs=(P(("cent", "dp"), None), P(("cent", "dp")), P(("dp", "cent"))),
        check_vma=False,
    )
```

```python
import functools

import jax
import jax.numpy as jnp
from jax import lax
from jax.experimental import pallas as pl
from jax.experimental.pallas import tpu as pltpu
from jax.sharding import PartitionSpec as P

TEMPER = 0.8
PRIOR = 1.0
SIDE = 8
VMEM = pl.BlockSpec(memory_space=pltpu.VMEM)
PARAMS = pltpu.CompilerParams(vmem_limit_bytes=24 << 20)


def partner(size, mask):
    return [(i, i ^ mask) for i in range(size)]


def swap(x, axis, size, mask):
    return lax.ppermute(x, axis, partner(size, mask))


def merge(a, b):
    top = jnp.maximum(a[0], b[0])
    return top, a[1] * jnp.exp(a[0] - top) + b[1] * jnp.exp(b[0] - top)


def score_kernel(n_cent, n_half, n_rows, picks, begin, starts, r, *refs):
    cent_refs, refs = refs[:n_cent], refs[n_cent:]
    half_refs, refs = refs[:n_half], refs[n_half:]
    row_refs, refs = refs[:n_rows], refs[n_rows:]
    early_refs, (score_ref, pair_ref, *half_out) = refs[: len(starts)], refs[len(starts) :]
    lanes = min(r, 128)
    halves = [ref[...] for ref in half_refs]
    for ref in cent_refs[n_half:]:
        squares = jnp.square(ref[...].astype(jnp.float32))
        half = 0.5 * jnp.sum(squares, axis=1, keepdims=True)
        halves.append(jnp.broadcast_to(half, (half.shape[0], lanes)))
    for ref in half_out:
        ref[...] = halves[-1]
    halves = [jnp.concatenate([half] * (r // lanes), axis=1) for half in halves]
    for j, (i, at) in enumerate(picks):
        parts, first = [], 0
        for ref, half in zip(cent_refs, halves):
            product = lax.dot_general(
                ref[...],
                row_refs[i][at : at + r],
                (((1,), (1,)), ((), ())),
                preferred_element_type=jnp.float32,
            )
            s = (product - half) * (1.0 / TEMPER)
            score_ref[j, first : first + s.shape[0]] = s
            first += s.shape[0]
            parts.append(s)
        top = functools.reduce(jnp.maximum, [jnp.max(s, axis=0, keepdims=True) for s in parts])
        total = sum(jnp.sum(jnp.exp(s - top), axis=0, keepdims=True) for s in parts)
        at = begin + j
        for ref, start in zip(early_refs, starts):
            if start <= at < start + ref.shape[1]:
                k = slice(at - start, at - start + 1)
                top, total = merge((top, total), (ref[0, k], ref[1, k]))
        pair_ref[0, at : at + 1] = top
        pair_ref[1, at : at + 1] = total
    for ref, start in zip(early_refs, starts):
        for k in range(ref.shape[1]):
            if not begin <= start + k < begin + len(picks):
                pair_ref[:, start + k : start + k + 1] = ref[:, k : k + 1]


def score(centers, halves, rows, r, picks, early=(), begin=0, give_half=False, weight=1):
    n_r = len(picks)
    depth = rows[0].shape[1]
    c = sum(x.shape[0] for x in centers)
    starts = [sum(e.shape[1] for e in early[:i]) for i in range(len(early))]
    n_out = max(begin + n_r, sum(e.shape[1] for e in early))
    operands = [*centers, *halves, *rows, *early]
    shapes = [(n_r, c, r), (2, n_out, r)]
    if give_half:
        shapes.append((centers[-1].shape[0], min(r, 128)))
    return pl.pallas_call(
        functools.partial(
            score_kernel, len(centers), len(halves), len(rows), picks, begin, starts, r
        ),
        out_shape=[jax.ShapeDtypeStruct(shape, jnp.float32) for shape in shapes],
        in_specs=[VMEM] * len(operands),
        out_specs=[VMEM] * len(shapes),
        compiler_params=PARAMS,
        cost_estimate=pl.CostEstimate(
            flops=int(2 * n_r * c * r * depth * weight),
            bytes_accessed=int(2 * (n_r * r + c) * depth * weight),
            transcendentals=n_r * c * r,
        ),
        name="score_rows",
    )(*operands)


def join_kernel(places, last, pair_ref, *refs):
    out_ref = refs[-1]
    top, total = pair_ref[0], pair_ref[1]
    for ref, where in zip(refs[:-1], places):
        other = [jnp.concatenate([ref[i, p : p + 1] for p in where]) for i in range(2)]
        top, total = merge((top, total), other)
    if last:
        out_ref[...] = top + jnp.log(total)
    else:
        out_ref[0] = top
        out_ref[1] = total


def join(pairs, routes, places, last):
    others = [lax.ppermute(pairs, "cent", route) for route in routes]
    return pl.pallas_call(
        functools.partial(join_kernel, places, last),
        out_shape=jax.ShapeDtypeStruct(pairs.shape[1:] if last else pairs.shape, jnp.float32),
        in_specs=[VMEM] * (1 + len(others)),
        out_specs=VMEM,
        compiler_params=PARAMS,
        name="join_rows",
    )(pairs, *others)


def sums_kernel(n_parts, picks, parts, lognorm_ref, *refs):
    score_refs, row_refs = refs[:n_parts], refs[n_parts : -len(parts)]
    outs = refs[-len(parts) :]
    ones = jnp.ones((SIDE, max(ref.shape[0] for ref in row_refs)), jnp.bfloat16)
    for out, (places, size, unit) in zip(outs, parts):
        total, tally = None, None
        for i, ref in enumerate(row_refs):
            mine = [j for j, pick in enumerate(picks) if pick[0] == i]
            resp = []
            for j in mine:
                k, block, first = places[j]
                s = score_refs[k][block, first : first + size, :]
                resp.append(jnp.exp(s - lognorm_ref[j : j + 1]).astype(jnp.bfloat16))
            resp = jnp.concatenate(resp, axis=1)
            more = jnp.dot(resp, ref[...], preferred_element_type=jnp.float32)
            count = lax.dot_general(
                ones[:, : ref.shape[0]],
                resp,
                (((1,), (1,)), ((), ())),
                preferred_element_type=jnp.float32,
            )
            total = more if total is None else total + more
            tally = count if tally is None else tally + count
        wide = jnp.concatenate(
            [tally, jnp.zeros((SIDE, total.shape[1] - size), jnp.float32)], axis=1
        )
        if unit:
            total, wide = pack(total, wide[0:1], unit)
        out[0:size] = total
        out[size : size + SIDE] = wide


def pack(total, tally, unit):
    peak = jnp.max(jnp.abs(total), axis=0, keepdims=True)
    power = jnp.clip(jnp.ceil(jnp.log2(peak)), -100.0, 100.0)
    high = jnp.floor(tally * unit)
    rest = (tally * unit - high) * 1024.0
    middle = jnp.floor(rest)
    low = (rest - middle) * 1024.0
    blank = jnp.zeros((SIDE - 4, total.shape[1]), jnp.float32)
    return total * jnp.exp2(14.0 - power), jnp.concatenate([power, high, middle, low, blank])


def unpack(values, unit):
    size = values.shape[0] - SIDE
    power, high, middle, low = (values[size + i : size + i + 1] for i in range(4))
    tally = (high + (middle + low * (1.0 / 1024.0)) * (1.0 / 1024.0)) * (1.0 / unit)
    return values[:size] * jnp.exp2(power - 14.0), tally


def relay_kernel(unit, own_ref, got_ref, out_ref):
    size = own_ref.shape[0] - SIDE
    more, count = unpack(got_ref[...], unit)
    total, wide = pack(own_ref[0:size] + more, own_ref[size : size + 1] + count, unit * 0.5)
    out_ref[0:size] = total
    out_ref[size : size + SIDE] = wide


def relay(own, got, unit):
    return pl.pallas_call(
        functools.partial(relay_kernel, unit),
        out_shape=jax.ShapeDtypeStruct(own.shape, jnp.float32),
        in_specs=[VMEM] * 2,
        out_specs=VMEM,
        compiler_params=PARAMS,
        name="relay_sums",
    )(own, got)


def final_kernel(units, *refs):
    own_ref, got_refs, codebook_ref, new_ref, tally_ref = refs[0], refs[1:-3], *refs[-3:]
    size, depth = codebook_ref.shape
    total, tally = own_ref[0:size], own_ref[size : size + 1]
    for ref, unit in zip(got_refs, units):
        more, count = unpack(ref[...], unit)
        total, tally = total + more, tally + count
    tally = tally[:, :size]
    tally_ref[...] = tally
    weight = 1.0 / (jnp.transpose(jnp.broadcast_to(tally, (size, size)))[:, 0:1] + PRIOR)
    new_ref[...] = (total + PRIOR * codebook_ref[...]) * weight


def finish(codebook, own, got):
    size = codebook.shape[0]
    arrays = [own] + [message.astype(jnp.float32) for message, _ in got] + [codebook]
    new, tally = pl.pallas_call(
        functools.partial(final_kernel, [unit for _, unit in got]),
        out_shape=(
            jax.ShapeDtypeStruct(codebook.shape, jnp.float32),
            jax.ShapeDtypeStruct((1, size), jnp.float32),
        ),
        in_specs=[VMEM] * len(arrays),
        out_specs=(VMEM, VMEM),
        compiler_params=PARAMS,
        name="update_centroids",
    )(*arrays)
    return new, tally[0]


def weighted(parts, lognorm, scores, rows, picks):
    size = parts[0][1]
    depth = rows[0].shape[1]
    n_r, r = lognorm.shape
    return pl.pallas_call(
        functools.partial(sums_kernel, len(scores), picks, parts),
        out_shape=[jax.ShapeDtypeStruct((size + SIDE, depth), jnp.float32) for _ in parts],
        in_specs=[VMEM] * (1 + len(scores) + len(rows)),
        out_specs=[VMEM] * len(parts),
        compiler_params=PARAMS,
        cost_estimate=pl.CostEstimate(
            flops=2 * len(parts) * n_r * size * r * depth,
            bytes_accessed=2 * n_r * r * depth,
            transcendentals=len(parts) * n_r * size * r,
        ),
        name="weighted_sums",
    )(lognorm, *scores, *rows)


def local(n_dp, n_cent, embeddings, codebook):
    own_rows = embeddings.shape[0]
    size = codebook.shape[0]
    unit = 1024.0 / (own_rows * n_cent)
    rounded = codebook.astype(jnp.bfloat16)
    if n_cent == 8:
        by_p = [(i, i ^ (4 if i & 1 else 2)) for i in range(n_cent)]
        by_q = [(i, i ^ (2 if i & 1 else 4)) for i in range(n_cent)]
        from_p = lax.ppermute(embeddings, "cent", by_p)
        from_q = lax.ppermute(embeddings, "cent", by_q)
    if n_dp == 4:
        far = swap(rounded, "dp", n_dp, 2)
        near = swap(rounded, "dp", n_dp, 1)
        most, final = [rounded, near, far], [swap(far, "dp", n_dp, 1)]
    else:
        most = [rounded] + [swap(rounded, "dp", n_dp, m) for m in range(1, n_dp - 1)]
        final = [swap(rounded, "dp", n_dp, n_dp - 1)]
    end = (n_dp - 1) * size
    if n_cent == 8:
        diag = lax.ppermute(from_p, "cent", by_q)
        three = jnp.concatenate([embeddings, from_p, from_q], axis=0)
        give = three
        most = [jnp.concatenate(most, axis=0)]
        of_three = [(0, j * own_rows) for j in range(3)]
        s_0, pair_0, half = score(most, [], [three], own_rows, of_three, give_half=True, weight=1)
        three_core = swap(give, "cent", n_cent, 1)
        diag, pair_0 = lax.optimization_barrier((diag, pair_0))
        s_1, pair_1 = score(most, [half], [diag], own_rows, [(0, 0)], weight=.1)
        give, pair_1 = lax.optimization_barrier((diag, pair_1))
        diag_core = swap(give, "cent", n_cent, 1)
        rows = [three, diag, three_core, diag_core]
        order = [0, 2, 4, 6, 1, 5, 3, 7]
        picks = of_three + [(1, 0)] + [(2, at) for _, at in of_three] + [(3, 0)]
        s_2, pair_2, last = score(
            final, [], rows[:2], own_rows, picks[:4], [pair_0, pair_1], give_half=True, weight=60
        )
        three_core, last = lax.optimization_barrier((three_core, last))
        rows[2], both, halves = three_core, most + final, [half, last]
        s_3, pair_3 = score(both, halves, [three_core], own_rows, of_three, weight=.1)
        s_4, pairs = score(both, halves, rows[3:], own_rows, [(0, 0)], [pair_2, pair_3], 7)
        scores = [s_0, s_1, s_3, s_4]
        places = [(0, j) for j in range(3)] + [(1, 0)] + [(2, j) for j in range(3)] + [(3, 0)]
        last_scores = [s_2, s_3, s_4]
        last_places = [(0, j, 0) for j in range(4)] + [(1, j, end) for j in range(3)] + [(2, 0, end)]
    else:
        rows = [embeddings] + [swap(embeddings, "cent", n_cent, m) for m in range(1, n_cent)]
        order = list(range(n_cent))
        picks = [(j, 0) for j in order]
        s_0, pair_0 = score(most, [], rows, own_rows, picks)
        scores = [s_0]
        places = [(0, j) for j in order]
        s_1, pairs = score(final, [], rows, own_rows, picks, [pair_0])
        last_scores, last_places = [s_1], [(0, j, 0) for j in order]
    if n_cent == 8:
        where = [order.index((j ^ 1) & 1 | (j & 2) << 1 | (j & 4) >> 1) for j in order]
        pairs = join(pairs, [partner(n_cent, 1)], [where], False)
        routes = [by_p, by_q, partner(n_cent, 6)]
        where = [[order.index(j ^ mask) for j in order] for mask in (2, 4, 6)]
        lognorm = join(pairs, routes, where, True)
    else:
        for bit in range(n_cent.bit_length() - 1):
            where = [j ^ (1 << bit) for j in order]
            pairs = join(pairs, [partner(n_cent, 1 << bit)], [where], 2 << bit >= n_cent)
        lognorm = pairs

    def part(k, unit):
        return [(i, j, k * size) for i, j in places], size, unit

    (first,) = weighted([(last_places, size, unit)], lognorm, last_scores, rows, picks)
    first = first.astype(jnp.float16)
    if n_dp == 4:
        first = swap(first, "dp", n_dp, 1)
        parts = [part(2, 0), part(1, unit), part(0, 0)]
        far_out, near_out, own = weighted(parts, lognorm, scores, rows, picks)
        far_out = relay(far_out, first.astype(jnp.float32), unit).astype(jnp.float16)
        far_out, near_out = lax.optimization_barrier((far_out, near_out))
        far_out = swap(far_out, "dp", n_dp, 2)
        near_out = swap(near_out.astype(jnp.float16), "dp", n_dp, 1)
        got = [(near_out, unit), (far_out, unit * 0.5)]
    else:
        parts = [part(k, unit if k else 0) for k in range(n_dp - 1)]
        out = weighted(parts, lognorm, scores, rows, picks)
        own = out[0]
        sent = [o.astype(jnp.float16) for o in out[1:]] + [first]
        got = [(swap(m, "dp", n_dp, k + 1), unit) for k, m in enumerate(sent)]
    new_codebook, tally = finish(codebook, own, got)
    return new_codebook, tally, lognorm[0]


def solution(mesh):
    n_dp, n_cent = mesh.shape["dp"], mesh.shape["cent"]

    def run(embeddings, codebook):
        return local(n_dp, n_cent, embeddings, codebook)

    return jax.shard_map(
        run,
        mesh=mesh,
        in_specs=(P(("dp", "cent"), None), P(("cent", "dp"), None)),
        out_specs=(P(("cent", "dp"), None), P(("cent", "dp")), P(("dp", "cent"))),
        check_vma=False,
    )
```

```python
import functools

import jax
import jax.numpy as jnp
from jax import lax
from jax.experimental import pallas as pl
from jax.experimental.pallas import tpu as pltpu
from jax.sharding import PartitionSpec as P

TEMPER = 0.8
PRIOR = 1.0
SIDE = 8
VMEM = pl.BlockSpec(memory_space=pltpu.VMEM)
PARAMS = pltpu.CompilerParams(vmem_limit_bytes=24 << 20)


def partner(size, mask):
    return [(i, i ^ mask) for i in range(size)]


def swap(x, axis, size, mask):
    return lax.ppermute(x, axis, partner(size, mask))


def merge(a, b):
    top = jnp.maximum(a[0], b[0])
    return top, a[1] * jnp.exp(a[0] - top) + b[1] * jnp.exp(b[0] - top)


def score_kernel(n_cent, n_half, n_rows, picks, begin, starts, r, *refs):
    cent_refs, refs = refs[:n_cent], refs[n_cent:]
    half_refs, refs = refs[:n_half], refs[n_half:]
    row_refs, refs = refs[:n_rows], refs[n_rows:]
    early_refs, (score_ref, pair_ref, *half_out) = refs[: len(starts)], refs[len(starts) :]
    lanes = min(r, 128)
    halves = [ref[...] for ref in half_refs]
    for ref in cent_refs[n_half:]:
        squares = jnp.square(ref[...].astype(jnp.float32))
        half = 0.5 * jnp.sum(squares, axis=1, keepdims=True)
        halves.append(jnp.broadcast_to(half, (half.shape[0], lanes)))
    for ref in half_out:
        ref[...] = halves[-1]
    halves = [jnp.concatenate([half] * (r // lanes), axis=1) for half in halves]
    for j, (i, at) in enumerate(picks):
        parts, first = [], 0
        for ref, half in zip(cent_refs, halves):
            product = lax.dot_general(
                ref[...],
                row_refs[i][at : at + r],
                (((1,), (1,)), ((), ())),
                preferred_element_type=jnp.float32,
            )
            s = (product - half) * (1.0 / TEMPER)
            score_ref[j, first : first + s.shape[0]] = s
            first += s.shape[0]
            parts.append(s)
        top = functools.reduce(jnp.maximum, [jnp.max(s, axis=0, keepdims=True) for s in parts])
        total = sum(jnp.sum(jnp.exp(s - top), axis=0, keepdims=True) for s in parts)
        at = begin + j
        for ref, start in zip(early_refs, starts):
            if start <= at < start + ref.shape[1]:
                k = slice(at - start, at - start + 1)
                top, total = merge((top, total), (ref[0, k], ref[1, k]))
        pair_ref[0, at : at + 1] = top
        pair_ref[1, at : at + 1] = total
    for ref, start in zip(early_refs, starts):
        for k in range(ref.shape[1]):
            if not begin <= start + k < begin + len(picks):
                pair_ref[:, start + k : start + k + 1] = ref[:, k : k + 1]


def score(centers, halves, rows, r, picks, early=(), begin=0, give_half=False, weight=1):
    n_r = len(picks)
    depth = rows[0].shape[1]
    c = sum(x.shape[0] for x in centers)
    starts = [sum(e.shape[1] for e in early[:i]) for i in range(len(early))]
    n_out = max(begin + n_r, sum(e.shape[1] for e in early))
    operands = [*centers, *halves, *rows, *early]
    shapes = [(n_r, c, r), (2, n_out, r)]
    if give_half:
        shapes.append((centers[-1].shape[0], min(r, 128)))
    return pl.pallas_call(
        functools.partial(
            score_kernel, len(centers), len(halves), len(rows), picks, begin, starts, r
        ),
        out_shape=[jax.ShapeDtypeStruct(shape, jnp.float32) for shape in shapes],
        in_specs=[VMEM] * len(operands),
        out_specs=[VMEM] * len(shapes),
        compiler_params=PARAMS,
        cost_estimate=pl.CostEstimate(
            flops=int(2 * n_r * c * r * depth * weight),
            bytes_accessed=int(2 * (n_r * r + c) * depth * weight),
            transcendentals=n_r * c * r,
        ),
        name="score_rows",
    )(*operands)


def join_kernel(places, last, pair_ref, *refs):
    out_ref = refs[-1]
    top, total = pair_ref[0], pair_ref[1]
    for ref, where in zip(refs[:-1], places):
        other = [jnp.concatenate([ref[i, p : p + 1] for p in where]) for i in range(2)]
        top, total = merge((top, total), other)
    if last:
        out_ref[...] = top + jnp.log(total)
    else:
        out_ref[0] = top
        out_ref[1] = total


def join(pairs, routes, places, last):
    others = [lax.ppermute(pairs, "cent", route) for route in routes]
    return pl.pallas_call(
        functools.partial(join_kernel, places, last),
        out_shape=jax.ShapeDtypeStruct(pairs.shape[1:] if last else pairs.shape, jnp.float32),
        in_specs=[VMEM] * (1 + len(others)),
        out_specs=VMEM,
        compiler_params=PARAMS,
        name="join_rows",
    )(pairs, *others)


def sums_kernel(n_parts, picks, parts, lognorm_ref, *refs):
    score_refs, row_refs = refs[:n_parts], refs[n_parts : -len(parts)]
    outs = refs[-len(parts) :]
    ones = jnp.ones((SIDE, max(ref.shape[0] for ref in row_refs)), jnp.bfloat16)
    for out, (places, size, unit) in zip(outs, parts):
        total, tally = None, None
        for i, ref in enumerate(row_refs):
            mine = [j for j, pick in enumerate(picks) if pick[0] == i]
            resp = []
            for j in mine:
                k, block, first = places[j]
                s = score_refs[k][block, first : first + size, :]
                resp.append(jnp.exp(s - lognorm_ref[j : j + 1]).astype(jnp.bfloat16))
            resp = jnp.concatenate(resp, axis=1)
            more = jnp.dot(resp, ref[...], preferred_element_type=jnp.float32)
            count = lax.dot_general(
                ones[:, : ref.shape[0]],
                resp,
                (((1,), (1,)), ((), ())),
                preferred_element_type=jnp.float32,
            )
            total = more if total is None else total + more
            tally = count if tally is None else tally + count
        wide = jnp.concatenate(
            [tally, jnp.zeros((SIDE, total.shape[1] - size), jnp.float32)], axis=1
        )
        if unit:
            total, wide = pack(total, wide[0:1], unit)
        out[0:size] = total
        out[size : size + SIDE] = wide


def pack(total, tally, unit):
    peak = jnp.max(jnp.abs(total), axis=0, keepdims=True)
    power = jnp.clip(jnp.ceil(jnp.log2(peak)), -100.0, 100.0)
    high = jnp.floor(tally * unit)
    rest = (tally * unit - high) * 1024.0
    middle = jnp.floor(rest)
    low = (rest - middle) * 1024.0
    blank = jnp.zeros((SIDE - 4, total.shape[1]), jnp.float32)
    return total * jnp.exp2(14.0 - power), jnp.concatenate([power, high, middle, low, blank])


def unpack(values, unit):
    size = values.shape[0] - SIDE
    power, high, middle, low = (values[size + i : size + i + 1] for i in range(4))
    tally = (high + (middle + low * (1.0 / 1024.0)) * (1.0 / 1024.0)) * (1.0 / unit)
    return values[:size] * jnp.exp2(power - 14.0), tally


def add_kernel(unit, packed, at, own_ref, got_ref, out_ref):
    size, depth = out_ref.shape[0] - SIDE, out_ref.shape[1]
    more, tally = unpack(got_ref[...], unit)
    total = own_ref[0:size, at : at + depth] + more
    tally = own_ref[size : size + 1, at : at + depth] + tally
    if packed:
        total, wide = pack(total, tally, packed)
    else:
        wide = jnp.concatenate([tally, jnp.zeros((SIDE - 1, depth), jnp.float32)])
    out_ref[0:size] = total
    out_ref[size : size + SIDE] = wide


def add_part(own, got, at, unit, packed, weight=0):
    got = got.astype(jnp.float32)
    return pl.pallas_call(
        functools.partial(add_kernel, unit, packed, at),
        out_shape=jax.ShapeDtypeStruct(got.shape, jnp.float32),
        in_specs=[VMEM] * 2,
        out_specs=VMEM,
        compiler_params=PARAMS,
        cost_estimate=pl.CostEstimate(
            flops=got.size * (1 + weight), bytes_accessed=0, transcendentals=0
        ),
        name="add_sums",
    )(own, got)


def final_kernel(units, *refs):
    part_refs, got_refs = refs[: -3 - len(units)], refs[-3 - len(units) : -3]
    codebook_ref, new_ref, tally_ref = refs[-3:]
    size = codebook_ref.shape[0]
    total = jnp.concatenate([ref[0:size] for ref in part_refs], axis=1)
    tally = part_refs[0][size : size + 1, 0:size]
    for ref, unit in zip(got_refs, units):
        more, count = unpack(ref[...], unit)
        total, tally = total + more, tally + count[:, 0:size]
    tally_ref[...] = tally
    weight = 1.0 / (jnp.transpose(jnp.broadcast_to(tally, (size, size)))[:, 0:1] + PRIOR)
    new_ref[...] = (total + PRIOR * codebook_ref[...]) * weight


def finish(codebook, parts, got):
    size = codebook.shape[0]
    arrays = [*parts, *[message.astype(jnp.float32) for message, _ in got], codebook]
    new, tally = pl.pallas_call(
        functools.partial(final_kernel, [unit for _, unit in got]),
        out_shape=(
            jax.ShapeDtypeStruct(codebook.shape, jnp.float32),
            jax.ShapeDtypeStruct((1, size), jnp.float32),
        ),
        in_specs=[VMEM] * len(arrays),
        out_specs=(VMEM, VMEM),
        compiler_params=PARAMS,
        name="update_centroids",
    )(*arrays)
    return new, tally[0]


def weighted(parts, lognorm, scores, rows, picks):
    size = parts[0][1]
    depth = rows[0].shape[1]
    n_r, r = lognorm.shape
    return pl.pallas_call(
        functools.partial(sums_kernel, len(scores), picks, parts),
        out_shape=[jax.ShapeDtypeStruct((size + SIDE, depth), jnp.float32) for _ in parts],
        in_specs=[VMEM] * (1 + len(scores) + len(rows)),
        out_specs=[VMEM] * len(parts),
        compiler_params=PARAMS,
        cost_estimate=pl.CostEstimate(
            flops=2 * len(parts) * n_r * size * r * depth,
            bytes_accessed=2 * n_r * r * depth,
            transcendentals=len(parts) * n_r * size * r,
        ),
        name="weighted_sums",
    )(lognorm, *scores, *rows)


def local(n_dp, n_cent, embeddings, codebook):
    own_rows = embeddings.shape[0]
    size = codebook.shape[0]
    unit = 1024.0 / (own_rows * n_cent)
    rounded = codebook.astype(jnp.bfloat16)
    if n_cent == 8:
        by_p = [(i, i ^ (4 if i & 1 else 2)) for i in range(n_cent)]
        by_q = [(i, i ^ (2 if i & 1 else 4)) for i in range(n_cent)]
        from_p = lax.ppermute(embeddings, "cent", by_p)
        from_q = lax.ppermute(embeddings, "cent", by_q)
    if n_dp == 4:
        far = swap(rounded, "dp", n_dp, 2)
        near = swap(rounded, "dp", n_dp, 1)
        most, final = [rounded, near, far], [swap(far, "dp", n_dp, 1)]
    else:
        most = [rounded] + [swap(rounded, "dp", n_dp, m) for m in range(1, n_dp - 1)]
        final = [swap(rounded, "dp", n_dp, n_dp - 1)]
    end = (n_dp - 1) * size
    if n_cent == 8:
        diag = lax.ppermute(from_p, "cent", by_q)
        three = jnp.concatenate([embeddings, from_p, from_q], axis=0)
        give = three
        most = [jnp.concatenate(most, axis=0)]
        of_three = [(0, j * own_rows) for j in range(3)]
        s_0, pair_0, half = score(most, [], [three], own_rows, of_three, give_half=True, weight=1)
        three_core = swap(give, "cent", n_cent, 1)
        diag, pair_0 = lax.optimization_barrier((diag, pair_0))
        s_1, pair_1 = score(most, [half], [diag], own_rows, [(0, 0)], weight=.1)
        give, pair_1 = lax.optimization_barrier((diag, pair_1))
        diag_core = swap(give, "cent", n_cent, 1)
        rows = [three, diag, three_core, diag_core]
        order = [0, 2, 4, 6, 1, 5, 3, 7]
        picks = of_three + [(1, 0)] + [(2, at) for _, at in of_three] + [(3, 0)]
        s_2, pair_2, last = score(
            final, [], rows[:2], own_rows, picks[:4], [pair_0, pair_1], give_half=True, weight=60
        )
        three_core, last = lax.optimization_barrier((three_core, last))
        rows[2], both, halves = three_core, most + final, [half, last]
        s_3, pair_3 = score(both, halves, [three_core], own_rows, of_three, weight=.1)
        s_4, pairs = score(both, halves, rows[3:], own_rows, [(0, 0)], [pair_2, pair_3], 7)
        scores = [s_0, s_1, s_3, s_4]
        places = [(0, j) for j in range(3)] + [(1, 0)] + [(2, j) for j in range(3)] + [(3, 0)]
        last_scores = [s_2, s_3, s_4]
        last_places = [(0, j, 0) for j in range(4)] + [(1, j, end) for j in range(3)] + [(2, 0, end)]
    else:
        rows = [embeddings] + [swap(embeddings, "cent", n_cent, m) for m in range(1, n_cent)]
        order = list(range(n_cent))
        picks = [(j, 0) for j in order]
        s_0, pair_0 = score(most, [], rows, own_rows, picks)
        scores = [s_0]
        places = [(0, j) for j in order]
        s_1, pairs = score(final, [], rows, own_rows, picks, [pair_0])
        last_scores, last_places = [s_1], [(0, j, 0) for j in order]
    if n_cent == 8:
        where = [order.index((j ^ 1) & 1 | (j & 2) << 1 | (j & 4) >> 1) for j in order]
        pairs = join(pairs, [partner(n_cent, 1)], [where], False)
        routes = [by_p, by_q, partner(n_cent, 6)]
        where = [[order.index(j ^ mask) for j in order] for mask in (2, 4, 6)]
        lognorm = join(pairs, routes, where, True)
    else:
        for bit in range(n_cent.bit_length() - 1):
            where = [j ^ (1 << bit) for j in order]
            pairs = join(pairs, [partner(n_cent, 1 << bit)], [where], 2 << bit >= n_cent)
        lognorm = pairs

    def part(k, unit):
        return [(i, j, k * size) for i, j in places], size, unit

    (first,) = weighted([(last_places, size, unit)], lognorm, last_scores, rows, picks)
    if n_dp == 4:
        cut = first.shape[1] // 2
        first = [swap(first[:, i : i + cut].astype(jnp.float16), "dp", n_dp, 1) for i in (0, cut)]
        parts = [part(2, 0), part(1, unit), part(0, 0)]
        far_sum, near_sum, own = weighted(parts, lognorm, scores, rows, picks)
        far = []
        for i, got in enumerate(first):
            message = add_part(far_sum, got, i * cut, unit, unit * 0.5)
            far.append(swap(message.astype(jnp.float16), "dp", n_dp, 2))
        near = swap(near_sum.astype(jnp.float16), "dp", n_dp, 1)
        parts = [add_part(own, far[0], 0, unit * 0.5, 0, 200000), None]
        far[1], parts[0] = lax.optimization_barrier((far[1], parts[0]))
        parts[1] = add_part(own, far[1], cut, unit * 0.5, 0)
        got = [(near, unit)]
    else:
        parts = [part(k, unit if k else 0) for k in range(n_dp - 1)]
        own, *others = weighted(parts, lognorm, scores, rows, picks)
        parts = [own]
        others = [other.astype(jnp.float16) for other in others + [first]]
        got = [(swap(other, "dp", n_dp, k + 1), unit) for k, other in enumerate(others)]
    new_codebook, tally = finish(codebook, parts, got)
    return new_codebook, tally, lognorm[0]


def solution(mesh):
    n_dp, n_cent = mesh.shape["dp"], mesh.shape["cent"]

    def run(embeddings, codebook):
        return local(n_dp, n_cent, embeddings, codebook)

    return jax.shard_map(
        run,
        mesh=mesh,
        in_specs=(P(("dp", "cent"), None), P(("cent", "dp"), None)),
        out_specs=(P(("cent", "dp"), None), P(("cent", "dp")), P(("dp", "cent"))),
        check_vma=False,
    )
```

```python
import functools

import jax
import jax.numpy as jnp
from jax import lax
from jax.experimental import pallas as pl
from jax.experimental.pallas import tpu as pltpu
from jax.sharding import PartitionSpec as P

TEMPER = 0.8
PRIOR = 1.0
SIDE = 8
VMEM = pl.BlockSpec(memory_space=pltpu.VMEM)
PARAMS = pltpu.CompilerParams(vmem_limit_bytes=24 << 20)


def partner(size, mask):
    return [(i, i ^ mask) for i in range(size)]


def swap(x, axis, size, mask):
    return lax.ppermute(x, axis, partner(size, mask))


def merge(a, b):
    top = jnp.maximum(a[0], b[0])
    return top, a[1] * jnp.exp(a[0] - top) + b[1] * jnp.exp(b[0] - top)


def score_kernel(n_cent, n_half, n_rows, picks, begin, starts, r, *refs):
    cent_refs, refs = refs[:n_cent], refs[n_cent:]
    half_refs, refs = refs[:n_half], refs[n_half:]
    row_refs, refs = refs[:n_rows], refs[n_rows:]
    early_refs, (score_ref, pair_ref, *half_out) = refs[: len(starts)], refs[len(starts) :]
    lanes = min(r, 128)
    halves = [ref[...] for ref in half_refs]
    for ref in cent_refs[n_half:]:
        squares = jnp.square(ref[...].astype(jnp.float32))
        half = 0.5 * jnp.sum(squares, axis=1, keepdims=True)
        halves.append(jnp.broadcast_to(half, (half.shape[0], lanes)))
    for ref in half_out:
        ref[...] = halves[-1]
    halves = [jnp.concatenate([half] * (r // lanes), axis=1) for half in halves]
    for j, (i, at) in enumerate(picks):
        parts, first = [], 0
        for ref, half in zip(cent_refs, halves):
            product = lax.dot_general(
                ref[...],
                row_refs[i][at : at + r],
                (((1,), (1,)), ((), ())),
                preferred_element_type=jnp.float32,
            )
            s = (product - half) * (1.0 / TEMPER)
            score_ref[j, first : first + s.shape[0]] = s
            first += s.shape[0]
            parts.append(s)
        top = functools.reduce(jnp.maximum, [jnp.max(s, axis=0, keepdims=True) for s in parts])
        total = sum(jnp.sum(jnp.exp(s - top), axis=0, keepdims=True) for s in parts)
        at = begin + j
        for ref, start in zip(early_refs, starts):
            if start <= at < start + ref.shape[1]:
                k = slice(at - start, at - start + 1)
                top, total = merge((top, total), (ref[0, k], ref[1, k]))
        pair_ref[0, at : at + 1] = top
        pair_ref[1, at : at + 1] = total
    for ref, start in zip(early_refs, starts):
        for k in range(ref.shape[1]):
            if not begin <= start + k < begin + len(picks):
                pair_ref[:, start + k : start + k + 1] = ref[:, k : k + 1]


def score(centers, halves, rows, r, picks, early=(), begin=0, give_half=False, weight=1):
    n_r = len(picks)
    depth = rows[0].shape[1]
    c = sum(x.shape[0] for x in centers)
    starts = [sum(e.shape[1] for e in early[:i]) for i in range(len(early))]
    n_out = max(begin + n_r, sum(e.shape[1] for e in early))
    operands = [*centers, *halves, *rows, *early]
    shapes = [(n_r, c, r), (2, n_out, r)]
    if give_half:
        shapes.append((centers[-1].shape[0], min(r, 128)))
    return pl.pallas_call(
        functools.partial(
            score_kernel, len(centers), len(halves), len(rows), picks, begin, starts, r
        ),
        out_shape=[jax.ShapeDtypeStruct(shape, jnp.float32) for shape in shapes],
        in_specs=[VMEM] * len(operands),
        out_specs=[VMEM] * len(shapes),
        compiler_params=PARAMS,
        cost_estimate=pl.CostEstimate(
            flops=int(2 * n_r * c * r * depth * weight),
            bytes_accessed=int(2 * (n_r * r + c) * depth * weight),
            transcendentals=n_r * c * r,
        ),
        name="score_rows",
    )(*operands)


def join_kernel(places, last, pair_ref, *refs):
    out_ref = refs[-1]
    top, total = pair_ref[0], pair_ref[1]
    for ref, where in zip(refs[:-1], places):
        other = [jnp.concatenate([ref[i, p : p + 1] for p in where]) for i in range(2)]
        top, total = merge((top, total), other)
    if last:
        out_ref[...] = top + jnp.log(total)
    else:
        out_ref[0] = top
        out_ref[1] = total


def join(pairs, routes, places, last):
    others = [lax.ppermute(pairs, "cent", route) for route in routes]
    return pl.pallas_call(
        functools.partial(join_kernel, places, last),
        out_shape=jax.ShapeDtypeStruct(pairs.shape[1:] if last else pairs.shape, jnp.float32),
        in_specs=[VMEM] * (1 + len(others)),
        out_specs=VMEM,
        compiler_params=PARAMS,
        name="join_rows",
    )(pairs, *others)


def sums_kernel(n_parts, picks, parts, lognorm_ref, *refs):
    score_refs, row_refs = refs[:n_parts], refs[n_parts : -len(parts)]
    outs = refs[-len(parts) :]
    ones = jnp.ones((SIDE, max(ref.shape[0] for ref in row_refs)), jnp.bfloat16)
    for out, (places, size, unit) in zip(outs, parts):
        total, tally = None, None
        for i, ref in enumerate(row_refs):
            mine = [j for j, pick in enumerate(picks) if pick[0] == i]
            resp = []
            for j in mine:
                k, block, first = places[j]
                s = score_refs[k][block, first : first + size, :]
                resp.append(jnp.exp(s - lognorm_ref[j : j + 1]).astype(jnp.bfloat16))
            resp = jnp.concatenate(resp, axis=1)
            more = jnp.dot(resp, ref[...], preferred_element_type=jnp.float32)
            count = lax.dot_general(
                ones[:, : ref.shape[0]],
                resp,
                (((1,), (1,)), ((), ())),
                preferred_element_type=jnp.float32,
            )
            total = more if total is None else total + more
            tally = count if tally is None else tally + count
        wide = jnp.concatenate(
            [tally, jnp.zeros((SIDE, total.shape[1] - size), jnp.float32)], axis=1
        )
        if unit:
            total, wide = pack(total, wide[0:1], unit)
        out[0:size] = total
        out[size : size + SIDE] = wide


def pack(total, tally, unit):
    peak = jnp.max(jnp.abs(total), axis=0, keepdims=True)
    power = jnp.clip(jnp.ceil(jnp.log2(peak)), -100.0, 100.0)
    high = jnp.floor(tally * unit)
    rest = (tally * unit - high) * 1024.0
    middle = jnp.floor(rest)
    low = (rest - middle) * 1024.0
    blank = jnp.zeros((SIDE - 4, total.shape[1]), jnp.float32)
    return total * jnp.exp2(14.0 - power), jnp.concatenate([power, high, middle, low, blank])


def unpack(values, unit):
    size = values.shape[0] - SIDE
    power, high, middle, low = (values[size + i : size + i + 1] for i in range(4))
    tally = (high + (middle + low * (1.0 / 1024.0)) * (1.0 / 1024.0)) * (1.0 / unit)
    return values[:size] * jnp.exp2(power - 14.0), tally


def add_kernel(unit, packed, at, own_ref, got_ref, out_ref):
    size, depth = out_ref.shape[0] - SIDE, out_ref.shape[1]
    total, tally = unpack(got_ref[...], unit)
    if at >= 0:
        total = own_ref[0:size, at : at + depth] + total
        tally = own_ref[size : size + 1, at : at + depth] + tally
    if packed:
        total, wide = pack(total, tally, packed)
    else:
        wide = jnp.concatenate([tally, jnp.zeros((SIDE - 1, depth), jnp.float32)])
    out_ref[0:size] = total
    out_ref[size : size + SIDE] = wide


def add_part(own, got, at, unit, packed, weight=0):
    got = got.astype(jnp.float32)
    return pl.pallas_call(
        functools.partial(add_kernel, unit, packed, at),
        out_shape=jax.ShapeDtypeStruct(got.shape, jnp.float32),
        in_specs=[VMEM] * 2,
        out_specs=VMEM,
        compiler_params=PARAMS,
        cost_estimate=pl.CostEstimate(
            flops=got.size * (1 + weight), bytes_accessed=0, transcendentals=0
        ),
        name="add_sums",
    )(own, got)


def final_kernel(units, *refs):
    own_ref, half_refs, got_refs = refs[0], refs[1 : -3 - len(units)], refs[-3 - len(units) : -3]
    codebook_ref, new_ref, tally_ref = refs[-3:]
    size = codebook_ref.shape[0]
    total, tally = own_ref[0:size], own_ref[size : size + 1, 0:size]
    if half_refs:
        total = total + jnp.concatenate([ref[0:size] for ref in half_refs], axis=1)
        tally = tally + half_refs[0][size : size + 1, 0:size]
    for ref, unit in zip(got_refs, units):
        more, count = unpack(ref[...], unit)
        total, tally = total + more, tally + count[:, 0:size]
    tally_ref[...] = tally
    weight = 1.0 / (jnp.transpose(jnp.broadcast_to(tally, (size, size)))[:, 0:1] + PRIOR)
    new_ref[...] = (total + PRIOR * codebook_ref[...]) * weight


def finish(codebook, own, half_sums, got):
    size = codebook.shape[0]
    arrays = [own, *half_sums, *[message.astype(jnp.float32) for message, _ in got], codebook]
    new, tally = pl.pallas_call(
        functools.partial(final_kernel, [unit for _, unit in got]),
        out_shape=(
            jax.ShapeDtypeStruct(codebook.shape, jnp.float32),
            jax.ShapeDtypeStruct((1, size), jnp.float32),
        ),
        in_specs=[VMEM] * len(arrays),
        out_specs=(VMEM, VMEM),
        compiler_params=PARAMS,
        name="update_centroids",
    )(*arrays)
    return new, tally[0]


def weighted(parts, lognorm, scores, rows, picks):
    size = parts[0][1]
    depth = rows[0].shape[1]
    n_r, r = lognorm.shape
    return pl.pallas_call(
        functools.partial(sums_kernel, len(scores), picks, parts),
        out_shape=[jax.ShapeDtypeStruct((size + SIDE, depth), jnp.float32) for _ in parts],
        in_specs=[VMEM] * (1 + len(scores) + len(rows)),
        out_specs=[VMEM] * len(parts),
        compiler_params=PARAMS,
        cost_estimate=pl.CostEstimate(
            flops=2 * len(parts) * n_r * size * r * depth,
            bytes_accessed=2 * n_r * r * depth,
            transcendentals=len(parts) * n_r * size * r,
        ),
        name="weighted_sums",
    )(lognorm, *scores, *rows)


def local(n_dp, n_cent, embeddings, codebook):
    own_rows = embeddings.shape[0]
    size = codebook.shape[0]
    unit = 1024.0 / (own_rows * n_cent)
    rounded = codebook.astype(jnp.bfloat16)
    if n_cent == 8:
        by_p = [(i, i ^ (4 if i & 1 else 2)) for i in range(n_cent)]
        by_q = [(i, i ^ (2 if i & 1 else 4)) for i in range(n_cent)]
        from_p = lax.ppermute(embeddings, "cent", by_p)
        from_q = lax.ppermute(embeddings, "cent", by_q)
    if n_dp == 4:
        far = swap(rounded, "dp", n_dp, 2)
        near = swap(rounded, "dp", n_dp, 1)
        most, final = [rounded, near, far], [swap(far, "dp", n_dp, 1)]
    else:
        most = [rounded] + [swap(rounded, "dp", n_dp, m) for m in range(1, n_dp - 1)]
        final = [swap(rounded, "dp", n_dp, n_dp - 1)]
    end = (n_dp - 1) * size
    if n_cent == 8:
        diag = lax.ppermute(from_p, "cent", by_q)
        three = jnp.concatenate([embeddings, from_p, from_q], axis=0)
        give = three
        most = [jnp.concatenate(most, axis=0)]
        of_three = [(0, j * own_rows) for j in range(3)]
        s_0, pair_0, half = score(most, [], [three], own_rows, of_three, give_half=True, weight=1)
        three_core = swap(give, "cent", n_cent, 1)
        diag, pair_0 = lax.optimization_barrier((diag, pair_0))
        s_1, pair_1 = score(most, [half], [diag], own_rows, [(0, 0)], weight=.1)
        give, pair_1 = lax.optimization_barrier((diag, pair_1))
        diag_core = swap(give, "cent", n_cent, 1)
        rows = [three, diag, three_core, diag_core]
        order = [0, 2, 4, 6, 1, 5, 3, 7]
        picks = of_three + [(1, 0)] + [(2, at) for _, at in of_three] + [(3, 0)]
        s_2, pair_2, last = score(
            final, [], rows[:2], own_rows, picks[:4], [pair_0, pair_1], give_half=True, weight=60
        )
        three_core, last = lax.optimization_barrier((three_core, last))
        rows[2], both, halves = three_core, most + final, [half, last]
        s_3, pair_3 = score(both, halves, [three_core], own_rows, of_three, weight=.1)
        s_4, pairs = score(both, halves, rows[3:], own_rows, [(0, 0)], [pair_2, pair_3], 7)
        scores = [s_0, s_1, s_3, s_4]
        places = [(0, j) for j in range(3)] + [(1, 0)] + [(2, j) for j in range(3)] + [(3, 0)]
        last_scores = [s_2, s_3, s_4]
        last_places = [(0, j, 0) for j in range(4)] + [(1, j, end) for j in range(3)] + [(2, 0, end)]
    else:
        rows = [embeddings] + [swap(embeddings, "cent", n_cent, m) for m in range(1, n_cent)]
        order = list(range(n_cent))
        picks = [(j, 0) for j in order]
        s_0, pair_0 = score(most, [], rows, own_rows, picks)
        scores = [s_0]
        places = [(0, j) for j in order]
        s_1, pairs = score(final, [], rows, own_rows, picks, [pair_0])
        last_scores, last_places = [s_1], [(0, j, 0) for j in order]
    if n_cent == 8:
        where = [order.index((j ^ 1) & 1 | (j & 2) << 1 | (j & 4) >> 1) for j in order]
        pairs = join(pairs, [partner(n_cent, 1)], [where], False)
        routes = [by_p, by_q, partner(n_cent, 6)]
        where = [[order.index(j ^ mask) for j in order] for mask in (2, 4, 6)]
        lognorm = join(pairs, routes, where, True)
    else:
        for bit in range(n_cent.bit_length() - 1):
            where = [j ^ (1 << bit) for j in order]
            pairs = join(pairs, [partner(n_cent, 1 << bit)], [where], 2 << bit >= n_cent)
        lognorm = pairs

    def part(k, unit):
        return [(i, j, k * size) for i, j in places], size, unit

    (first,) = weighted([(last_places, size, unit)], lognorm, last_scores, rows, picks)
    if n_dp == 4:
        cut = first.shape[1] // 2
        first = [swap(first[:, i : i + cut].astype(jnp.float16), "dp", n_dp, 1) for i in (0, cut)]
        parts = [part(2, 0), part(1, unit), part(0, 0)]
        far_sum, near, own = weighted(parts, lognorm, scores, rows, picks)
        far = []
        for i, got in enumerate(first):
            message = add_part(far_sum, got, i * cut, unit, unit * 0.5)
            far.append(swap(message.astype(jnp.float16), "dp", n_dp, 2))
        near = swap(near.astype(jnp.float16), "dp", n_dp, 1)
        half_sum = add_part(own, far[0], -1, unit * 0.5, 0, 32000)
        near, half_sum = lax.optimization_barrier((near, half_sum))
        own = add_part(own, near, 0, unit, 0, 100000)
        far[1], own = lax.optimization_barrier((far[1], own))
        half_sums = [half_sum, add_part(own, far[1], -1, unit * 0.5, 0)]
        got = []
    else:
        parts = [part(k, unit if k else 0) for k in range(n_dp - 1)]
        own, *others = weighted(parts, lognorm, scores, rows, picks)
        half_sums = []
        others = [other.astype(jnp.float16) for other in others + [first]]
        got = [(swap(other, "dp", n_dp, k + 1), unit) for k, other in enumerate(others)]
    new_codebook, tally = finish(codebook, own, half_sums, got)
    return new_codebook, tally, lognorm[0]


def solution(mesh):
    n_dp, n_cent = mesh.shape["dp"], mesh.shape["cent"]

    def run(embeddings, codebook):
        return local(n_dp, n_cent, embeddings, codebook)

    return jax.shard_map(
        run,
        mesh=mesh,
        in_specs=(P(("dp", "cent"), None), P(("cent", "dp"), None)),
        out_specs=(P(("cent", "dp"), None), P(("cent", "dp")), P(("dp", "cent"))),
        check_vma=False,
    )
```

```python
import functools

import jax
import jax.numpy as jnp
from jax import lax
from jax.experimental import pallas as pl
from jax.experimental.pallas import tpu as pltpu
from jax.sharding import PartitionSpec as P

TEMPER = 0.8
PRIOR = 1.0
SIDE = 8
VMEM = pl.BlockSpec(memory_space=pltpu.VMEM)
PARAMS = pltpu.CompilerParams(vmem_limit_bytes=24 << 20)


def partner(size, mask):
    return [(i, i ^ mask) for i in range(size)]


def swap(x, axis, size, mask):
    return lax.ppermute(x, axis, partner(size, mask))


def merge(a, b):
    top = jnp.maximum(a[0], b[0])
    return top, a[1] * jnp.exp(a[0] - top) + b[1] * jnp.exp(b[0] - top)


def score_kernel(n_cent, n_half, n_rows, picks, begin, starts, r, *refs):
    cent_refs, refs = refs[:n_cent], refs[n_cent:]
    half_refs, refs = refs[:n_half], refs[n_half:]
    row_refs, refs = refs[:n_rows], refs[n_rows:]
    early_refs, (score_ref, pair_ref, *half_out) = refs[: len(starts)], refs[len(starts) :]
    lanes = min(r, 128)
    halves = [ref[...] for ref in half_refs]
    for ref in cent_refs[n_half:]:
        squares = jnp.square(ref[...].astype(jnp.float32))
        half = 0.5 * jnp.sum(squares, axis=1, keepdims=True)
        halves.append(jnp.broadcast_to(half, (half.shape[0], lanes)))
    for ref in half_out:
        ref[...] = halves[-1]
    halves = [jnp.concatenate([half] * (r // lanes), axis=1) for half in halves]
    for j, (i, at) in enumerate(picks):
        parts, first = [], 0
        for ref, half in zip(cent_refs, halves):
            product = lax.dot_general(
                ref[...],
                row_refs[i][at : at + r],
                (((1,), (1,)), ((), ())),
                preferred_element_type=jnp.float32,
            )
            s = (product - half) * (1.0 / TEMPER)
            score_ref[j, first : first + s.shape[0]] = s
            first += s.shape[0]
            parts.append(s)
        top = functools.reduce(jnp.maximum, [jnp.max(s, axis=0, keepdims=True) for s in parts])
        total = sum(jnp.sum(jnp.exp(s - top), axis=0, keepdims=True) for s in parts)
        at = begin + j
        for ref, start in zip(early_refs, starts):
            if start <= at < start + ref.shape[1]:
                k = slice(at - start, at - start + 1)
                top, total = merge((top, total), (ref[0, k], ref[1, k]))
        pair_ref[0, at : at + 1] = top
        pair_ref[1, at : at + 1] = total
    for ref, start in zip(early_refs, starts):
        for k in range(ref.shape[1]):
            if not begin <= start + k < begin + len(picks):
                pair_ref[:, start + k : start + k + 1] = ref[:, k : k + 1]


def score(centers, halves, rows, r, picks, early=(), begin=0, give_half=False, weight=1):
    n_r = len(picks)
    depth = rows[0].shape[1]
    c = sum(x.shape[0] for x in centers)
    starts = [sum(e.shape[1] for e in early[:i]) for i in range(len(early))]
    n_out = max(begin + n_r, sum(e.shape[1] for e in early))
    operands = [*centers, *halves, *rows, *early]
    shapes = [(n_r, c, r), (2, n_out, r)]
    if give_half:
        shapes.append((centers[-1].shape[0], min(r, 128)))
    return pl.pallas_call(
        functools.partial(
            score_kernel, len(centers), len(halves), len(rows), picks, begin, starts, r
        ),
        out_shape=[jax.ShapeDtypeStruct(shape, jnp.float32) for shape in shapes],
        in_specs=[VMEM] * len(operands),
        out_specs=[VMEM] * len(shapes),
        compiler_params=PARAMS,
        cost_estimate=pl.CostEstimate(
            flops=int(2 * n_r * c * r * depth * weight),
            bytes_accessed=int(2 * (n_r * r + c) * depth * weight),
            transcendentals=n_r * c * r,
        ),
        name="score_rows",
    )(*operands)


def join_kernel(places, last, pair_ref, *refs):
    out_ref = refs[-1]
    top, total = pair_ref[0], pair_ref[1]
    for ref, where in zip(refs[:-1], places):
        other = [jnp.concatenate([ref[i, p : p + 1] for p in where]) for i in range(2)]
        top, total = merge((top, total), other)
    if last:
        out_ref[...] = top + jnp.log(total)
    else:
        out_ref[0] = top
        out_ref[1] = total


def join(pairs, routes, places, last):
    others = [lax.ppermute(pairs, "cent", route) for route in routes]
    return pl.pallas_call(
        functools.partial(join_kernel, places, last),
        out_shape=jax.ShapeDtypeStruct(pairs.shape[1:] if last else pairs.shape, jnp.float32),
        in_specs=[VMEM] * (1 + len(others)),
        out_specs=VMEM,
        compiler_params=PARAMS,
        name="join_rows",
    )(pairs, *others)


def sums_kernel(n_parts, picks, parts, lognorm_ref, *refs):
    score_refs, row_refs = refs[:n_parts], refs[n_parts : -len(parts)]
    outs = refs[-len(parts) :]
    ones = jnp.ones((SIDE, max(ref.shape[0] for ref in row_refs)), jnp.bfloat16)
    for out, (places, size, unit) in zip(outs, parts):
        total, tally = None, None
        for i, ref in enumerate(row_refs):
            mine = [j for j, pick in enumerate(picks) if pick[0] == i]
            resp = []
            for j in mine:
                k, block, first = places[j]
                s = score_refs[k][block, first : first + size, :]
                resp.append(jnp.exp(s - lognorm_ref[j : j + 1]).astype(jnp.bfloat16))
            resp = jnp.concatenate(resp, axis=1)
            more = jnp.dot(resp, ref[...], preferred_element_type=jnp.float32)
            count = lax.dot_general(
                ones[:, : ref.shape[0]],
                resp,
                (((1,), (1,)), ((), ())),
                preferred_element_type=jnp.float32,
            )
            total = more if total is None else total + more
            tally = count if tally is None else tally + count
        wide = jnp.concatenate(
            [tally, jnp.zeros((SIDE, total.shape[1] - size), jnp.float32)], axis=1
        )
        if unit:
            total, wide = pack(total, wide[0:1], unit)
        out[0:size] = total
        out[size : size + SIDE] = wide


def pack(total, tally, unit):
    peak = jnp.max(jnp.abs(total), axis=0, keepdims=True)
    power = jnp.clip(jnp.ceil(jnp.log2(peak)), -100.0, 100.0)
    high = jnp.floor(tally * unit)
    rest = (tally * unit - high) * 1024.0
    middle = jnp.floor(rest)
    low = (rest - middle) * 1024.0
    blank = jnp.zeros((SIDE - 4, total.shape[1]), jnp.float32)
    return total * jnp.exp2(14.0 - power), jnp.concatenate([power, high, middle, low, blank])


def unpack(values, unit):
    size = values.shape[0] - SIDE
    power, high, middle, low = (values[size + i : size + i + 1] for i in range(4))
    tally = (high + (middle + low * (1.0 / 1024.0)) * (1.0 / 1024.0)) * (1.0 / unit)
    return values[:size] * jnp.exp2(power - 14.0), tally


def add_kernel(unit, packed, at, own_ref, got_ref, out_ref):
    size, depth = out_ref.shape[0] - SIDE, out_ref.shape[1]
    total, tally = unpack(got_ref[...], unit)
    if at >= 0:
        total = own_ref[0:size, at : at + depth] + total
        tally = own_ref[size : size + 1, at : at + depth] + tally
    if packed:
        total, wide = pack(total, tally, packed)
    else:
        wide = jnp.concatenate([tally, jnp.zeros((SIDE - 1, depth), jnp.float32)])
    out_ref[0:size] = total
    out_ref[size : size + SIDE] = wide


def add_part(own, got, at, unit, packed, weight=0):
    got = got.astype(jnp.float32)
    return pl.pallas_call(
        functools.partial(add_kernel, unit, packed, at),
        out_shape=jax.ShapeDtypeStruct(got.shape, jnp.float32),
        in_specs=[VMEM] * 2,
        out_specs=VMEM,
        compiler_params=PARAMS,
        cost_estimate=pl.CostEstimate(
            flops=got.size * (1 + weight), bytes_accessed=0, transcendentals=0
        ),
        name="add_sums",
    )(own, got)


def final_kernel(units, *refs):
    arrived = len(refs) - 5 - len(units)
    own_ref, half_refs, got_refs = refs[0], refs[1:arrived], refs[arrived:-5]
    codebook_ref, lognorm_ref, new_ref, tally_ref, norm_ref = refs[-5:]
    norm_ref[...] = lognorm_ref[0:1]
    size = codebook_ref.shape[0]
    total, tally = own_ref[0:size], own_ref[size : size + 1, 0:size]
    if half_refs:
        total = total + jnp.concatenate([ref[0:size] for ref in half_refs], axis=1)
        tally = tally + half_refs[0][size : size + 1, 0:size]
    for ref, unit in zip(got_refs, units):
        more, count = unpack(ref[...], unit)
        total, tally = total + more, tally + count[:, 0:size]
    tally_ref[...] = tally
    weight = 1.0 / (jnp.transpose(jnp.broadcast_to(tally, (size, size)))[:, 0:1] + PRIOR)
    new_ref[...] = (total + PRIOR * codebook_ref[...]) * weight


def finish(codebook, lognorm, own, half_sums, got):
    size = codebook.shape[0]
    arrays = [own, *half_sums, *[message.astype(jnp.float32) for message, _ in got], codebook, lognorm]
    new, tally, norm = pl.pallas_call(
        functools.partial(final_kernel, [unit for _, unit in got]),
        out_shape=(
            jax.ShapeDtypeStruct(codebook.shape, jnp.float32),
            jax.ShapeDtypeStruct((1, size), jnp.float32),
            jax.ShapeDtypeStruct((1, lognorm.shape[1]), jnp.float32),
        ),
        in_specs=[VMEM] * len(arrays),
        out_specs=(VMEM,) * 3,
        compiler_params=PARAMS,
        name="update_centroids",
    )(*arrays)
    return new, tally[0], norm[0]


def weighted(parts, lognorm, scores, rows, picks):
    size = parts[0][1]
    depth = rows[0].shape[1]
    n_r, r = lognorm.shape
    return pl.pallas_call(
        functools.partial(sums_kernel, len(scores), picks, parts),
        out_shape=[jax.ShapeDtypeStruct((size + SIDE, depth), jnp.float32) for _ in parts],
        in_specs=[VMEM] * (1 + len(scores) + len(rows)),
        out_specs=[VMEM] * len(parts),
        compiler_params=PARAMS,
        cost_estimate=pl.CostEstimate(
            flops=2 * len(parts) * n_r * size * r * depth,
            bytes_accessed=2 * n_r * r * depth,
            transcendentals=len(parts) * n_r * size * r,
        ),
        name="weighted_sums",
    )(lognorm, *scores, *rows)


def local(n_dp, n_cent, embeddings, codebook):
    own_rows = embeddings.shape[0]
    size = codebook.shape[0]
    unit = 1024.0 / (own_rows * n_cent)
    rounded = codebook.astype(jnp.bfloat16)
    if n_cent == 8:
        by_p = [(i, i ^ (4 if i & 1 else 2)) for i in range(n_cent)]
        by_q = [(i, i ^ (2 if i & 1 else 4)) for i in range(n_cent)]
        from_p = lax.ppermute(embeddings, "cent", by_p)
        from_q = lax.ppermute(embeddings, "cent", by_q)
    if n_dp == 4:
        far = swap(rounded, "dp", n_dp, 2)
        near = swap(rounded, "dp", n_dp, 1)
        most, final = [rounded, near, far], [swap(far, "dp", n_dp, 1)]
    else:
        most = [rounded] + [swap(rounded, "dp", n_dp, m) for m in range(1, n_dp - 1)]
        final = [swap(rounded, "dp", n_dp, n_dp - 1)]
    end = (n_dp - 1) * size
    if n_cent == 8:
        diag = lax.ppermute(from_p, "cent", by_q)
        three = jnp.concatenate([embeddings, from_p, from_q], axis=0)
        give = three
        most = [jnp.concatenate(most, axis=0)]
        of_three = [(0, j * own_rows) for j in range(3)]
        s_0, pair_0, half = score(most, [], [three], own_rows, of_three, give_half=True, weight=1)
        three_core = swap(give, "cent", n_cent, 1)
        diag, pair_0 = lax.optimization_barrier((diag, pair_0))
        s_1, pair_1 = score(most, [half], [diag], own_rows, [(0, 0)], weight=.1)
        give, pair_1 = lax.optimization_barrier((diag, pair_1))
        diag_core = swap(give, "cent", n_cent, 1)
        rows = [three, diag, three_core, diag_core]
        order = [0, 2, 4, 6, 1, 5, 3, 7]
        picks = of_three + [(1, 0)] + [(2, at) for _, at in of_three] + [(3, 0)]
        s_2, pair_2, last = score(
            final, [], rows[:2], own_rows, picks[:4], [pair_0, pair_1], give_half=True, weight=60
        )
        three_core, last = lax.optimization_barrier((three_core, last))
        rows[2], both, halves = three_core, most + final, [half, last]
        s_3, pair_3 = score(both, halves, [three_core], own_rows, of_three, weight=.1)
        s_4, pairs = score(both, halves, rows[3:], own_rows, [(0, 0)], [pair_2, pair_3], 7)
        scores = [s_0, s_1, s_3, s_4]
        places = [(0, j) for j in range(3)] + [(1, 0)] + [(2, j) for j in range(3)] + [(3, 0)]
        last_scores = [s_2, s_3, s_4]
        last_places = [(0, j, 0) for j in range(4)] + [(1, j, end) for j in range(3)] + [(2, 0, end)]
    else:
        rows = [embeddings] + [swap(embeddings, "cent", n_cent, m) for m in range(1, n_cent)]
        order = list(range(n_cent))
        picks = [(j, 0) for j in order]
        s_0, pair_0 = score(most, [], rows, own_rows, picks)
        scores = [s_0]
        places = [(0, j) for j in order]
        s_1, pairs = score(final, [], rows, own_rows, picks, [pair_0])
        last_scores, last_places = [s_1], [(0, j, 0) for j in order]
    if n_cent == 8:
        where = [order.index((j ^ 1) & 1 | (j & 2) << 1 | (j & 4) >> 1) for j in order]
        pairs = join(pairs, [partner(n_cent, 1)], [where], False)
        routes = [by_p, by_q, partner(n_cent, 6)]
        where = [[order.index(j ^ mask) for j in order] for mask in (2, 4, 6)]
        lognorm = join(pairs, routes, where, True)
    else:
        for bit in range(n_cent.bit_length() - 1):
            where = [j ^ (1 << bit) for j in order]
            pairs = join(pairs, [partner(n_cent, 1 << bit)], [where], 2 << bit >= n_cent)
        lognorm = pairs

    def part(k, unit):
        return [(i, j, k * size) for i, j in places], size, unit

    (first,) = weighted([(last_places, size, unit)], lognorm, last_scores, rows, picks)
    if n_dp == 4:
        cut = first.shape[1] // 2
        first = [swap(first[:, i : i + cut].astype(jnp.float16), "dp", n_dp, 1) for i in (0, cut)]
        parts = [part(2, 0), part(1, unit), part(0, 0)]
        far_sum, near, own = weighted(parts, lognorm, scores, rows, picks)
        far = []
        for i, got in enumerate(first):
            message = add_part(far_sum, got, i * cut, unit, unit * 0.5)
            far.append(swap(message.astype(jnp.float16), "dp", n_dp, 2))
        near = swap(near.astype(jnp.float16), "dp", n_dp, 1)
        half_sum = add_part(own, far[0], -1, unit * 0.5, 0, 32000)
        near, half_sum = lax.optimization_barrier((near, half_sum))
        own = add_part(own, near, 0, unit, 0, 100000)
        far[1], own = lax.optimization_barrier((far[1], own))
        half_sums = [half_sum, add_part(own, far[1], -1, unit * 0.5, 0)]
        got = []
    else:
        parts = [part(k, unit if k else 0) for k in range(n_dp - 1)]
        own, *others = weighted(parts, lognorm, scores, rows, picks)
        half_sums = []
        others = [other.astype(jnp.float16) for other in others + [first]]
        got = [(swap(other, "dp", n_dp, k + 1), unit) for k, other in enumerate(others)]
    return finish(codebook, lognorm, own, half_sums, got)


def solution(mesh):
    n_dp, n_cent = mesh.shape["dp"], mesh.shape["cent"]

    def run(embeddings, codebook):
        return local(n_dp, n_cent, embeddings, codebook)

    return jax.shard_map(
        run,
        mesh=mesh,
        in_specs=(P(("dp", "cent"), None), P(("cent", "dp"), None)),
        out_specs=(P(("cent", "dp"), None), P(("cent", "dp")), P(("dp", "cent"))),
        check_vma=False,
    )
```

```python
import functools

import jax
import jax.numpy as jnp
from jax import lax
from jax.experimental import pallas as pl
from jax.experimental.pallas import tpu as pltpu
from jax.sharding import PartitionSpec as P

TEMPER = 0.8
PRIOR = 1.0
SIDE = 8
VMEM = pl.BlockSpec(memory_space=pltpu.VMEM)
PARAMS = pltpu.CompilerParams(vmem_limit_bytes=24 << 20)


def partner(size, mask):
    return [(i, i ^ mask) for i in range(size)]


def swap(x, axis, size, mask):
    return lax.ppermute(x, axis, partner(size, mask))


def merge(a, b):
    top = jnp.maximum(a[0], b[0])
    return top, a[1] * jnp.exp(a[0] - top) + b[1] * jnp.exp(b[0] - top)


def score_kernel(n_cent, n_half, n_rows, picks, begin, starts, r, *refs):
    cent_refs, refs = refs[:n_cent], refs[n_cent:]
    half_refs, refs = refs[:n_half], refs[n_half:]
    row_refs, refs = refs[:n_rows], refs[n_rows:]
    early_refs, (score_ref, pair_ref, *half_out) = refs[: len(starts)], refs[len(starts) :]
    lanes = min(r, 128)
    halves = [ref[...] for ref in half_refs]
    for ref in cent_refs[n_half:]:
        squares = jnp.square(ref[...].astype(jnp.float32))
        half = 0.5 * jnp.sum(squares, axis=1, keepdims=True)
        halves.append(jnp.broadcast_to(half, (half.shape[0], lanes)))
    for ref in half_out:
        ref[...] = halves[-1]
    halves = [jnp.concatenate([half] * (r // lanes), axis=1) for half in halves]
    for j, (i, at) in enumerate(picks):
        parts, first = [], 0
        for ref, half in zip(cent_refs, halves):
            product = lax.dot_general(
                ref[...],
                row_refs[i][at : at + r],
                (((1,), (1,)), ((), ())),
                preferred_element_type=jnp.float32,
            )
            s = (product - half) * (1.0 / TEMPER)
            score_ref[j, first : first + s.shape[0]] = s
            first += s.shape[0]
            parts.append(s)
        top = functools.reduce(jnp.maximum, [jnp.max(s, axis=0, keepdims=True) for s in parts])
        total = sum(jnp.sum(jnp.exp(s - top), axis=0, keepdims=True) for s in parts)
        at = begin + j
        for ref, start in zip(early_refs, starts):
            if start <= at < start + ref.shape[1]:
                k = slice(at - start, at - start + 1)
                top, total = merge((top, total), (ref[0, k], ref[1, k]))
        pair_ref[0, at : at + 1] = top
        pair_ref[1, at : at + 1] = total
    for ref, start in zip(early_refs, starts):
        for k in range(ref.shape[1]):
            if not begin <= start + k < begin + len(picks):
                pair_ref[:, start + k : start + k + 1] = ref[:, k : k + 1]


def score(centers, halves, rows, r, picks, early=(), begin=0, give_half=False, weight=1):
    n_r = len(picks)
    depth = rows[0].shape[1]
    c = sum(x.shape[0] for x in centers)
    starts = [sum(e.shape[1] for e in early[:i]) for i in range(len(early))]
    n_out = max(begin + n_r, sum(e.shape[1] for e in early))
    operands = [*centers, *halves, *rows, *early]
    shapes = [(n_r, c, r), (2, n_out, r)]
    if give_half:
        shapes.append((centers[-1].shape[0], min(r, 128)))
    return pl.pallas_call(
        functools.partial(
            score_kernel, len(centers), len(halves), len(rows), picks, begin, starts, r
        ),
        out_shape=[jax.ShapeDtypeStruct(shape, jnp.float32) for shape in shapes],
        in_specs=[VMEM] * len(operands),
        out_specs=[VMEM] * len(shapes),
        compiler_params=PARAMS,
        cost_estimate=pl.CostEstimate(
            flops=int(2 * n_r * c * r * depth * weight),
            bytes_accessed=int(2 * (n_r * r + c) * depth * weight),
            transcendentals=n_r * c * r,
        ),
        name="score_rows",
    )(*operands)


def join_kernel(places, last, pair_ref, *refs):
    out_ref = refs[-1]
    top, total = pair_ref[0], pair_ref[1]
    for ref, where in zip(refs[:-1], places):
        other = [jnp.concatenate([ref[i, p : p + 1] for p in where]) for i in range(2)]
        top, total = merge((top, total), other)
    if last:
        out_ref[...] = top + jnp.log(total)
    else:
        out_ref[0] = top
        out_ref[1] = total


def join(pairs, routes, places, last):
    others = [lax.ppermute(pairs, "cent", route) for route in routes]
    return pl.pallas_call(
        functools.partial(join_kernel, places, last),
        out_shape=jax.ShapeDtypeStruct(pairs.shape[1:] if last else pairs.shape, jnp.float32),
        in_specs=[VMEM] * (1 + len(others)),
        out_specs=VMEM,
        compiler_params=PARAMS,
        name="join_rows",
    )(pairs, *others)


def sums_kernel(n_parts, picks, parts, lognorm_ref, *refs):
    score_refs, row_refs = refs[:n_parts], refs[n_parts : -len(parts)]
    outs = refs[-len(parts) :]
    ones = jnp.ones((SIDE, max(ref.shape[0] for ref in row_refs)), jnp.bfloat16)
    for out, (places, size, unit) in zip(outs, parts):
        total, tally = None, None
        for i, ref in enumerate(row_refs):
            mine = [j for j, pick in enumerate(picks) if pick[0] == i]
            resp = []
            for j in mine:
                k, block, first = places[j]
                s = score_refs[k][block, first : first + size, :]
                resp.append(jnp.exp(s - lognorm_ref[j : j + 1]).astype(jnp.bfloat16))
            resp = jnp.concatenate(resp, axis=1)
            more = jnp.dot(resp, ref[...], preferred_element_type=jnp.float32)
            count = lax.dot_general(
                ones[:, : ref.shape[0]],
                resp,
                (((1,), (1,)), ((), ())),
                preferred_element_type=jnp.float32,
            )
            total = more if total is None else total + more
            tally = count if tally is None else tally + count
        wide = jnp.concatenate(
            [tally, jnp.zeros((SIDE, total.shape[1] - size), jnp.float32)], axis=1
        )
        if unit:
            total, wide = pack(total, wide[0:1], unit)
        out[0:size] = total
        out[size : size + SIDE] = wide


def pack(total, tally, unit):
    peak = jnp.max(jnp.abs(total), axis=0, keepdims=True)
    power = jnp.clip(jnp.ceil(jnp.log2(peak)), -100.0, 100.0)
    high = jnp.floor(tally * unit)
    rest = (tally * unit - high) * 1024.0
    middle = jnp.floor(rest)
    low = (rest - middle) * 1024.0
    blank = jnp.zeros((SIDE - 4, total.shape[1]), jnp.float32)
    return total * jnp.exp2(14.0 - power), jnp.concatenate([power, high, middle, low, blank])


def unpack(values, unit):
    size = values.shape[0] - SIDE
    power, high, middle, low = (values[size + i : size + i + 1] for i in range(4))
    tally = (high + (middle + low * (1.0 / 1024.0)) * (1.0 / 1024.0)) * (1.0 / unit)
    return values[:size] * jnp.exp2(power - 14.0), tally


def add_kernel(unit, packed, at, own_ref, got_ref, out_ref):
    size, depth = out_ref.shape[0] - SIDE, out_ref.shape[1]
    total, tally = unpack(got_ref[...], unit)
    if at >= 0:
        total = own_ref[0:size, at : at + depth] + total
        tally = own_ref[size : size + 1, at : at + depth] + tally
    if packed:
        total, wide = pack(total, tally, packed)
    else:
        wide = jnp.concatenate([tally, jnp.zeros((SIDE - 1, depth), jnp.float32)])
    out_ref[0:size] = total
    out_ref[size : size + SIDE] = wide


def add_part(own, got, at, unit, packed, weight=0):
    got = got.astype(jnp.float32)
    return pl.pallas_call(
        functools.partial(add_kernel, unit, packed, at),
        out_shape=jax.ShapeDtypeStruct(got.shape, jnp.float32),
        in_specs=[VMEM] * 2,
        out_specs=VMEM,
        compiler_params=PARAMS,
        cost_estimate=pl.CostEstimate(
            flops=got.size * (1 + weight), bytes_accessed=0, transcendentals=0
        ),
        name="add_sums",
    )(own, got)


def final_kernel(units, *refs):
    own_ref, half_refs, got_refs = refs[0], refs[1 : -3 - len(units)], refs[-3 - len(units) : -3]
    codebook_ref, new_ref, tally_ref = refs[-3:]
    size = codebook_ref.shape[0]
    total, tally = own_ref[0:size], own_ref[size : size + 1, 0:size]
    if half_refs:
        total = total + jnp.concatenate([ref[0:size] for ref in half_refs], axis=1)
        tally = tally + half_refs[0][size : size + 1, 0:size]
    for ref, unit in zip(got_refs, units):
        more, count = unpack(ref[...], unit)
        total, tally = total + more, tally + count[:, 0:size]
    tally_ref[...] = tally
    weight = 1.0 / (jnp.transpose(jnp.broadcast_to(tally, (size, size)))[:, 0:1] + PRIOR)
    new_ref[...] = (total + PRIOR * codebook_ref[...]) * weight


def finish(codebook, own, half_sums, got):
    size = codebook.shape[0]
    arrays = [own, *half_sums, *[message.astype(jnp.float32) for message, _ in got], codebook]
    new, tally = pl.pallas_call(
        functools.partial(final_kernel, [unit for _, unit in got]),
        out_shape=(
            jax.ShapeDtypeStruct(codebook.shape, jnp.float32),
            jax.ShapeDtypeStruct((1, size), jnp.float32),
        ),
        in_specs=[VMEM] * len(arrays),
        out_specs=(VMEM, VMEM),
        compiler_params=PARAMS,
        name="update_centroids",
    )(*arrays)
    return new, tally[0]


def weighted(parts, lognorm, scores, rows, picks):
    size = parts[0][1]
    depth = rows[0].shape[1]
    n_r, r = lognorm.shape
    return pl.pallas_call(
        functools.partial(sums_kernel, len(scores), picks, parts),
        out_shape=[jax.ShapeDtypeStruct((size + SIDE, depth), jnp.float32) for _ in parts],
        in_specs=[VMEM] * (1 + len(scores) + len(rows)),
        out_specs=[VMEM] * len(parts),
        compiler_params=PARAMS,
        cost_estimate=pl.CostEstimate(
            flops=2 * len(parts) * n_r * size * r * depth,
            bytes_accessed=2 * n_r * r * depth,
            transcendentals=len(parts) * n_r * size * r,
        ),
        name="weighted_sums",
    )(lognorm, *scores, *rows)


def local(n_dp, n_cent, embeddings, codebook):
    own_rows = embeddings.shape[0]
    size = codebook.shape[0]
    unit = 1024.0 / (own_rows * n_cent)
    rounded = codebook.astype(jnp.bfloat16)
    if n_cent == 8:
        by_p = [(i, i ^ (4 if i & 1 else 2)) for i in range(n_cent)]
        by_q = [(i, i ^ (2 if i & 1 else 4)) for i in range(n_cent)]
        from_p = lax.ppermute(embeddings, "cent", by_p)
        from_q = lax.ppermute(embeddings, "cent", by_q)
    if n_dp == 4:
        far = swap(rounded, "dp", n_dp, 2)
        near = swap(rounded, "dp", n_dp, 1)
        most, final = [rounded, near, far], [swap(far, "dp", n_dp, 1)]
    else:
        most = [rounded] + [swap(rounded, "dp", n_dp, m) for m in range(1, n_dp - 1)]
        final = [swap(rounded, "dp", n_dp, n_dp - 1)]
    end = (n_dp - 1) * size
    if n_cent == 8:
        diag = lax.ppermute(from_p, "cent", by_q)
        three = jnp.concatenate([embeddings, from_p, from_q], axis=0)
        give = three
        most = [jnp.concatenate(most, axis=0)]
        of_three = [(0, j * own_rows) for j in range(3)]
        s_0, pair_0, half = score(most, [], [three], own_rows, of_three, give_half=True, weight=1)
        three_core = swap(give, "cent", n_cent, 1)
        diag, pair_0 = lax.optimization_barrier((diag, pair_0))
        s_1, pair_1 = score(most, [half], [diag], own_rows, [(0, 0)], weight=.1)
        give, pair_1 = lax.optimization_barrier((diag, pair_1))
        diag_core = swap(give, "cent", n_cent, 1)
        rows = [three, diag, three_core, diag_core]
        order = [0, 2, 4, 6, 1, 5, 3, 7]
        picks = of_three + [(1, 0)] + [(2, at) for _, at in of_three] + [(3, 0)]
        s_2, pair_2, last = score(
            final, [], rows[:2], own_rows, picks[:4], [pair_0, pair_1], give_half=True, weight=60
        )
        three_core, last = lax.optimization_barrier((three_core, last))
        rows[2], both, halves = three_core, most + final, [half, last]
        s_3, pair_3 = score(both, halves, [three_core], own_rows, of_three, weight=.1)
        s_4, pairs = score(both, halves, rows[3:], own_rows, [(0, 0)], [pair_2, pair_3], 7)
        scores = [s_0, s_1, s_3, s_4]
        places = [(0, j) for j in range(3)] + [(1, 0)] + [(2, j) for j in range(3)] + [(3, 0)]
        last_scores = [s_2, s_3, s_4]
        last_places = [(0, j, 0) for j in range(4)] + [(1, j, end) for j in range(3)] + [(2, 0, end)]
    else:
        rows = [embeddings] + [swap(embeddings, "cent", n_cent, m) for m in range(1, n_cent)]
        order = list(range(n_cent))
        picks = [(j, 0) for j in order]
        s_0, pair_0 = score(most, [], rows, own_rows, picks)
        scores = [s_0]
        places = [(0, j) for j in order]
        s_1, pairs = score(final, [], rows, own_rows, picks, [pair_0])
        last_scores, last_places = [s_1], [(0, j, 0) for j in order]
    if n_cent == 8:
        where = [order.index((j ^ 1) & 1 | (j & 2) << 1 | (j & 4) >> 1) for j in order]
        pairs = join(pairs, [partner(n_cent, 1)], [where], False)
        routes = [by_p, by_q, partner(n_cent, 6)]
        where = [[order.index(j ^ mask) for j in order] for mask in (2, 4, 6)]
        lognorm = join(pairs, routes, where, True)
    else:
        for bit in range(n_cent.bit_length() - 1):
            where = [j ^ (1 << bit) for j in order]
            pairs = join(pairs, [partner(n_cent, 1 << bit)], [where], 2 << bit >= n_cent)
        lognorm = pairs

    def part(k, unit):
        return [(i, j, k * size) for i, j in places], size, unit

    (first,) = weighted([(last_places, size, unit)], lognorm, last_scores, rows, picks)
    if n_dp == 4:
        cut = first.shape[1] // 2
        first = [swap(first[:, i : i + cut].astype(jnp.float16), "dp", n_dp, 1) for i in (0, cut)]
        parts = [part(2, 0), part(1, unit), part(0, 0)]
        far_sum, near, own = weighted(parts, lognorm, scores, rows, picks)
        far = []
        for i, got in enumerate(first):
            message = add_part(far_sum, got, i * cut, unit, unit * 0.5)
            far.append(swap(message.astype(jnp.float16), "dp", n_dp, 2))
        near = swap(near.astype(jnp.float16), "dp", n_dp, 1)
        half_sum = add_part(own, far[0], -1, unit * 0.5, 0, 32000)
        near, half_sum, lognorm = lax.optimization_barrier((near, half_sum, lognorm))
        own = add_part(own, near, 0, unit, 0, 100000)
        far[1], own = lax.optimization_barrier((far[1], own))
        half_sums = [half_sum, add_part(own, far[1], -1, unit * 0.5, 0)]
        got = []
    else:
        parts = [part(k, unit if k else 0) for k in range(n_dp - 1)]
        own, *others = weighted(parts, lognorm, scores, rows, picks)
        half_sums = []
        others = [other.astype(jnp.float16) for other in others + [first]]
        got = [(swap(other, "dp", n_dp, k + 1), unit) for k, other in enumerate(others)]
    new_codebook, tally = finish(codebook, own, half_sums, got)
    return new_codebook, tally, lognorm[0]


def solution(mesh):
    n_dp, n_cent = mesh.shape["dp"], mesh.shape["cent"]

    def run(embeddings, codebook):
        return local(n_dp, n_cent, embeddings, codebook)

    return jax.shard_map(
        run,
        mesh=mesh,
        in_specs=(P(("dp", "cent"), None), P(("cent", "dp"), None)),
        out_specs=(P(("cent", "dp"), None), P(("cent", "dp")), P(("dp", "cent"))),
        check_vma=False,
    )
```
